32 devices in a mesh: groups: 2 (over x), samp: 16 (over z, y, core).
Axes of the slice: x: 2, y: 2, z: 4, core: 2. Of those that a mesh axis runs over, the one named last changes fastest.
Arguments:
- samples: int32 [32, 32768], P('groups', 'samp'), parts along dimension 0, may hold values from 0 to 65520
- generator: int32 [16], replicated, may hold values from 1 to 65520
- weight_index: int32 [16], replicated, may hold values from 0 to 7
- preconditioner: float32 [1024, 1024], P('samp'), may hold values from -2 to 2, as said below
- solution: float32 [32, 1024], P('groups', 'samp'), parts along dimension 0, may hold values from -24 to 24
- residual: float32 [32, 1024], P('groups', 'samp'), parts along dimension 0, may hold values from -24 to 24
- direction: float32 [32, 1024], P('groups', 'samp'), parts along dimension 0, may hold values from -24 to 24
Outputs:
- new_solution: float32 [32, 1024], P('groups', 'samp'), parts along dimension 0
- new_residual: float32 [32, 1024], P('groups', 'samp'), parts along dimension 0
- new_direction: float32 [32, 1024], P('groups', 'samp'), parts along dimension 0
The draws below stay inside these ranges and needn't reach their ends.
There are 2 independent parts, one for each index of `groups`. The reference program is written for one: setup_inputs(seed, part) draws one part's arguments, and reference() takes and returns one part's arrays. A program takes and returns all parts, laid end to end along the dimension named above; an argument that names none is the same for every part. Nothing has to cross between parts.
Inputs may be any that keep to these rules, and one draw needn't show every extreme that they name: generator entries are nonzero residues of the prime 65521. `weight_index`: weight indices select gamma = 0.5 * 0.75 ** index. `preconditioner`: upper triangular, diagonal between 1 and 2.
All inputs are finite; a program needn't handle non-finite values.
Results may differ from the reference program's by a relative error of at most 0.0003.
Values sent between devices are 32-bit elements; how exact they have to be, the bound alone decides.
No kernel may reach another device: no remote copies, remote signals or barrier semaphores. Data moves between devices by JAX's collectives and lax.ppermute only.
A program may use at most 64 MiB of HBM per device.

```python
import math
import jax
import jax.numpy as jnp
from jax import lax

DIMS = 16
OUTS = 16
LATTICE = 65521
S_DEV = 2048
CEN_DEV = 64
NSAMP = 32768
M = 1024
N_SAMP = 16


def state_values(key, salt_value):
    base_key = jax.random.fold_in(key, salt_value)
    column_ramp = jnp.arange(M, dtype=jnp.float32) / M
    row_ramp = jnp.arange(OUTS, dtype=jnp.float32) / OUTS
    weighting = jnp.exp(jnp.log(10.0) * (column_ramp[None, :] - 0.5)) * jnp.exp(jnp.log(10.0) * 0.5 * (row_ramp[:, None] - 0.5))
    values = jnp.clip(jax.random.normal(base_key, (OUTS, M), jnp.float32), -4.0, 4.0)
    return values * weighting


def draw_samples(key, part):
    key = jax.random.fold_in(key, 505)
    values = jax.random.randint(key, (DIMS, NSAMP), 0, LATTICE, dtype=jnp.int32)
    values = values.at[0, 0].set(0)
    values = values.at[1, 0].set(LATTICE - 1)
    return values.astype(jnp.int32)


def draw_solution(key, part):
    return state_values(key, 101)


def draw_residual(key, part):
    return state_values(key, 202)


def draw_direction(key, part):
    return state_values(key, 303)


def draw_preconditioner(key, part):
    base_key = jax.random.fold_in(key, 404)
    diag_key, entry_key = jax.random.split(base_key)
    row_index = jnp.arange(M)[:, None]
    column_index = jnp.arange(M)[None, :]
    diagonal = jax.random.uniform(diag_key, (M,), jnp.float32, 1.0, 2.0)
    entries = jnp.clip(jax.random.normal(entry_key, (M, M), jnp.float32), -4.0, 4.0)
    entries = entries * (0.8 * M ** (-0.5))
    above_diagonal = jnp.where(column_index > row_index, entries, 0.0)
    return jnp.where(column_index == row_index, diagonal[:, None], above_diagonal).astype(jnp.float32)


def set_ends(result, rng, least, largest):
    dims = result.shape
    spot = [jax.random.randint(jax.random.fold_in(rng, axis), (), 0, dims[axis]) for axis in range(len(dims))]
    result = result.at[tuple(spot)].set(least)
    longest = dims.index(max(dims))
    spot[longest] = (spot[longest] + 1) % dims[longest]
    return result.at[tuple(spot)].set(largest)


def setup_inputs(seed: int = 0, part: int = 0) -> dict:
    seeds = jax.random.split(jax.random.key(seed), 8)
    own_keys = jax.random.split(jax.random.fold_in(seeds[7], part), 8)
    samples = draw_samples(jax.random.fold_in(jax.random.fold_in(seeds[7], part), 71), part)
    generator = set_ends(jax.random.randint(seeds[1], (DIMS,), 1, LATTICE), jax.random.fold_in(seeds[1], 1), 1, LATTICE - 1).astype(jnp.int32)
    weight_index = set_ends(jax.random.randint(seeds[2], (DIMS,), 0, 8), jax.random.fold_in(seeds[2], 1), 0, 7).astype(jnp.int32)
    preconditioner = draw_preconditioner(jax.random.fold_in(seeds[7], 71), part)
    solution = draw_solution(jax.random.fold_in(jax.random.fold_in(seeds[7], part), 71), part)
    residual = draw_residual(jax.random.fold_in(jax.random.fold_in(seeds[7], part), 71), part)
    direction = draw_direction(jax.random.fold_in(jax.random.fold_in(seeds[7], part), 71), part)
    return dict(samples=samples, generator=generator, weight_index=weight_index, preconditioner=preconditioner, solution=solution, residual=residual, direction=direction)


ridge_weight = 0.25
bernoulli_factor = 2.0 * math.pi * math.pi


def centre_coords(lattice_index, generator):
    upper_digits = generator // 256
    lower_digits = generator % 256
    column = lattice_index[None, :]
    partial_value = (column * upper_digits[:, None]) % LATTICE
    return (partial_value * 256 + column * lower_digits[:, None]) % LATTICE


def kernel_block(left_points, right_points, weights_dim):
    product = jnp.ones((left_points.shape[1], right_points.shape[1]), jnp.float32)
    for axis_number in range(left_points.shape[0]):
        offset = (left_points[axis_number][:, None] - right_points[axis_number][None, :]) % LATTICE
        fraction = offset.astype(jnp.float32) / LATTICE
        product = product * (1.0 + weights_dim[axis_number] * bernoulli_factor * (fraction * fraction - fraction + 1.0 / 6.0))
    return product


def reference(samples, generator, weight_index, preconditioner, solution, residual, direction):
    highest = lax.Precision.HIGHEST
    weights_dim = 0.5 * jnp.power(0.75, weight_index.astype(jnp.float32))
    centres = centre_coords(jnp.arange(M, dtype=jnp.int32), generator)
    coefficients = jnp.dot(direction, preconditioner.T, precision=highest, preferred_element_type=jnp.float32)
    sample_blocks = samples.reshape(DIMS, N_SAMP, S_DEV).transpose(1, 0, 2)

    def accumulate(backward, points):
        kernel_rows = kernel_block(points, centres, weights_dim)
        fitted = jnp.dot(coefficients, kernel_rows.T, precision=highest, preferred_element_type=jnp.float32)
        return backward + jnp.dot(fitted, kernel_rows, precision=highest, preferred_element_type=jnp.float32), None

    backward, _ = lax.scan(accumulate, jnp.zeros((OUTS, M), jnp.float32), sample_blocks)
    centre_blocks = centres.reshape(DIMS, N_SAMP, CEN_DEV).transpose(1, 0, 2)

    def centre_rows(points):
        kernel_rows = kernel_block(points, centres, weights_dim)
        return jnp.dot(coefficients, kernel_rows.T, precision=highest, preferred_element_type=jnp.float32)

    kernel_products = lax.map(centre_rows, centre_blocks).transpose(1, 0, 2).reshape(OUTS, M)
    scale_total = float(NSAMP) * float(M)
    applied = backward / scale_total + ridge_weight * kernel_products / M
    image_rows = jnp.dot(applied, preconditioner, precision=highest, preferred_element_type=jnp.float32)
    norm_old = jnp.sum(residual * residual, axis=1)
    curvature = jnp.sum(direction * image_rows, axis=1)
    step_length = norm_old / curvature
    new_solution = solution + step_length[:, None] * direction
    new_residual = residual - step_length[:, None] * image_rows
    norm_new = jnp.sum(new_residual * new_residual, axis=1)
    new_direction = new_residual + (norm_new / norm_old)[:, None] * direction
    return (new_solution, new_residual, new_direction)
```

```python
import functools
import math

import jax
import jax.numpy as jnp
from jax import lax
from jax.experimental import pallas as pl
from jax.experimental.pallas import tpu as pltpu
from jax.sharding import PartitionSpec as P

LATTICE = 65521

ridge_weight = 0.25
VMEM_BYTES = 48 << 20
STORE_BYTES = 12 << 20
F32 = jnp.float32
BF16 = jnp.bfloat16


def centre_coords(lattice_index, generator):
    upper_digits = generator // 256
    lower_digits = generator % 256
    column = lattice_index[None, :]
    partial_value = column * upper_digits[:, None] % LATTICE
    return (partial_value * 256 + column * lower_digits[:, None]) % LATTICE


def swap(value, bit, devices):
    return lax.ppermute(value, "samp", [(i, i ^ bit) for i in range(devices)])


def reduce_all(value, devices):
    bit = 1
    while bit < devices:
        value = value + swap(value, bit, devices)
        bit *= 2
    return value


def gather_all(value, devices, index):
    bit = 1
    while bit < devices:
        other = swap(value, bit, devices)
        upper = (index & bit) != 0
        value = jnp.where(
            upper,
            jnp.concatenate([other, value], axis=1),
            jnp.concatenate([value, other], axis=1),
        )
        bit *= 2
    return value


def split3(value):
    high = value.astype(BF16)
    rest = value - high.astype(F32)
    middle = rest.astype(BF16)
    low = (rest - middle.astype(F32)).astype(BF16)
    return high, middle, low


def kernel_tile(points, centre_ref, shift_ref, floor_ref, first, width):
    rows, dims = points.shape
    product = None
    for axis_number in range(dims):
        centre = centre_ref[axis_number : axis_number + 1, pl.ds(first, width)]
        point = jnp.broadcast_to(points[:, axis_number : axis_number + 1], (rows, width))
        arm = jnp.abs(point - centre) - shift_ref[axis_number]
        factor = arm * arm + floor_ref[axis_number]
        product = factor if product is None else product * factor
    return product


def fill_kernel(rows, points, centre_ref, shift_ref, floor_ref, high_ref, low_ref):
    centres_all = centre_ref.shape[1]
    width = min(512, centres_all)
    span = min(1024, centres_all)

    def part(base):
        for piece in range(span // width):
            first = base + piece * width
            if not isinstance(first, int):
                first = pl.multiple_of(first, width)
            tile = kernel_tile(points, centre_ref, shift_ref, floor_ref, first, width)
            high = tile.astype(BF16)
            high_ref[rows, pl.ds(first, width)] = high
            low_ref[rows, pl.ds(first, width)] = (tile - high.astype(F32)).astype(BF16)

    if centres_all == span:
        part(0)
    else:
        lax.fori_loop(0, centres_all // span, lambda i, _: part(i * span), None)


def generate(step_rows, shift_ref, floor_ref, scale_ref, sample_ref, centre_ref, high_ref, low_ref):
    for step in range(sample_ref.shape[1] // step_rows):
        rows = pl.ds(step * step_rows, step_rows)
        points = (sample_ref[:, rows].astype(F32) * scale_ref[...]).T
        fill_kernel(rows, points, centre_ref, shift_ref, floor_ref, high_ref, low_ref)


def kernel_rows(samples, first_block, blocks, block_rows, centre_scaled, shift, floor, scale):
    dims, centres_all = centre_scaled.shape
    rows = blocks * block_rows
    smem = pl.BlockSpec(memory_space=pltpu.SMEM)
    return pl.pallas_call(
        functools.partial(generate, 128),
        grid=(blocks,),
        in_specs=[
            smem,
            smem,
            pl.BlockSpec((dims, 1), lambda i: (0, 0)),
            pl.BlockSpec((dims, block_rows), lambda i: (0, first_block + i)),
            pl.BlockSpec((dims, centres_all), lambda i: (0, 0)),
        ],
        out_specs=[pl.BlockSpec((block_rows, centres_all), lambda i: (i, 0))] * 2,
        out_shape=[jax.ShapeDtypeStruct((rows, centres_all), BF16)] * 2,
        compiler_params=pltpu.CompilerParams(vmem_limit_bytes=VMEM_BYTES),
        cost_estimate=pl.CostEstimate(
            flops=6 * dims * rows * centres_all,
            bytes_accessed=4 * rows * centres_all,
            transcendentals=0,
        ),
        name="kernel_rows",
    )(shift, floor, scale, samples, centre_scaled)


def apply_kernel(high, low, coefficients, outs):
    contract = (((1,), (1,)), ((), ()))
    fitted = lax.dot_general(coefficients, high, contract, preferred_element_type=F32)
    fitted = fitted + lax.dot_general(coefficients, low, contract, preferred_element_type=F32)
    return fitted[0:outs] + (fitted[outs : 2 * outs] + fitted[2 * outs : 3 * outs])


def products(
    outs, step_rows, shift_ref, floor_ref, coef_ref, own_ref, centre_ref, first_ref, second_ref,
    backward_ref, own_out_ref, parts_ref, sum_ref, own_high_ref, own_low_ref, *made,
):
    step = pl.program_id(0)
    if made:
        high_ref, low_ref = made
        generate(step_rows, shift_ref, floor_ref, second_ref, first_ref, centre_ref, high_ref, low_ref)
    else:
        high_ref, low_ref = first_ref, second_ref

    @pl.when(step == 0)
    def _():
        high, middle, low = split3(coef_ref[...])
        parts_ref[0:outs] = high
        parts_ref[outs : 2 * outs] = middle
        parts_ref[2 * outs : 3 * outs] = low
        sum_ref[...] = jnp.zeros_like(sum_ref)
        rows = pl.ds(0, own_ref.shape[1])
        fill_kernel(
            rows, own_ref[...].T, centre_ref, shift_ref, floor_ref, own_high_ref, own_low_ref
        )
        own_out_ref[...] = apply_kernel(
            own_high_ref[...], own_low_ref[...], parts_ref[...], outs
        )

    fitted = apply_kernel(high_ref[...], low_ref[...], parts_ref[...], outs)
    parts = jnp.concatenate(split3(fitted), axis=0)
    sum_ref[...] += jnp.dot(parts, high_ref[...], preferred_element_type=F32) + jnp.dot(
        parts, low_ref[...], preferred_element_type=F32
    )

    @pl.when(step == pl.num_programs(0) - 1)
    def _():
        backward_ref[...] = sum_ref[0:outs] + (
            sum_ref[outs : 2 * outs] + sum_ref[2 * outs : 3 * outs]
        )


def apply_products(
    first, second, coefficients, own_scaled, centre_scaled, shift, floor, block_rows, stored
):
    outs, centres_all = coefficients.shape
    dims, own_rows = own_scaled.shape
    rows = first.shape[0] if stored else first.shape[1]
    smem = pl.BlockSpec(memory_space=pltpu.SMEM)

    def whole(shape):
        return pl.BlockSpec(shape, lambda i: (0, 0))

    if stored:
        sources = [pl.BlockSpec((block_rows, centres_all), lambda i: (i, 0))] * 2
        made = []
    else:
        sources = [pl.BlockSpec((dims, block_rows), lambda i: (0, i)), whole((dims, 1))]
        made = [pltpu.VMEM((block_rows, centres_all), BF16)] * 2

    return pl.pallas_call(
        functools.partial(products, outs, 128),
        grid=(rows // block_rows,),
        in_specs=[
            smem,
            smem,
            whole((outs, centres_all)),
            whole((dims, own_rows)),
            whole((dims, centres_all)),
            *sources,
        ],
        out_specs=[whole((outs, centres_all)), whole((outs, own_rows))],
        out_shape=[
            jax.ShapeDtypeStruct((outs, centres_all), F32),
            jax.ShapeDtypeStruct((outs, own_rows), F32),
        ],
        scratch_shapes=[
            pltpu.VMEM((3 * outs, centres_all), BF16),
            pltpu.VMEM((3 * outs, centres_all), F32),
            pltpu.VMEM((own_rows, centres_all), BF16),
            pltpu.VMEM((own_rows, centres_all), BF16),
            *made,
        ],
        compiler_params=pltpu.CompilerParams(vmem_limit_bytes=VMEM_BYTES),
        cost_estimate=pl.CostEstimate(
            flops=24 * outs * rows * centres_all,
            bytes_accessed=4 * rows * centres_all,
            transcendentals=0,
        ),
        name="products",
    )(shift, floor, coefficients, own_scaled, centre_scaled, first, second)


def contract_last(left_array, right_array):
    return lax.dot_general(
        left_array,
        right_array,
        (((1,), (1,)), ((), ())),
        precision=lax.Precision.HIGHEST,
        preferred_element_type=F32,
    )


def body(samples, generator, weight_index, preconditioner, solution, residual, direction):
    highest = lax.Precision.HIGHEST
    devices = lax.axis_size("samp")
    index = lax.axis_index("samp")
    cen_dev, centres_all = preconditioner.shape
    samples_dev = samples.shape[1]
    outs = direction.shape[0]

    weights_dim = 0.5 * jnp.power(0.75, weight_index.astype(F32))
    curve = 2.0 * math.pi * math.pi * weights_dim
    floor = 1.0 - curve / 12.0
    root = jnp.sqrt(curve)
    shift = 0.5 * root
    scale = (root / LATTICE)[:, None]
    centres = centre_coords(jnp.arange(centres_all, dtype=jnp.int32), generator)
    first_row = index * cen_dev
    own = lax.dynamic_slice_in_dim(centres, first_row, cen_dev, 1)
    centre_scaled = centres.astype(F32) * scale
    own_scaled = own.astype(F32) * scale

    state = gather_all(jnp.concatenate([direction, residual], axis=0), devices, index)
    direction_full, residual_full = state[:outs], state[outs:]
    coef_rows = contract_last(direction_full, preconditioner)
    coefficients = gather_all(coef_rows, devices, index)

    block_rows = 256
    stored = 4 * samples_dev * centres_all <= STORE_BYTES
    if stored:
        first, second = kernel_rows(
            samples, 0, samples_dev // block_rows, block_rows, centre_scaled, shift, floor, scale
        )
    else:
        first, second = samples, scale
    backward, kernel_products = apply_products(
        first, second, coefficients, own_scaled, centre_scaled, shift, floor, block_rows, stored
    )
    summed = reduce_all(backward, devices)
    backward_rows = lax.dynamic_slice_in_dim(summed, first_row, cen_dev, 1)
    scale_total = float(samples_dev * devices) * float(centres_all)
    applied = backward_rows / scale_total + ridge_weight * kernel_products / centres_all
    partial_image = jnp.dot(applied, preconditioner, precision=highest, preferred_element_type=F32)
    image = reduce_all(partial_image, devices)

    norm_old = jnp.sum(residual_full * residual_full, axis=1, keepdims=True)
    curvature = jnp.sum(direction_full * image, axis=1, keepdims=True)
    step_length = norm_old / curvature
    next_full = residual_full - step_length * image
    norm_new = jnp.sum(next_full * next_full, axis=1, keepdims=True)
    new_residual = lax.dynamic_slice_in_dim(next_full, first_row, cen_dev, 1)
    new_solution = solution + step_length * direction
    new_direction = new_residual + (norm_new / norm_old) * direction
    return (new_solution, new_residual, new_direction)


def solution(mesh):
    placed = (
        P("groups", "samp"),
        P(),
        P(),
        P("samp", None),
        P("groups", "samp"),
        P("groups", "samp"),
        P("groups", "samp"),
    )
    return jax.shard_map(
        body,
        mesh=mesh,
        in_specs=placed,
        out_specs=(P("groups", "samp"), P("groups", "samp"), P("groups", "samp")),
        check_vma=False,
    )
```

```python
import functools
import math

import jax
import jax.numpy as jnp
from jax import lax
from jax.experimental import pallas as pl
from jax.experimental.pallas import tpu as pltpu
from jax.sharding import PartitionSpec as P

LATTICE = 65521

ridge_weight = 0.25
VMEM_BYTES = 48 << 20
STORE_BYTES = 12 << 20
HELD_BYTES = 16 << 20
F32 = jnp.float32
BF16 = jnp.bfloat16


def centre_coords(lattice_index, generator):
    upper_digits = generator // 256
    lower_digits = generator % 256
    column = lattice_index[None, :]
    partial_value = column * upper_digits[:, None] % LATTICE
    return (partial_value * 256 + column * lower_digits[:, None]) % LATTICE


def swap(value, bit, devices):
    return lax.ppermute(value, "samp", [(i, i ^ bit) for i in range(devices)])


def after(value, *others):
    return lax.optimization_barrier((value, *others))[0]


def reduce_all(value, devices):
    bit = 1
    while bit < devices:
        value = value + swap(value, bit, devices)
        bit *= 2
    return value


def plan(devices, piece_bytes):
    bits = [1 << k for k in range(devices.bit_length() - 1)]
    held = []
    for bit in [b for b in (devices // 4, *bits) if 0 < b < devices // 2]:
        if bit not in held and (2 << len(held)) * piece_bytes <= HELD_BYTES:
            held.append(bit)
    held = held[:1] + held[:0:-1] if len(held) > 1 else held
    return held, [b for b in bits if b not in held]


def split3(value):
    high = value.astype(BF16)
    rest = value - high.astype(F32)
    middle = rest.astype(BF16)
    low = (rest - middle.astype(F32)).astype(BF16)
    return high, middle, low


def kernel_tile(points, centre_ref, shift_ref, floor_ref, first, width):
    rows, dims = points.shape
    product = None
    for axis_number in range(dims):
        centre = centre_ref[axis_number : axis_number + 1, pl.ds(first, width)]
        point = jnp.broadcast_to(points[:, axis_number : axis_number + 1], (rows, width))
        arm = jnp.abs(point - centre) - shift_ref[axis_number]
        factor = arm * arm + floor_ref[axis_number]
        product = factor if product is None else product * factor
    return product


def fill_kernel(rows, points, centre_ref, shift_ref, floor_ref, high_ref, low_ref):
    centres_all = centre_ref.shape[1]
    width = min(512, centres_all)
    span = min(1024, centres_all)

    def part(base):
        for piece in range(span // width):
            first = base + piece * width
            if not isinstance(first, int):
                first = pl.multiple_of(first, width)
            tile = kernel_tile(points, centre_ref, shift_ref, floor_ref, first, width)
            high = tile.astype(BF16)
            high_ref[rows, pl.ds(first, width)] = high
            low_ref[rows, pl.ds(first, width)] = (tile - high.astype(F32)).astype(BF16)

    if centres_all == span:
        part(0)
    else:
        lax.fori_loop(0, centres_all // span, lambda i, _: part(i * span), None)


def generate(step_rows, rows_all, shift_ref, floor_ref, scale_ref, sample_ref, centre_ref, high_ref, low_ref):
    for step in range(rows_all // step_rows):
        rows = pl.ds(step * step_rows, step_rows)
        points = (sample_ref[:, rows].astype(F32) * scale_ref[...]).T
        fill_kernel(rows, points, centre_ref, shift_ref, floor_ref, high_ref, low_ref)


def store_rows(step_rows, shift_ref, floor_ref, scale_ref, sample_ref, centre_ref, *refs):
    high_ref, low_ref, token_ref = refs[-3:]
    generate(
        step_rows, sample_ref.shape[1], shift_ref, floor_ref, scale_ref, sample_ref, centre_ref,
        high_ref, low_ref,
    )
    token_ref[...] = jnp.zeros_like(token_ref)


def kernel_rows(store, samples, first_block, blocks, block_rows, rows_stored, constants):
    centre_scaled, shift, floor, scale = constants
    dims, centres_all = centre_scaled.shape
    rows = blocks * block_rows
    smem = pl.BlockSpec(memory_space=pltpu.SMEM)
    given = [] if store is None else list(store)
    kept = jax.ShapeDtypeStruct((rows_stored, centres_all), BF16)
    high, low, token = pl.pallas_call(
        functools.partial(store_rows, 128),
        grid=(blocks,),
        in_specs=[
            smem,
            smem,
            pl.BlockSpec((dims, 1), lambda i: (0, 0)),
            pl.BlockSpec((dims, block_rows), lambda i: (0, first_block + i)),
            pl.BlockSpec((dims, centres_all), lambda i: (0, 0)),
            *[pl.BlockSpec(memory_space=pl.ANY)] * len(given),
        ],
        out_specs=[
            *[pl.BlockSpec((block_rows, centres_all), lambda i: (first_block + i, 0))] * 2,
            pl.BlockSpec((8, 128), lambda i: (0, 0)),
        ],
        out_shape=[kept, kept, jax.ShapeDtypeStruct((8, 128), F32)],
        input_output_aliases={5: 0, 6: 1} if given else {},
        compiler_params=pltpu.CompilerParams(vmem_limit_bytes=VMEM_BYTES),
        cost_estimate=pl.CostEstimate(
            flops=6 * dims * rows * centres_all,
            bytes_accessed=4 * rows * centres_all,
            transcendentals=0,
        ),
        name="kernel_rows",
    )(shift, floor, scale, samples, centre_scaled, *given)
    return (high, low), token


def apply_kernel(high, low, coefficients, outs):
    contract = (((1,), (1,)), ((), ()))
    fitted = lax.dot_general(coefficients, high, contract, preferred_element_type=F32)
    fitted = fitted + lax.dot_general(coefficients, low, contract, preferred_element_type=F32)
    return fitted[0:outs] + (fitted[outs : 2 * outs] + fitted[2 * outs : 3 * outs])


def back_products(high, low, coefficients, outs):
    parts = jnp.concatenate(split3(apply_kernel(high, low, coefficients, outs)), axis=0)
    return jnp.dot(parts, high, preferred_element_type=F32) + jnp.dot(
        parts, low, preferred_element_type=F32
    )


def products(
    outs, step_rows, stored, shift_ref, floor_ref, scale_ref, coef_ref, own_ref, centre_ref,
    sample_ref, *refs,
):
    step = pl.program_id(0)
    steps = pl.num_programs(0)
    if stored:
        high_ref, low_ref, *refs = refs
    backward_ref, own_out_ref, parts_ref, sum_ref, made_high, made_low = refs
    own_rows = own_ref.shape[1]

    @pl.when(step == 0)
    def _():
        high, middle, low = split3(coef_ref[...])
        parts_ref[0:outs] = high
        parts_ref[outs : 2 * outs] = middle
        parts_ref[2 * outs : 3 * outs] = low
        sum_ref[...] = jnp.zeros_like(sum_ref)
        own_high, own_low = made_high.at[1], made_low.at[1]
        rows = pl.ds(0, own_rows)
        fill_kernel(rows, own_ref[...].T, centre_ref, shift_ref, floor_ref, own_high, own_low)
        own_out_ref[...] = apply_kernel(own_high[rows], own_low[rows], parts_ref[...], outs)
        made_high[1] = jnp.zeros(made_high.shape[1:], BF16)
        made_low[1] = jnp.zeros(made_low.shape[1:], BF16)

    now = lax.rem(step, 2)
    coefficients = parts_ref[...]
    before = 1 - now
    total = back_products(made_high[before], made_low[before], coefficients, outs)
    if stored:
        total = total + back_products(high_ref[...], low_ref[...], coefficients, outs)
    generate(
        step_rows, sample_ref.shape[1], shift_ref, floor_ref, scale_ref, sample_ref, centre_ref,
        made_high.at[now], made_low.at[now],
    )
    sum_ref[...] += total

    @pl.when(step == steps - 1)
    def _():
        last = sum_ref[...] + back_products(made_high[now], made_low[now], coefficients, outs)
        backward_ref[...] = last[0:outs] + (last[outs : 2 * outs] + last[2 * outs : 3 * outs])


def apply_products(store, samples, coefficients, own_scaled, block_rows, constants):
    centre_scaled, shift, floor, scale = constants
    outs, centres_all = coefficients.shape
    dims, own_rows = own_scaled.shape
    rows_stored = 0 if store is None else store[0].shape[0]
    first = rows_stored // block_rows
    steps = samples.shape[1] // block_rows - first
    smem = pl.BlockSpec(memory_space=pltpu.SMEM)

    def whole(shape):
        return pl.BlockSpec(shape, lambda i: (0, 0))

    made = pltpu.VMEM((2, block_rows, centres_all), BF16)
    given = [] if store is None else list(store)
    return pl.pallas_call(
        functools.partial(products, outs, 128, store is not None),
        grid=(steps,),
        in_specs=[
            smem,
            smem,
            whole((dims, 1)),
            whole((outs, centres_all)),
            whole((dims, own_rows)),
            whole((dims, centres_all)),
            pl.BlockSpec((dims, block_rows), lambda i: (0, first + i)),
            *[pl.BlockSpec((block_rows, centres_all), lambda i: (i, 0))] * len(given),
        ],
        out_specs=[whole((outs, centres_all)), whole((outs, own_rows))],
        out_shape=[
            jax.ShapeDtypeStruct((outs, centres_all), F32),
            jax.ShapeDtypeStruct((outs, own_rows), F32),
        ],
        scratch_shapes=[
            pltpu.VMEM((3 * outs, centres_all), BF16),
            pltpu.VMEM((3 * outs, centres_all), F32),
            made,
            made,
        ],
        compiler_params=pltpu.CompilerParams(vmem_limit_bytes=VMEM_BYTES),
        cost_estimate=pl.CostEstimate(
            flops=6 * dims * steps * block_rows * centres_all,
            bytes_accessed=4 * rows_stored * centres_all,
            transcendentals=0,
        ),
        name="products",
    )(shift, floor, scale, coefficients, own_scaled, centre_scaled, samples, *given)


def contract_last(left_array, right_array):
    return lax.dot_general(
        left_array,
        right_array,
        (((1,), (1,)), ((), ())),
        precision=lax.Precision.HIGHEST,
        preferred_element_type=F32,
    )


def body(samples, generator, weight_index, preconditioner, solution, residual, direction):
    highest = lax.Precision.HIGHEST
    devices = lax.axis_size("samp")
    index = lax.axis_index("samp")
    cen_dev, centres_all = preconditioner.shape
    samples_dev = samples.shape[1]
    outs = direction.shape[0]
    held, others = plan(devices, 4 * cen_dev * centres_all)

    weights_dim = 0.5 * jnp.power(0.75, weight_index.astype(F32))
    curve = 2.0 * math.pi * math.pi * weights_dim
    floor = 1.0 - curve / 12.0
    root = jnp.sqrt(curve)
    shift = 0.5 * root
    scale = (root / LATTICE)[:, None]

    order = [0]
    for bit in (*held, *others):
        order = order + [k ^ bit for k in order]
    owners = index ^ jnp.array(order, jnp.int32)
    lattice_index = owners[:, None] * cen_dev + jnp.arange(cen_dev, dtype=jnp.int32)[None, :]
    centres = centre_coords(lattice_index.reshape(centres_all), generator)
    centre_scaled = centres.astype(F32) * scale
    own_scaled = centre_scaled[:, :cen_dev]
    constants = (centre_scaled, shift, floor, scale)

    block_rows = 128
    half = samples_dev // 2
    use_store = 4 * half * centres_all <= STORE_BYTES
    store, token, filled = None, None, 0

    def fill(blocks, *ready):
        nonlocal store, token, filled
        if use_store:
            blocks = min(blocks, half // block_rows - filled)
            if blocks > 0:
                tied = (centre_scaled, shift, floor, after(scale, *ready))
                store, token = kernel_rows(
                    store, samples, filled, blocks, block_rows, half, tied
                )
                filled += blocks

    def then(value):
        return value if token is None else after(value, token)

    state = jnp.concatenate([direction, residual], axis=0)
    pieces = [preconditioner]
    waiting = list(held)
    bit = 1
    while bit < devices:
        if waiting and bit in (1, devices // 4):
            pieces.append(swap(jnp.concatenate(pieces, axis=0), waiting.pop(0), devices))
        tied = then(state)
        other = swap(tied, bit, devices)
        if bit > 1:
            fill(2 if 2 * bit == devices else 1, tied)
        upper = (index & bit) != 0
        state = jnp.where(
            upper,
            jnp.concatenate([other, tied], axis=1),
            jnp.concatenate([tied, other], axis=1),
        )
        bit *= 2
    direction_full, residual_full = state[:outs], state[outs:]
    fill(2, state)
    for bit in waiting:
        joined = jnp.concatenate(pieces, axis=0)
        pieces.append(swap(then(joined), bit, devices))

    coefficients = jnp.concatenate([contract_last(direction_full, p) for p in pieces], axis=1)
    for bit in others:
        tied = then(coefficients)
        other = swap(tied, bit, devices)
        fill(2, tied)
        coefficients = jnp.concatenate([tied, other], axis=1)
    fill(half // block_rows, coefficients)

    backward, kernel_products = apply_products(
        store, samples, coefficients, own_scaled, 256, constants
    )
    for bit in reversed(others):
        width = backward.shape[1] // 2
        backward = backward[:, :width] + swap(backward[:, width:], bit, devices)
    scale_total = float(samples_dev * devices) * float(centres_all)
    own_term = ridge_weight * kernel_products / centres_all
    applied = backward / scale_total + jnp.pad(
        own_term, ((0, 0), (0, backward.shape[1] - cen_dev))
    )
    partial_image, first = 0.0, 0
    for p in pieces:
        part = applied[:, first : first + p.shape[0]]
        partial_image += jnp.dot(part, p, precision=highest, preferred_element_type=F32)
        first += p.shape[0]
    image = reduce_all(partial_image, devices)

    first_row = index * cen_dev
    norm_old = jnp.sum(residual_full * residual_full, axis=1, keepdims=True)
    curvature = jnp.sum(direction_full * image, axis=1, keepdims=True)
    step_length = norm_old / curvature
    next_full = residual_full - step_length * image
    norm_new = jnp.sum(next_full * next_full, axis=1, keepdims=True)
    new_residual = lax.dynamic_slice_in_dim(next_full, first_row, cen_dev, 1)
    new_solution = solution + step_length * direction
    new_direction = new_residual + (norm_new / norm_old) * direction
    return (new_solution, new_residual, new_direction)


def solution(mesh):
    placed = (
        P("groups", "samp"),
        P(),
        P(),
        P("samp", None),
        P("groups", "samp"),
        P("groups", "samp"),
        P("groups", "samp"),
    )
    return jax.shard_map(
        body,
        mesh=mesh,
        in_specs=placed,
        out_specs=(P("groups", "samp"), P("groups", "samp"), P("groups", "samp")),
        check_vma=False,
    )
```

```python
import functools
import math

import jax
import jax.numpy as jnp
from jax import lax
from jax.experimental import pallas as pl
from jax.experimental.pallas import tpu as pltpu
from jax.sharding import PartitionSpec as P

LATTICE = 65521

ridge_weight = 0.25
VMEM_BYTES = 48 << 20
STORE_BYTES = 12 << 20
HELD_BYTES = 16 << 20
F32 = jnp.float32
BF16 = jnp.bfloat16


def swap(value, bit, devices):
    return lax.ppermute(value, "samp", [(i, i ^ bit) for i in range(devices)])


def after(value, *others):
    return lax.optimization_barrier((value, *others))[0]


def reduce_all(value, devices):
    bit = 1
    while bit < devices:
        value = value + swap(value, bit, devices)
        bit *= 2
    return value


def plan(devices, piece_bytes):
    bits = [1 << k for k in range(devices.bit_length() - 1)]
    held = []
    for bit in [b for b in (devices // 4, *bits) if 0 < b < devices // 2]:
        if bit not in held and (2 << len(held)) * piece_bytes <= HELD_BYTES:
            held.append(bit)
    held = held[:1] + held[:0:-1] if len(held) > 1 else held
    return held, [b for b in bits if b not in held]


def split3(value):
    high = value.astype(BF16)
    rest = value - high.astype(F32)
    middle = rest.astype(BF16)
    low = (rest - middle.astype(F32)).astype(BF16)
    return high, middle, low


def kernel_tile(points, centre_ref, shift_ref, floor_ref, first, width):
    rows, dims = points.shape
    product = None
    for axis_number in range(dims):
        centre = centre_ref[axis_number : axis_number + 1, pl.ds(first, width)]
        point = jnp.broadcast_to(points[:, axis_number : axis_number + 1], (rows, width))
        arm = jnp.abs(point - centre) - shift_ref[axis_number]
        factor = arm * arm + floor_ref[axis_number]
        product = factor if product is None else product * factor
    return product


def fill_kernel(rows, points, centre_ref, shift_ref, floor_ref, high_ref, low_ref):
    centres_all = centre_ref.shape[1]
    width = min(512, centres_all)
    span = min(1024, centres_all)

    def part(base):
        for piece in range(span // width):
            first = base + piece * width
            if not isinstance(first, int):
                first = pl.multiple_of(first, width)
            tile = kernel_tile(points, centre_ref, shift_ref, floor_ref, first, width)
            high = tile.astype(BF16)
            high_ref[rows, pl.ds(first, width)] = high
            low_ref[rows, pl.ds(first, width)] = (tile - high.astype(F32)).astype(BF16)

    if centres_all == span:
        part(0)
    else:
        lax.fori_loop(0, centres_all // span, lambda i, _: part(i * span), None)


def generate(step_rows, rows_all, shift_ref, floor_ref, scale_ref, sample_ref, centre_ref, high_ref, low_ref):
    for step in range(rows_all // step_rows):
        rows = pl.ds(step * step_rows, step_rows)
        points = (sample_ref[:, rows].astype(F32) * scale_ref[...]).T
        fill_kernel(rows, points, centre_ref, shift_ref, floor_ref, high_ref, low_ref)


def store_rows(
    row_sets, step_rows, shift_ref, floor_ref, scale_ref, sample_ref, centre_ref, ready_ref, *refs
):
    high_ref, low_ref, token_ref = refs[-3:]
    del ready_ref

    def step(i, _):
        first = pl.multiple_of(row_sets[0] + i * step_rows, step_rows)
        rows = pl.ds(first, step_rows)
        points = (sample_ref[:, rows].astype(F32) * scale_ref[...]).T
        fill_kernel(rows, points, centre_ref, shift_ref, floor_ref, high_ref, low_ref)

    lax.fori_loop(0, row_sets[1], step, None)
    token_ref[...] = jnp.zeros_like(token_ref)


def kernel_rows(store, ready, samples, first_row, rows, rows_stored, constants):
    centre_scaled, shift, floor, scale = constants
    dims, centres_all = centre_scaled.shape
    smem = pl.BlockSpec(memory_space=pltpu.SMEM)
    vmem = pl.BlockSpec(memory_space=pltpu.VMEM)
    free = pl.BlockSpec(memory_space=pl.ANY)
    given = [] if store is None else list(store)
    kept = pltpu.VMEM((rows_stored, centres_all), BF16)
    step_rows = min(128, rows)
    high, low, token = pl.pallas_call(
        functools.partial(store_rows, (first_row, rows // step_rows), step_rows),
        in_specs=[smem, smem, vmem, vmem, vmem, free, *[vmem] * len(given)],
        out_specs=[vmem, vmem, vmem],
        out_shape=[kept, kept, jax.ShapeDtypeStruct((8, 128), jnp.int32)],
        input_output_aliases={6: 0, 7: 1} if given else {},
        compiler_params=pltpu.CompilerParams(vmem_limit_bytes=VMEM_BYTES),
        cost_estimate=pl.CostEstimate(
            flops=6 * dims * rows * centres_all,
            bytes_accessed=4 * rows * centres_all,
            transcendentals=0,
        ),
        name="kernel_rows",
    )(shift, floor, scale, samples, centre_scaled, ready, *given)
    return (high, low), token[0, 0]


def apply_kernel(high, low, coefficients, outs):
    contract = (((1,), (1,)), ((), ()))
    fitted = lax.dot_general(coefficients, high, contract, preferred_element_type=F32)
    fitted = fitted + lax.dot_general(coefficients, low, contract, preferred_element_type=F32)
    return fitted[0:outs] + (fitted[outs : 2 * outs] + fitted[2 * outs : 3 * outs])


def back_products(high, low, coefficients, outs):
    parts = jnp.concatenate(split3(apply_kernel(high, low, coefficients, outs)), axis=0)
    return jnp.dot(parts, high, preferred_element_type=F32) + jnp.dot(
        parts, low, preferred_element_type=F32
    )


def products(
    outs, block_rows, stored_rows, shift_ref, floor_ref, scale_ref, coef_ref, own_ref, centre_ref,
    sample_ref, *refs,
):
    if stored_rows:
        high_ref, low_ref, *refs = refs
    backward_ref, own_out_ref, parts_ref, sum_ref, made_high, made_low = refs
    own_rows = own_ref.shape[1]
    steps = (sample_ref.shape[1] - stored_rows) // block_rows
    share = stored_rows // steps

    high, middle, low = split3(coef_ref[...])
    parts_ref[0:outs] = high
    parts_ref[outs : 2 * outs] = middle
    parts_ref[2 * outs : 3 * outs] = low
    sum_ref[...] = jnp.zeros_like(sum_ref)
    own_high, own_low = made_high.at[1], made_low.at[1]
    rows = pl.ds(0, own_rows)
    fill_kernel(rows, own_ref[...].T, centre_ref, shift_ref, floor_ref, own_high, own_low)
    own_out_ref[...] = apply_kernel(own_high[rows], own_low[rows], parts_ref[...], outs)
    made_high[1] = jnp.zeros(made_high.shape[1:], BF16)
    made_low[1] = jnp.zeros(made_low.shape[1:], BF16)

    def step(i, _):
        now = lax.rem(i, 2)
        before = 1 - now
        coefficients = parts_ref[...]
        total = back_products(made_high[before], made_low[before], coefficients, outs)
        if share:
            rows = pl.ds(pl.multiple_of(i * share, share), share)
            total = total + back_products(high_ref[rows], low_ref[rows], coefficients, outs)
        columns = pl.ds(pl.multiple_of(stored_rows + i * block_rows, block_rows), block_rows)
        points = (sample_ref[:, columns].astype(F32) * scale_ref[...]).T
        for first in range(0, block_rows, 128):
            rows = pl.ds(first, 128)
            fill_kernel(
                rows, points[first : first + 128], centre_ref, shift_ref, floor_ref,
                made_high.at[now], made_low.at[now],
            )
        sum_ref[...] += total

    lax.fori_loop(0, steps, step, None)
    now = (steps - 1) % 2
    last = sum_ref[...] + back_products(made_high[now], made_low[now], parts_ref[...], outs)
    backward_ref[...] = last[0:outs] + (last[outs : 2 * outs] + last[2 * outs : 3 * outs])


def apply_products(store, samples, coefficients, own_scaled, block_rows, constants):
    centre_scaled, shift, floor, scale = constants
    outs, centres_all = coefficients.shape
    dims, own_rows = own_scaled.shape
    given = [] if store is None else list(store)
    stored_rows = given[0].shape[0] if given else 0
    smem = pl.BlockSpec(memory_space=pltpu.SMEM)
    vmem = pl.BlockSpec(memory_space=pltpu.VMEM)
    made = pltpu.VMEM((2, block_rows, centres_all), BF16)
    return pl.pallas_call(
        functools.partial(products, outs, block_rows, stored_rows),
        in_specs=[smem, smem, *[vmem] * (5 + len(given))],
        out_specs=[vmem, vmem],
        out_shape=[
            jax.ShapeDtypeStruct((outs, centres_all), F32),
            jax.ShapeDtypeStruct((outs, own_rows), F32),
        ],
        scratch_shapes=[
            pltpu.VMEM((3 * outs, centres_all), BF16),
            pltpu.VMEM((3 * outs, centres_all), F32),
            made,
            made,
        ],
        compiler_params=pltpu.CompilerParams(vmem_limit_bytes=VMEM_BYTES),
        cost_estimate=pl.CostEstimate(
            flops=6 * dims * (samples.shape[1] - stored_rows) * centres_all,
            bytes_accessed=4 * stored_rows * centres_all,
            transcendentals=0,
        ),
        name="products",
    )(shift, floor, scale, coefficients, own_scaled, centre_scaled, samples, *given)


def modulo(value):
    turns = (value.astype(F32) * (1.0 / LATTICE)).astype(jnp.int32)
    rest = value - turns * LATTICE
    rest = jnp.where(rest < 0, rest + LATTICE, rest)
    return jnp.where(rest >= LATTICE, rest - LATTICE, rest)


def prepare(lattice_ref, generator_ref, scale_ref, direction_ref, residual_ref, state_ref, centre_ref):
    outs = direction_ref.shape[0]
    state_ref[:outs] = direction_ref[...]
    state_ref[outs:] = residual_ref[...]
    generator = generator_ref[...]
    column = lattice_ref[...]
    upper = modulo(column * (generator >> 8))
    centre = modulo(upper * 256 + column * (generator & 255))
    centre_ref[...] = centre.astype(F32) * scale_ref[...]


def contract_last(left_array, right_array):
    return lax.dot_general(
        left_array,
        right_array,
        (((1,), (1,)), ((), ())),
        precision=lax.Precision.HIGHEST,
        preferred_element_type=F32,
    )


def body(samples, generator, weight_index, preconditioner, solution, residual, direction):
    highest = lax.Precision.HIGHEST
    devices = lax.axis_size("samp")
    index = lax.axis_index("samp")
    cen_dev, centres_all = preconditioner.shape
    samples_dev = samples.shape[1]
    outs = direction.shape[0]
    held, others = plan(devices, 4 * cen_dev * centres_all)

    weights_dim = 0.5 * jnp.power(0.75, weight_index.astype(F32))
    curve = 2.0 * math.pi * math.pi * weights_dim
    floor = 1.0 - curve / 12.0
    root = jnp.sqrt(curve)
    shift = 0.5 * root
    scale = (root / LATTICE)[:, None]

    order = [0]
    for bit in (*held, *others):
        order = order + [k ^ bit for k in order]
    lattice_index = (index ^ jnp.array(order, jnp.int32))[:, None] * cen_dev
    lattice_index = lattice_index + jnp.arange(cen_dev, dtype=jnp.int32)[None, :]
    state, centre_scaled = pl.pallas_call(
        prepare,
        out_shape=[
            jax.ShapeDtypeStruct((2 * outs, cen_dev), F32),
            jax.ShapeDtypeStruct((generator.shape[0], centres_all), F32),
        ],
        name="prepare",
    )(lattice_index.reshape(1, centres_all), generator[:, None], scale, direction, residual)
    own_scaled = centre_scaled[:, :cen_dev]
    constants = (centre_scaled, shift, floor, scale)

    half = samples_dev // 2
    use_store = 4 * half * centres_all <= STORE_BYTES
    store, filled = None, 0

    def fill(rows, ready):
        nonlocal store, filled
        rows = min(rows, half - filled) if use_store else 0
        if rows == 0:
            return 0
        store, token = kernel_rows(store, ready, samples, filled, rows, half, constants)
        filled += rows
        return token

    pieces = [preconditioner]
    early = [swap(preconditioner, bit, devices) for bit in held[:2]]
    pieces += early[:1]
    if len(early) > 1:
        pieces += [early[1], swap(early[0], held[1], devices)]
    bit = 1
    while bit < devices:
        other = swap(state, bit, devices)
        token = 0
        if bit > 1:
            token = fill(256 if 2 * bit == devices else 128, state)
        upper = (index & bit) + token != 0
        state = jnp.where(
            upper,
            jnp.concatenate([other, state], axis=1),
            jnp.concatenate([state, other], axis=1),
        )
        bit *= 2
    direction_full, residual_full = state[:outs], state[outs:]
    for bit in held[2:]:
        pieces += [swap(p, bit, devices) for p in pieces]

    coefficients = jnp.concatenate([contract_last(direction_full, p) for p in pieces], axis=1)
    token = fill(256, state)
    for bit in others:
        other = swap(coefficients, bit, devices)
        token = token + fill(256, coefficients)
        coefficients = jnp.concatenate([coefficients, other + jnp.asarray(token, F32)], axis=1)
    if use_store and filled < half:
        fill(half, coefficients)

    backward, kernel_products = apply_products(
        store, samples, coefficients, own_scaled, 256, constants
    )
    for bit in reversed(others):
        width = backward.shape[1] // 2
        backward = backward[:, :width] + swap(backward[:, width:], bit, devices)
    scale_total = float(samples_dev * devices) * float(centres_all)
    own_term = ridge_weight * kernel_products / centres_all
    applied = backward / scale_total + jnp.pad(
        own_term, ((0, 0), (0, backward.shape[1] - cen_dev))
    )
    partial_image, first = 0.0, 0
    for p in pieces:
        part = applied[:, first : first + p.shape[0]]
        partial_image += jnp.dot(part, p, precision=highest, preferred_element_type=F32)
        first += p.shape[0]
    image = reduce_all(partial_image, devices)

    first_row = index * cen_dev
    norm_old = jnp.sum(residual_full * residual_full, axis=1, keepdims=True)
    curvature = jnp.sum(direction_full * image, axis=1, keepdims=True)
    step_length = norm_old / curvature
    next_full = residual_full - step_length * image
    norm_new = jnp.sum(next_full * next_full, axis=1, keepdims=True)
    new_residual = lax.dynamic_slice_in_dim(next_full, first_row, cen_dev, 1)
    new_solution = solution + step_length * direction
    new_direction = new_residual + (norm_new / norm_old) * direction
    return (new_solution, new_residual, new_direction)


def solution(mesh):
    placed = (
        P("groups", "samp"),
        P(),
        P(),
        P("samp", None),
        P("groups", "samp"),
        P("groups", "samp"),
        P("groups", "samp"),
    )
    return jax.shard_map(
        body,
        mesh=mesh,
        in_specs=placed,
        out_specs=(P("groups", "samp"), P("groups", "samp"), P("groups", "samp")),
        check_vma=False,
    )
```

```python
import functools
import math

import jax
import jax.numpy as jnp
from jax import lax
from jax.experimental import pallas as pl
from jax.experimental.pallas import tpu as pltpu
from jax.sharding import PartitionSpec as P

LATTICE = 65521

ridge_weight = 0.25
STORE_BYTES = 12 << 20
HELD_BYTES = 16 << 20
VMEM = pl.BlockSpec(memory_space=pltpu.VMEM)
SMEM = pl.BlockSpec(memory_space=pltpu.SMEM)
F32 = jnp.float32
BF16 = jnp.bfloat16


def swap(value, bit, devices):
    return lax.ppermute(value, "samp", [(i, i ^ bit) for i in range(devices)])


def plan(devices, piece_bytes):
    bits = [1 << k for k in range(devices.bit_length() - 1)]
    held = []
    for bit in [b for b in (devices // 4, *bits) if 0 < b < devices // 2]:
        if bit not in held and (2 << len(held)) * piece_bytes <= HELD_BYTES:
            held.append(bit)
    held = held[:1] + held[:0:-1] if len(held) > 1 else held
    return held, [b for b in bits if b not in held]


def split3(value):
    high = value.astype(BF16)
    rest = value - high.astype(F32)
    middle = rest.astype(BF16)
    low = (rest - middle.astype(F32)).astype(BF16)
    return high, middle, low


def stack3(value):
    return jnp.concatenate(split3(value), axis=0)


def add_parts(value, outs):
    return value[:outs] + (value[outs : 2 * outs] + value[2 * outs :])


def kernel_tile(points, centre_ref, shift_ref, floor_ref, first, width):
    rows, dims = points.shape
    product = None
    for axis_number in range(dims):
        centre = centre_ref[axis_number : axis_number + 1, pl.ds(first, width)]
        point = jnp.broadcast_to(points[:, axis_number : axis_number + 1], (rows, width))
        arm = jnp.abs(point - centre) - shift_ref[axis_number]
        factor = arm * arm + floor_ref[axis_number]
        product = factor if product is None else product * factor
    return product


def fill_kernel(rows, points, centre_ref, shift_ref, floor_ref, high_ref, low_ref):
    centres_all = centre_ref.shape[1]
    width = min(512, centres_all)
    span = min(1024, centres_all)

    def part(base):
        for piece in range(span // width):
            first = base + piece * width
            if not isinstance(first, int):
                first = pl.multiple_of(first, width)
            tile = kernel_tile(points, centre_ref, shift_ref, floor_ref, first, width)
            high = tile.astype(BF16)
            high_ref[rows, pl.ds(first, width)] = high
            low_ref[rows, pl.ds(first, width)] = (tile - high.astype(F32)).astype(BF16)

    if centres_all == span:
        part(0)
    else:
        lax.fori_loop(0, centres_all // span, lambda i, _: part(i * span), None)


def store_rows(row_set, step_rows, shift_ref, floor_ref, scale_ref, sample_ref, centre_ref, passed_ref, *refs):
    high_ref, low_ref, handed_ref = refs[-3:]

    def step(i, _):
        first = pl.multiple_of(row_set[0] + i * step_rows, step_rows)
        rows = pl.ds(first, step_rows)
        points = (sample_ref[:, rows].astype(F32) * scale_ref[...]).T
        fill_kernel(rows, points, centre_ref, shift_ref, floor_ref, high_ref, low_ref)

    lax.fori_loop(0, row_set[1], step, None)
    handed_ref[...] = passed_ref[...]


def kernel_rows(store, passed, samples, first_row, rows, rows_stored, constants):
    centre_scaled, shift, floor, scale = constants
    dims, centres_all = centre_scaled.shape
    given = [] if store is None else list(store)
    kept = pltpu.VMEM((rows_stored, centres_all), BF16)
    step_rows = min(128, rows)
    high, low, handed = pl.pallas_call(
        functools.partial(store_rows, (first_row, rows // step_rows), step_rows),
        in_specs=[SMEM, SMEM, *[VMEM] * (4 + len(given))],
        out_specs=[VMEM, VMEM, VMEM],
        out_shape=[kept, kept, jax.ShapeDtypeStruct(passed.shape, passed.dtype)],
        input_output_aliases={6: 0, 7: 1} if given else {},
        compiler_params=pltpu.CompilerParams(vmem_limit_bytes=8 << 20),
        cost_estimate=pl.CostEstimate(
            flops=6 * dims * rows * centres_all,
            bytes_accessed=4 * rows * centres_all,
            transcendentals=0,
        ),
        name="kernel_rows",
    )(shift, floor, scale, samples, centre_scaled, passed, *given)
    return (high, low), handed


def apply_kernel(high, low, coefficients, outs):
    contract = (((1,), (1,)), ((), ()))
    fitted = lax.dot_general(coefficients, high, contract, preferred_element_type=F32)
    fitted = fitted + lax.dot_general(coefficients, low, contract, preferred_element_type=F32)
    return add_parts(fitted, outs)


def back_products(high, low, coefficients, outs):
    parts = stack3(apply_kernel(high, low, coefficients, outs))
    return jnp.dot(parts, high, preferred_element_type=F32) + jnp.dot(
        parts, low, preferred_element_type=F32
    )


def products(
    outs, block_rows, stored_rows, shift_ref, floor_ref, scale_ref, coef_ref, centre_ref,
    sample_ref, *refs,
):
    if stored_rows:
        high_ref, low_ref, *refs = refs
    *backward_refs, own_out_ref, parts_ref, sum_ref, made_high, made_low = refs
    own_rows = own_out_ref.shape[1]
    steps = (sample_ref.shape[1] - stored_rows) // block_rows
    share = stored_rows // steps

    parts_ref[...] = stack3(coef_ref[...])
    sum_ref[...] = jnp.zeros_like(sum_ref)
    own_high, own_low = made_high.at[1], made_low.at[1]
    rows = pl.ds(0, own_rows)
    own_points = centre_ref[:, :own_rows]
    fill_kernel(rows, own_points.T, centre_ref, shift_ref, floor_ref, own_high, own_low)
    own_out_ref[...] = apply_kernel(own_high[rows], own_low[rows], parts_ref[...], outs)
    made_high[1] = jnp.zeros(made_high.shape[1:], BF16)
    made_low[1] = jnp.zeros(made_low.shape[1:], BF16)

    def step(i, _):
        now = lax.rem(i, 2)
        before = 1 - now
        coefficients = parts_ref[...]
        total = back_products(made_high[before], made_low[before], coefficients, outs)
        if share:
            rows = pl.ds(pl.multiple_of(i * share, share), share)
            total = total + back_products(high_ref[rows], low_ref[rows], coefficients, outs)
        columns = pl.ds(pl.multiple_of(stored_rows + i * block_rows, block_rows), block_rows)
        points = (sample_ref[:, columns].astype(F32) * scale_ref[...]).T
        for first in range(0, block_rows, 128):
            rows = pl.ds(first, 128)
            fill_kernel(
                rows, points[first : first + 128], centre_ref, shift_ref, floor_ref,
                made_high.at[now], made_low.at[now],
            )
        sum_ref[...] += total

    lax.fori_loop(0, steps, step, None)
    now = (steps - 1) % 2
    last = sum_ref[...] + back_products(made_high[now], made_low[now], parts_ref[...], outs)
    last = add_parts(last, outs)
    width = last.shape[1] // len(backward_refs)
    for i, backward_ref in enumerate(backward_refs):
        backward_ref[...] = last[:, i * width : (i + 1) * width]


def apply_products(store, samples, coefficients, own_rows, block_rows, constants):
    centre_scaled, shift, floor, scale = constants
    outs, centres_all = coefficients.shape
    dims = centre_scaled.shape[0]
    given = [] if store is None else list(store)
    stored_rows = given[0].shape[0] if given else 0
    made = pltpu.VMEM((2, block_rows, centres_all), BF16)
    return pl.pallas_call(
        functools.partial(products, outs, block_rows, stored_rows),
        in_specs=[SMEM, SMEM, *[VMEM] * (4 + len(given))],
        out_specs=[VMEM, VMEM, VMEM],
        out_shape=[
            jax.ShapeDtypeStruct((outs, centres_all // 2), F32),
            jax.ShapeDtypeStruct((outs, centres_all // 2), F32),
            jax.ShapeDtypeStruct((outs, own_rows), F32),
        ],
        scratch_shapes=[
            pltpu.VMEM((3 * outs, centres_all), BF16),
            pltpu.VMEM((3 * outs, centres_all), F32),
            made,
            made,
        ],
        compiler_params=pltpu.CompilerParams(vmem_limit_bytes=(10 << 20) + 16 * block_rows * centres_all),
        cost_estimate=pl.CostEstimate(
            flops=6 * dims * (samples.shape[1] - stored_rows) * centres_all,
            bytes_accessed=4 * stored_rows * centres_all,
            transcendentals=0,
        ),
        name="products",
    )(shift, floor, scale, coefficients, centre_scaled, samples, *given)


def modulo(value):
    turns = (value.astype(F32) * (1.0 / LATTICE)).astype(jnp.int32)
    rest = value - turns * LATTICE
    rest = jnp.where(rest < 0, rest + LATTICE, rest)
    return jnp.where(rest >= LATTICE, rest - LATTICE, rest)


def prepare(order_bits, cen_dev, generator_ref, root_ref, scale_ref, centre_ref):
    dims, centres_all = centre_ref.shape
    row = lax.broadcasted_iota(jnp.int32, (dims, 1), 0)
    generator = jnp.zeros((dims, 1), jnp.int32)
    root = jnp.zeros((dims, 1), F32)
    for axis_number in range(dims):
        here = row == axis_number
        generator = jnp.where(here, generator_ref[axis_number], generator)
        root = jnp.where(here, root_ref[axis_number], root)
    scale = root * (1.0 / LATTICE)
    scale_ref[...] = scale
    place = lax.broadcasted_iota(jnp.int32, (1, centres_all), 1)
    owner = jnp.zeros_like(place) + lax.axis_index("samp")
    for k, bit in enumerate(order_bits):
        block_bit = cen_dev << k
        owner = jnp.where((place & block_bit) != 0, owner ^ bit, owner)
    column = owner * cen_dev + (place & (cen_dev - 1))
    upper = modulo(column * (generator >> 8))
    centre = modulo(upper * 256 + column * (generator & 255))
    centre_ref[...] = centre.astype(F32) * scale


def row_products(outs, count, state_ref, *refs):
    coef_ref, parts_ref = refs[count:]
    state = stack3(state_ref[:outs])
    cen_dev = refs[0].shape[0]
    for i, piece_ref in enumerate(refs[:count]):
        rows = slice(i * cen_dev, (i + 1) * cen_dev)
        for k, part in enumerate(split3(piece_ref[...])):
            parts_ref[k, rows] = part
    total = None
    for k in range(3):
        term = lax.dot_general(
            state, parts_ref[k], (((1,), (1,)), ((), ())), preferred_element_type=F32
        )
        total = term if total is None else total + term
    coef_ref[...] = add_parts(total, outs)


def image_rows(scale_total, ridge, kept_ref, came_ref, own_ref, *refs):
    *part_refs, image_ref = refs
    outs, cen_dev = own_ref.shape
    applied = (kept_ref[...] + came_ref[...]) * (1.0 / scale_total)
    own = ridge * own_ref[...]
    rest = applied.shape[1] - cen_dev
    if rest:
        own = jnp.concatenate([own, jnp.zeros((outs, rest), F32)], axis=1)
    rows = stack3(applied + own)
    total, first = None, 0
    for part_ref in part_refs:
        some = rows[:, first : first + part_ref.shape[1]]
        first += part_ref.shape[1]
        for k in range(3):
            term = jnp.dot(some, part_ref[k], preferred_element_type=F32)
            total = term if total is None else total + term
    image_ref[...] = add_parts(total, outs)


def finish(
    image_ref, more_ref, state_ref, solution_ref, residual_ref, direction_ref,
    new_solution_ref, new_residual_ref, new_direction_ref,
):
    outs, cen_dev = solution_ref.shape
    image = image_ref[...] + more_ref[...]
    residual_full = state_ref[outs:]
    norm_old = jnp.sum(residual_full * residual_full, axis=1, keepdims=True)
    curvature = jnp.sum(state_ref[:outs] * image, axis=1, keepdims=True)
    step_length = norm_old / curvature
    next_full = residual_full - step_length * image
    norm_new = jnp.sum(next_full * next_full, axis=1, keepdims=True)
    direction = direction_ref[...]
    new_solution_ref[...] = solution_ref[...] + step_length * direction
    first = lax.axis_index("samp") * cen_dev
    turn = lax.rem(image.shape[1] - first, image.shape[1])
    own_image = pltpu.roll(image, turn, 1)[:, :cen_dev]
    new_residual = residual_ref[...] - step_length * own_image
    new_residual_ref[...] = new_residual
    new_direction_ref[...] = new_residual + (norm_new / norm_old) * direction


def body(samples, generator, weight_index, preconditioner, solution, residual, direction):
    devices = lax.axis_size("samp")
    index = lax.axis_index("samp")
    cen_dev, centres_all = preconditioner.shape
    samples_dev = samples.shape[1]
    outs = direction.shape[0]
    held, others = plan(devices, 4 * cen_dev * centres_all)

    weights_dim = 0.5 * jnp.power(0.75, weight_index.astype(F32))
    curve = 2.0 * math.pi * math.pi * weights_dim
    floor = 1.0 - curve / 12.0
    root = jnp.sqrt(curve)
    shift = 0.5 * root

    scale, centre_scaled = pl.pallas_call(
        functools.partial(prepare, (*held, *others), cen_dev),
        in_specs=[SMEM, SMEM],
        out_shape=[
            jax.ShapeDtypeStruct((generator.shape[0], 1), F32),
            jax.ShapeDtypeStruct((generator.shape[0], centres_all), F32),
        ],
        name="prepare",
    )(generator, root)
    constants = (centre_scaled, shift, floor, scale)

    half = samples_dev // 2
    use_store = 4 * half * centres_all <= STORE_BYTES
    store, filled = None, 0

    def fill(rows, passed):
        nonlocal store, filled
        rows = min(rows, half - filled) if use_store else 0
        if rows == 0:
            return passed
        store, handed = kernel_rows(store, passed, samples, filled, rows, half, constants)
        filled += rows
        return handed

    pieces = [preconditioner]
    early = [swap(preconditioner, bit, devices) for bit in held[:2]]
    pieces += early[:1]
    if len(early) > 1:
        pieces += [early[1], swap(early[0], held[1], devices)]
    bit = 1
    state = None
    while bit < devices:
        upper = (index & bit) != 0
        if state is None:
            mine = [direction, residual]
            other = [swap(direction, bit, devices), swap(residual, bit, devices)]
            joined = [jnp.concatenate(pair, axis=1) for pair in zip(other, mine)]
            turned = [jnp.concatenate(pair, axis=1) for pair in zip(mine, other)]
            state = jnp.where(upper, jnp.concatenate(joined), jnp.concatenate(turned))
        else:
            other = swap(state, bit, devices)
            mine = fill(256 if 2 * bit == devices else 128, state)
            state = jnp.where(
                upper,
                jnp.concatenate([other, mine], axis=1),
                jnp.concatenate([mine, other], axis=1),
            )
        bit *= 2

    def coefficients_of(group):
        rows = len(group) * cen_dev
        return pl.pallas_call(
            functools.partial(row_products, outs, len(group)),
            out_shape=[
                jax.ShapeDtypeStruct((outs, rows), F32),
                jax.ShapeDtypeStruct((3, rows, centres_all), BF16),
            ],
            compiler_params=pltpu.CompilerParams(
                vmem_limit_bytes=(4 << 20) + 24 * rows * centres_all
            ),
            name="row_products",
        )(state, *group)

    groups = [pieces]
    for bit in held[2:]:
        groups.append([swap(p, bit, devices) for p in sum(groups, [])])
    made = [coefficients_of(group) for group in groups]
    coefficients = jnp.concatenate([m[0] for m in made], axis=1)
    parts = [m[1] for m in made]
    for bit in others:
        other = swap(coefficients, bit, devices)
        mine = fill(512, coefficients)
        coefficients = jnp.concatenate([mine, other], axis=1)
    coefficients = fill(half, coefficients)

    kept, sent, kernel_products = apply_products(
        store, samples, coefficients, cen_dev, 256, constants
    )
    for bit in reversed(others):
        came = swap(sent, bit, devices)
        if bit != others[0]:
            summed = kept + came
            width = summed.shape[1] // 2
            kept, sent = summed[:, :width], summed[:, width:]
    scale_total = float(samples_dev * devices) * float(centres_all)
    image = pl.pallas_call(
        functools.partial(image_rows, scale_total, ridge_weight / centres_all),
        out_shape=jax.ShapeDtypeStruct((outs, centres_all), F32),
        compiler_params=pltpu.CompilerParams(
            vmem_limit_bytes=(4 << 20) + 8 * kept.shape[1] * centres_all
        ),
        name="image_rows",
    )(kept, came, kernel_products, *parts)
    bit = 1
    while 2 * bit < devices:
        image = image + swap(image, bit, devices)
        bit *= 2
    more = swap(image, bit, devices)
    own = jax.ShapeDtypeStruct(solution.shape, F32)
    return pl.pallas_call(
        finish,
        out_shape=[own, own, own],
        name="finish",
    )(image, more, state, solution, residual, direction)


def solution(mesh):
    placed = (
        P("groups", "samp"),
        P(),
        P(),
        P("samp", None),
        P("groups", "samp"),
        P("groups", "samp"),
        P("groups", "samp"),
    )
    return jax.shard_map(
        body,
        mesh=mesh,
        in_specs=placed,
        out_specs=(P("groups", "samp"), P("groups", "samp"), P("groups", "samp")),
        check_vma=False,
    )
```

```python
import functools
import math

import jax
import jax.numpy as jnp
from jax import lax
from jax.experimental import pallas as pl
from jax.experimental.pallas import tpu as pltpu
from jax.sharding import PartitionSpec as P

LATTICE = 65521

ridge_weight = 0.25
STORE_BYTES = 12 << 20
HELD_BYTES = 16 << 20
VMEM = pl.BlockSpec(memory_space=pltpu.VMEM)
FREE = pl.BlockSpec(memory_space=pl.ANY)
SMEM = pl.BlockSpec(memory_space=pltpu.SMEM)
F32 = jnp.float32
BF16 = jnp.bfloat16


def swap(value, bit, devices):
    return lax.ppermute(value, "samp", [(i, i ^ bit) for i in range(devices)])


def plan(devices, piece_bytes):
    bits = [1 << k for k in range(devices.bit_length() - 1)]
    held = []
    for bit in [b for b in (devices // 4, *bits) if 0 < b < devices // 2]:
        if bit not in held and (2 << len(held)) * piece_bytes <= HELD_BYTES:
            held.append(bit)
    held = held[:1] + held[:0:-1] if len(held) > 1 else held
    return held, [b for b in bits if b not in held]


def split3(value):
    high = value.astype(BF16)
    rest = value - high.astype(F32)
    middle = rest.astype(BF16)
    low = (rest - middle.astype(F32)).astype(BF16)
    return high, middle, low


def stack3(value):
    return jnp.concatenate(split3(value), axis=0)


def add_parts(value, outs):
    return value[:outs] + (value[outs : 2 * outs] + value[2 * outs :])


def kernel_tile(points, centre_ref, shift_ref, floor_ref, first, width):
    rows, dims = points.shape
    product = None
    for axis_number in range(dims):
        centre = centre_ref[axis_number : axis_number + 1, pl.ds(first, width)]
        point = jnp.broadcast_to(points[:, axis_number : axis_number + 1], (rows, width))
        arm = jnp.abs(point - centre) - shift_ref[axis_number]
        factor = arm * arm + floor_ref[axis_number]
        product = factor if product is None else product * factor
    return product


def fill_kernel(rows, points, centre_ref, shift_ref, floor_ref, high_ref, low_ref):
    centres_all = centre_ref.shape[1]
    width = min(512, centres_all)
    span = min(1024, centres_all)

    def part(base):
        for piece in range(span // width):
            first = base + piece * width
            if not isinstance(first, int):
                first = pl.multiple_of(first, width)
            tile = kernel_tile(points, centre_ref, shift_ref, floor_ref, first, width)
            high = tile.astype(BF16)
            high_ref[rows, pl.ds(first, width)] = high
            low_ref[rows, pl.ds(first, width)] = (tile - high.astype(F32)).astype(BF16)

    if centres_all == span:
        part(0)
    else:
        lax.fori_loop(0, centres_all // span, lambda i, _: part(i * span), None)


def fetch(pairs, sems):
    copies = [pltpu.make_async_copy(src, dst, sems.at[i]) for i, (src, dst) in enumerate(pairs)]
    for copy in copies:
        copy.start()
    return copies


def scale_column(shift_ref, dims):
    row = lax.broadcasted_iota(jnp.int32, (dims, 1), 0)
    scale = jnp.zeros((dims, 1), F32)
    for axis_number in range(dims):
        scale = jnp.where(row == axis_number, shift_ref[axis_number], scale)
    return scale * (2.0 / LATTICE)


def store_rows(
    first_row, step_rows, shift_ref, floor_ref, samples_hbm, centres_hbm, passed_ref,
    high_hbm, low_hbm, handed_ref, sample_ref, centre_ref, high_ref, low_ref, in_sems, out_sems,
):
    rows_all = high_hbm.shape[0]
    copies = fetch(
        [(samples_hbm.at[:, pl.ds(first_row, rows_all)], sample_ref), (centres_hbm, centre_ref)],
        in_sems,
    )
    handed_ref[...] = passed_ref[...]
    scale = scale_column(shift_ref, sample_ref.shape[0])
    for copy in copies:
        copy.wait()

    def sends(step):
        slot = lax.rem(step, 2)
        rows = pl.ds(pl.multiple_of(step * step_rows, step_rows), step_rows)
        return [
            pltpu.make_async_copy(high_ref.at[slot], high_hbm.at[rows], out_sems.at[slot, 0]),
            pltpu.make_async_copy(low_ref.at[slot], low_hbm.at[rows], out_sems.at[slot, 1]),
        ]

    steps = rows_all // step_rows

    def step(i, _):
        slot = lax.rem(i, 2)

        @pl.when(i >= 2)
        def _():
            for copy in sends(i - 2):
                copy.wait()

        columns = pl.ds(pl.multiple_of(i * step_rows, step_rows), step_rows)
        points = (sample_ref[:, columns].astype(F32) * scale).T
        rows = pl.ds(0, step_rows)
        fill_kernel(
            rows, points, centre_ref, shift_ref, floor_ref, high_ref.at[slot], low_ref.at[slot]
        )
        for copy in sends(i):
            copy.start()

    lax.fori_loop(0, steps, step, None)
    for last in range(max(0, steps - 2), steps):
        for copy in sends(last):
            copy.wait()


def kernel_rows(passed, samples, first_row, rows, constants):
    centre_scaled, shift, floor = constants
    dims, centres_all = centre_scaled.shape
    kept = jax.ShapeDtypeStruct((rows, centres_all), BF16)
    step_rows = min(128, rows)
    high, low, handed = pl.pallas_call(
        functools.partial(store_rows, first_row, step_rows),
        in_specs=[SMEM, SMEM, FREE, FREE, VMEM],
        out_specs=[FREE, FREE, VMEM],
        out_shape=[kept, kept, jax.ShapeDtypeStruct(passed.shape, passed.dtype)],
        scratch_shapes=[
            pltpu.VMEM((dims, rows), jnp.int32),
            pltpu.VMEM((dims, centres_all), F32),
            pltpu.VMEM((2, step_rows, centres_all), BF16),
            pltpu.VMEM((2, step_rows, centres_all), BF16),
            pltpu.SemaphoreType.DMA((2,)),
            pltpu.SemaphoreType.DMA((2, 2)),
        ],
        compiler_params=pltpu.CompilerParams(vmem_limit_bytes=12 << 20),
        cost_estimate=pl.CostEstimate(
            flops=6 * dims * rows * centres_all,
            bytes_accessed=4 * rows * centres_all,
            transcendentals=0,
        ),
        name="kernel_rows",
    )(shift, floor, samples, centre_scaled, passed)
    return (high, low), handed


def apply_kernel(high, low, coefficients, outs):
    contract = (((1,), (1,)), ((), ()))
    fitted = lax.dot_general(coefficients, high, contract, preferred_element_type=F32)
    fitted = fitted + lax.dot_general(coefficients, low, contract, preferred_element_type=F32)
    return add_parts(fitted, outs)


def back_products(high, low, coefficients, outs):
    parts = stack3(apply_kernel(high, low, coefficients, outs))
    return jnp.dot(parts, high, preferred_element_type=F32) + jnp.dot(
        parts, low, preferred_element_type=F32
    )


def products(
    outs, block_rows, stored, shift_ref, floor_ref, coef_ref, samples_hbm, centres_hbm, *refs
):
    stored_hbm, refs = refs[: 2 * len(stored)], refs[2 * len(stored) :]
    *backward_refs, own_out_ref = refs[:3]
    parts_ref, sum_ref, made_high, made_low, sample_ref, centre_ref, high_ref, low_ref, sems = refs[3:]
    own_rows = own_out_ref.shape[1]
    steps = sample_ref.shape[1] // block_rows
    stored_rows = sum(stored)
    share = stored_rows // steps
    columns = pl.ds(stored_rows, sample_ref.shape[1])
    copies = fetch([(samples_hbm.at[:, columns], sample_ref), (centres_hbm, centre_ref)], sems)
    first = 0
    for i, rows in enumerate(stored):
        pairs = zip(stored_hbm[2 * i : 2 * i + 2], (high_ref, low_ref))
        place = pl.ds(first, rows)
        copies += fetch([(src, dst.at[place]) for src, dst in pairs], sems.at[pl.ds(2 + 2 * i, 2)])
        first += rows

    scale = scale_column(shift_ref, sample_ref.shape[0])
    parts_ref[...] = stack3(coef_ref[...])
    sum_ref[...] = jnp.zeros_like(sum_ref)
    made_high[1] = jnp.zeros(made_high.shape[1:], BF16)
    made_low[1] = jnp.zeros(made_low.shape[1:], BF16)
    copies[0].wait()
    copies[1].wait()
    own_high, own_low = made_high.at[0], made_low.at[0]
    rows = pl.ds(0, own_rows)
    own_points = centre_ref[:, :own_rows]
    fill_kernel(rows, own_points.T, centre_ref, shift_ref, floor_ref, own_high, own_low)
    own_out_ref[...] = apply_kernel(own_high[rows], own_low[rows], parts_ref[...], outs)
    for copy in copies[2:]:
        copy.wait()

    def step(i, _):
        now = lax.rem(i, 2)
        before = 1 - now
        coefficients = parts_ref[...]
        total = back_products(made_high[before], made_low[before], coefficients, outs)
        if share:
            rows = pl.ds(pl.multiple_of(i * share, share), share)
            total = total + back_products(high_ref[rows], low_ref[rows], coefficients, outs)
        columns = pl.ds(pl.multiple_of(i * block_rows, block_rows), block_rows)
        points = (sample_ref[:, columns].astype(F32) * scale).T
        for first in range(0, block_rows, 128):
            rows = pl.ds(first, 128)
            fill_kernel(
                rows, points[first : first + 128], centre_ref, shift_ref, floor_ref,
                made_high.at[now], made_low.at[now],
            )
        sum_ref[...] += total

    lax.fori_loop(0, steps, step, None)
    now = (steps - 1) % 2
    last = sum_ref[...] + back_products(made_high[now], made_low[now], parts_ref[...], outs)
    last = add_parts(last, outs)
    width = last.shape[1] // len(backward_refs)
    for i, backward_ref in enumerate(backward_refs):
        backward_ref[...] = last[:, i * width : (i + 1) * width]


def apply_products(store, samples, coefficients, own_rows, block_rows, constants):
    centre_scaled, shift, floor = constants
    outs, centres_all = coefficients.shape
    dims = centre_scaled.shape[0]
    stored = tuple(high.shape[0] for high, _ in store)
    made = pltpu.VMEM((2, block_rows, centres_all), BF16)
    kept = pltpu.VMEM((max(16, sum(stored)), centres_all), BF16)
    rows = samples.shape[1] - sum(stored)
    return pl.pallas_call(
        functools.partial(products, outs, block_rows, stored),
        in_specs=[SMEM, SMEM, VMEM, *[FREE] * (2 + 2 * len(stored))],
        out_specs=[VMEM, VMEM, VMEM],
        out_shape=[
            jax.ShapeDtypeStruct((outs, centres_all // 2), F32),
            jax.ShapeDtypeStruct((outs, centres_all // 2), F32),
            jax.ShapeDtypeStruct((outs, own_rows), F32),
        ],
        scratch_shapes=[
            pltpu.VMEM((3 * outs, centres_all), BF16),
            pltpu.VMEM((3 * outs, centres_all), F32),
            made,
            made,
            pltpu.VMEM((dims, rows), jnp.int32),
            pltpu.VMEM((dims, centres_all), F32),
            kept,
            kept,
            pltpu.SemaphoreType.DMA((2 + 2 * len(stored),)),
        ],
        compiler_params=pltpu.CompilerParams(
            vmem_limit_bytes=(14 << 20) + (16 * block_rows + 4 * sum(stored)) * centres_all
        ),
        cost_estimate=pl.CostEstimate(
            flops=6 * dims * rows * centres_all,
            bytes_accessed=4 * sum(stored) * centres_all,
            transcendentals=0,
        ),
        name="products",
    )(shift, floor, coefficients, samples, centre_scaled, *[part for pair in store for part in pair])


def modulo(value):
    turns = (value.astype(F32) * (1.0 / LATTICE)).astype(jnp.int32)
    rest = value - turns * LATTICE
    rest = jnp.where(rest < 0, rest + LATTICE, rest)
    return jnp.where(rest >= LATTICE, rest - LATTICE, rest)


def prepare(order_bits, cen_dev, generator_ref, shift_ref, centre_ref):
    dims, centres_all = centre_ref.shape
    row = lax.broadcasted_iota(jnp.int32, (dims, 1), 0)
    generator = jnp.zeros((dims, 1), jnp.int32)
    for axis_number in range(dims):
        generator = jnp.where(row == axis_number, generator_ref[axis_number], generator)
    place = lax.broadcasted_iota(jnp.int32, (1, centres_all), 1)
    owner = jnp.zeros_like(place) + lax.axis_index("samp")
    for k, bit in enumerate(order_bits):
        block_bit = cen_dev << k
        owner = jnp.where((place & block_bit) != 0, owner ^ bit, owner)
    column = owner * cen_dev + (place & (cen_dev - 1))
    upper = modulo(column * (generator >> 8))
    centre = modulo(upper * 256 + column * (generator & 255))
    centre_ref[...] = centre.astype(F32) * scale_column(shift_ref, dims)


def row_products(outs, count, state_ref, *refs):
    coef_ref, parts_ref = refs[count:]
    state = stack3(state_ref[:outs])
    cen_dev = refs[0].shape[0]
    for i, piece_ref in enumerate(refs[:count]):
        rows = slice(i * cen_dev, (i + 1) * cen_dev)
        for k, part in enumerate(split3(piece_ref[...])):
            parts_ref[k, rows] = part
    total = None
    for k in range(3):
        term = lax.dot_general(
            state, parts_ref[k], (((1,), (1,)), ((), ())), preferred_element_type=F32
        )
        total = term if total is None else total + term
    coef_ref[...] = add_parts(total, outs)


def image_rows(scale_total, ridge, kept_ref, came_ref, own_ref, *refs):
    *part_refs, image_ref = refs
    outs, cen_dev = own_ref.shape
    applied = (kept_ref[...] + came_ref[...]) * (1.0 / scale_total)
    own = ridge * own_ref[...]
    rest = applied.shape[1] - cen_dev
    if rest:
        own = jnp.concatenate([own, jnp.zeros((outs, rest), F32)], axis=1)
    rows = stack3(applied + own)
    total, first = None, 0
    for part_ref in part_refs:
        some = rows[:, first : first + part_ref.shape[1]]
        first += part_ref.shape[1]
        for k in range(3):
            term = jnp.dot(some, part_ref[k], preferred_element_type=F32)
            total = term if total is None else total + term
    image_ref[...] = add_parts(total, outs)


def finish(
    image_ref, more_ref, state_ref, solution_ref, residual_ref, direction_ref,
    new_solution_ref, new_residual_ref, new_direction_ref,
):
    outs, cen_dev = solution_ref.shape
    image = image_ref[...] + more_ref[...]
    residual_full = state_ref[outs:]
    norm_old = jnp.sum(residual_full * residual_full, axis=1, keepdims=True)
    curvature = jnp.sum(state_ref[:outs] * image, axis=1, keepdims=True)
    step_length = norm_old / curvature
    next_full = residual_full - step_length * image
    norm_new = jnp.sum(next_full * next_full, axis=1, keepdims=True)
    direction = direction_ref[...]
    new_solution_ref[...] = solution_ref[...] + step_length * direction
    first = lax.axis_index("samp") * cen_dev
    turn = lax.rem(image.shape[1] - first, image.shape[1])
    own_image = pltpu.roll(image, turn, 1)[:, :cen_dev]
    new_residual = residual_ref[...] - step_length * own_image
    new_residual_ref[...] = new_residual
    new_direction_ref[...] = new_residual + (norm_new / norm_old) * direction


def body(samples, generator, weight_index, preconditioner, solution, residual, direction):
    devices = lax.axis_size("samp")
    index = lax.axis_index("samp")
    cen_dev, centres_all = preconditioner.shape
    samples_dev = samples.shape[1]
    outs = direction.shape[0]
    held, others = plan(devices, 4 * cen_dev * centres_all)

    weights_dim = 0.5 * jnp.power(0.75, weight_index.astype(F32))
    curve = 2.0 * math.pi * math.pi * weights_dim
    floor = 1.0 - curve / 12.0
    shift = 0.5 * jnp.sqrt(curve)

    centre_scaled = pl.pallas_call(
        functools.partial(prepare, (*held, *others), cen_dev),
        in_specs=[SMEM, SMEM],
        out_shape=jax.ShapeDtypeStruct((generator.shape[0], centres_all), F32),
        name="prepare",
    )(generator, shift)
    constants = (centre_scaled, shift, floor)

    half = samples_dev // 2
    use_store = 4 * half * centres_all <= STORE_BYTES
    store, filled = [], 0

    def fill(rows, passed):
        nonlocal filled
        rows = min(rows, half - filled) if use_store else 0
        if rows == 0:
            return passed
        made, handed = kernel_rows(passed, samples, filled, rows, constants)
        store.append(made)
        filled += rows
        return handed

    pieces = [preconditioner]
    early = [swap(preconditioner, bit, devices) for bit in held[:2]]
    pieces += early[:1]
    if len(early) > 1:
        pieces += [early[1], swap(early[0], held[1], devices)]
    bit = 1
    state = None
    while bit < devices:
        upper = (index & bit) != 0
        if state is None:
            mine = [direction, residual]
            other = [swap(direction, bit, devices), swap(residual, bit, devices)]
            joined = [jnp.concatenate(pair, axis=1) for pair in zip(other, mine)]
            turned = [jnp.concatenate(pair, axis=1) for pair in zip(mine, other)]
            state = jnp.where(upper, jnp.concatenate(joined), jnp.concatenate(turned))
        else:
            other = swap(state, bit, devices)
            mine = fill(256 if 2 * bit == devices else 128, state)
            state = jnp.where(
                upper,
                jnp.concatenate([other, mine], axis=1),
                jnp.concatenate([mine, other], axis=1),
            )
        bit *= 2

    def coefficients_of(group):
        rows = len(group) * cen_dev
        return pl.pallas_call(
            functools.partial(row_products, outs, len(group)),
            out_shape=[
                jax.ShapeDtypeStruct((outs, rows), F32),
                jax.ShapeDtypeStruct((3, rows, centres_all), BF16),
            ],
            compiler_params=pltpu.CompilerParams(
                vmem_limit_bytes=(4 << 20) + 24 * rows * centres_all
            ),
            name="row_products",
        )(state, *group)

    groups = [pieces]
    for bit in held[2:]:
        groups.append([swap(p, bit, devices) for p in sum(groups, [])])
    made = [coefficients_of(group) for group in groups]
    coefficients = jnp.concatenate([m[0] for m in made], axis=1)
    parts = [m[1] for m in made]
    for bit in others:
        other = swap(coefficients, bit, devices)
        mine = fill(512, coefficients)
        coefficients = jnp.concatenate([mine, other], axis=1)
    coefficients = fill(half, coefficients)

    kept, sent, kernel_products = apply_products(
        store, samples, coefficients, cen_dev, 256, constants
    )
    for bit in reversed(others):
        came = swap(sent, bit, devices)
        if bit != others[0]:
            summed = kept + came
            width = summed.shape[1] // 2
            kept, sent = summed[:, :width], summed[:, width:]
    scale_total = float(samples_dev * devices) * float(centres_all)
    image = pl.pallas_call(
        functools.partial(image_rows, scale_total, ridge_weight / centres_all),
        out_shape=jax.ShapeDtypeStruct((outs, centres_all), F32),
        compiler_params=pltpu.CompilerParams(
            vmem_limit_bytes=(4 << 20) + 8 * kept.shape[1] * centres_all
        ),
        name="image_rows",
    )(kept, came, kernel_products, *parts)
    bit = 1
    while 2 * bit < devices:
        image = image + swap(image, bit, devices)
        bit *= 2
    more = swap(image, bit, devices)
    own = jax.ShapeDtypeStruct(solution.shape, F32)
    return pl.pallas_call(
        finish,
        out_shape=[own, own, own],
        name="finish",
    )(image, more, state, solution, residual, direction)


def solution(mesh):
    placed = (
        P("groups", "samp"),
        P(),
        P(),
        P("samp", None),
        P("groups", "samp"),
        P("groups", "samp"),
        P("groups", "samp"),
    )
    return jax.shard_map(
        body,
        mesh=mesh,
        in_specs=placed,
        out_specs=(P("groups", "samp"), P("groups", "samp"), P("groups", "samp")),
        check_vma=False,
    )
```

```python
import functools
import math

import jax
import jax.numpy as jnp
from jax import lax
from jax.experimental import pallas as pl
from jax.experimental.pallas import tpu as pltpu
from jax.sharding import PartitionSpec as P

LATTICE = 65521

ridge_weight = 0.25
STORE_BYTES = 12 << 20
HELD_BYTES = 16 << 20
VMEM = pl.BlockSpec(memory_space=pltpu.VMEM)
FREE = pl.BlockSpec(memory_space=pl.ANY)
HBM = pl.BlockSpec(memory_space=pltpu.HBM)
SMEM = pl.BlockSpec(memory_space=pltpu.SMEM)
F32 = jnp.float32
BF16 = jnp.bfloat16


def swap(value, bit, devices):
    return lax.ppermute(value, "samp", [(i, i ^ bit) for i in range(devices)])


def plan(devices, piece_bytes):
    bits = [1 << k for k in range(devices.bit_length() - 1)]
    held = []
    for bit in [b for b in (devices // 4, *bits) if 0 < b < devices // 2]:
        if bit not in held and (2 << len(held)) * piece_bytes <= HELD_BYTES:
            held.append(bit)
    held = held[:1] + held[:0:-1] if len(held) > 1 else held
    return held, [b for b in bits if b not in held]


def split3(value):
    high = value.astype(BF16)
    rest = value - high.astype(F32)
    middle = rest.astype(BF16)
    low = (rest - middle.astype(F32)).astype(BF16)
    return high, middle, low


def stack3(value):
    return jnp.concatenate(split3(value), axis=0)


def add_parts(value, outs):
    return value[:outs] + (value[outs : 2 * outs] + value[2 * outs :])


def kernel_tile(points, centre_ref, shift_ref, floor_ref, first, width):
    rows, dims = points.shape
    product = None
    for axis_number in range(dims):
        centre = centre_ref[axis_number : axis_number + 1, pl.ds(first, width)]
        point = jnp.broadcast_to(points[:, axis_number : axis_number + 1], (rows, width))
        arm = jnp.abs(point - centre) - shift_ref[axis_number]
        factor = arm * arm + floor_ref[axis_number]
        product = factor if product is None else product * factor
    return product


def fill_kernel(rows, points, centre_ref, shift_ref, floor_ref, high_ref, low_ref):
    centres_all = centre_ref.shape[1]
    width = min(512, centres_all)
    span = min(1024, centres_all)

    def part(base):
        for piece in range(span // width):
            first = base + piece * width
            if not isinstance(first, int):
                first = pl.multiple_of(first, width)
            tile = kernel_tile(points, centre_ref, shift_ref, floor_ref, first, width)
            high = tile.astype(BF16)
            high_ref[rows, pl.ds(first, width)] = high
            low_ref[rows, pl.ds(first, width)] = (tile - high.astype(F32)).astype(BF16)

    if centres_all == span:
        part(0)
    else:
        lax.fori_loop(0, centres_all // span, lambda i, _: part(i * span), None)


def fetch(pairs, sems):
    copies = [pltpu.make_async_copy(src, dst, sems.at[i]) for i, (src, dst) in enumerate(pairs)]
    for copy in copies:
        copy.start()
    return copies


def modulo(value):
    turns = (value.astype(F32) * (1.0 / LATTICE)).astype(jnp.int32)
    rest = value - turns * LATTICE
    rest = jnp.where(rest < 0, rest + LATTICE, rest)
    return jnp.where(rest >= LATTICE, rest - LATTICE, rest)


def column_of(values_ref, dims, dtype):
    row = lax.broadcasted_iota(jnp.int32, (dims, 1), 0)
    column = jnp.zeros((dims, 1), dtype)
    for axis_number in range(dims):
        column = jnp.where(row == axis_number, values_ref[axis_number], column)
    return column


def set_up(order_bits, cen_dev, generator_ref, weight_ref, shift_ref, floor_ref, centre_ref):
    dims, centres_all = centre_ref.shape
    curves = [math.pi * math.pi * 0.75**weight for weight in range(8)]
    for axis_number in range(dims):
        weight = weight_ref[axis_number]
        shift, floor = 0.5 * math.sqrt(curves[7]), 1.0 - curves[7] / 12.0
        for k in range(7):
            shift = jnp.where(weight == k, F32(0.5 * math.sqrt(curves[k])), shift)
            floor = jnp.where(weight == k, F32(1.0 - curves[k] / 12.0), floor)
        shift_ref[axis_number] = shift
        floor_ref[axis_number] = floor
    scale = column_of(shift_ref, dims, F32) * (2.0 / LATTICE)
    generator = column_of(generator_ref, dims, jnp.int32)
    place = lax.broadcasted_iota(jnp.int32, (1, centres_all), 1)
    owner = jnp.zeros_like(place) + lax.axis_index("samp")
    for k, bit in enumerate(order_bits):
        owner = jnp.where((place & (cen_dev << k)) != 0, owner ^ bit, owner)
    column = owner * cen_dev + (place & (cen_dev - 1))
    upper = modulo(column * (generator >> 8))
    centre = modulo(upper * 256 + column * (generator & 255))
    centre_ref[...] = centre.astype(F32) * scale
    return scale


def store_rows(
    first_row, step_rows, order, generator_hbm, weight_hbm, samples_hbm, passed_ref,
    high_hbm, low_hbm, handed_ref, generator_ref, weight_ref, shift_ref, floor_ref, sample_ref,
    centre_ref, high_ref, low_ref, in_sems, out_sems,
):
    rows_all = high_hbm.shape[0]
    copies = fetch(
        [
            (generator_hbm, generator_ref),
            (weight_hbm, weight_ref),
            (samples_hbm.at[:, pl.ds(first_row, rows_all)], sample_ref),
        ],
        in_sems,
    )
    handed_ref[...] = passed_ref[...]
    copies[0].wait()
    copies[1].wait()
    scale = set_up(*order, generator_ref, weight_ref, shift_ref, floor_ref, centre_ref)
    copies[2].wait()

    def sends(step):
        slot = lax.rem(step, 2)
        rows = pl.ds(pl.multiple_of(step * step_rows, step_rows), step_rows)
        return [
            pltpu.make_async_copy(high_ref.at[slot], high_hbm.at[rows], out_sems.at[slot, 0]),
            pltpu.make_async_copy(low_ref.at[slot], low_hbm.at[rows], out_sems.at[slot, 1]),
        ]

    steps = rows_all // step_rows

    def step(i, _):
        slot = lax.rem(i, 2)

        @pl.when(i >= 2)
        def _():
            for copy in sends(i - 2):
                copy.wait()

        columns = pl.ds(pl.multiple_of(i * step_rows, step_rows), step_rows)
        points = (sample_ref[:, columns].astype(F32) * scale).T
        rows = pl.ds(0, step_rows)
        fill_kernel(
            rows, points, centre_ref, shift_ref, floor_ref, high_ref.at[slot], low_ref.at[slot]
        )
        for copy in sends(i):
            copy.start()

    lax.fori_loop(0, steps, step, None)
    for last in range(max(0, steps - 2), steps):
        for copy in sends(last):
            copy.wait()


def set_up_scratch(dims, rows, centres_all):
    return [
        pltpu.SMEM((dims,), jnp.int32),
        pltpu.SMEM((dims,), jnp.int32),
        pltpu.SMEM((dims,), F32),
        pltpu.SMEM((dims,), F32),
        pltpu.VMEM((dims, rows), jnp.int32),
        pltpu.VMEM((dims, centres_all), F32),
    ]


def kernel_rows(passed, first_row, rows, order, centres_all, lattice):
    dims = lattice[2].shape[0]
    kept = jax.ShapeDtypeStruct((rows, centres_all), BF16)
    step_rows = min(128, rows)
    high, low, handed = pl.pallas_call(
        functools.partial(store_rows, first_row, step_rows, order),
        in_specs=[HBM, HBM, HBM, VMEM],
        out_specs=[FREE, FREE, VMEM],
        out_shape=[kept, kept, jax.ShapeDtypeStruct(passed.shape, passed.dtype)],
        scratch_shapes=[
            *set_up_scratch(dims, rows, centres_all),
            pltpu.VMEM((2, step_rows, centres_all), BF16),
            pltpu.VMEM((2, step_rows, centres_all), BF16),
            pltpu.SemaphoreType.DMA((3,)),
            pltpu.SemaphoreType.DMA((2, 2)),
        ],
        compiler_params=pltpu.CompilerParams(vmem_limit_bytes=12 << 20),
        cost_estimate=pl.CostEstimate(
            flops=6 * dims * rows * centres_all,
            bytes_accessed=4 * rows * centres_all,
            transcendentals=0,
        ),
        name="kernel_rows",
    )(*lattice, passed)
    return (high, low), handed


def apply_kernel(high, low, coefficients, outs):
    contract = (((1,), (1,)), ((), ()))
    fitted = lax.dot_general(coefficients, high, contract, preferred_element_type=F32)
    fitted = fitted + lax.dot_general(coefficients, low, contract, preferred_element_type=F32)
    return add_parts(fitted, outs)


def back_products(high, low, coefficients, outs):
    parts = stack3(apply_kernel(high, low, coefficients, outs))
    return jnp.dot(parts, high, preferred_element_type=F32) + jnp.dot(
        parts, low, preferred_element_type=F32
    )


def products(
    outs, block_rows, stored, order, coef_ref, generator_hbm, weight_hbm, samples_hbm, *refs
):
    stored_hbm, refs = refs[: 2 * len(stored)], refs[2 * len(stored) :]
    *backward_refs, own_out_ref = refs[:3]
    generator_ref, weight_ref, shift_ref, floor_ref, sample_ref, centre_ref = refs[3:9]
    parts_ref, sum_ref, made_high, made_low, high_ref, low_ref, sems = refs[9:]
    own_rows = own_out_ref.shape[1]
    steps = sample_ref.shape[1] // block_rows
    stored_rows = sum(stored)
    share = stored_rows // steps
    columns = pl.ds(stored_rows, sample_ref.shape[1])
    copies = fetch(
        [
            (generator_hbm, generator_ref),
            (weight_hbm, weight_ref),
            (samples_hbm.at[:, columns], sample_ref),
        ],
        sems,
    )
    first = 0
    for i, rows in enumerate(stored):
        pairs = zip(stored_hbm[2 * i : 2 * i + 2], (high_ref, low_ref))
        place = pl.ds(first, rows)
        copies += fetch([(src, dst.at[place]) for src, dst in pairs], sems.at[pl.ds(3 + 2 * i, 2)])
        first += rows

    parts_ref[...] = stack3(coef_ref[...])
    sum_ref[...] = jnp.zeros_like(sum_ref)
    made_high[1] = jnp.zeros(made_high.shape[1:], BF16)
    made_low[1] = jnp.zeros(made_low.shape[1:], BF16)
    copies[0].wait()
    copies[1].wait()
    scale = set_up(*order, generator_ref, weight_ref, shift_ref, floor_ref, centre_ref)
    own_high, own_low = made_high.at[0], made_low.at[0]
    rows = pl.ds(0, own_rows)
    own_points = centre_ref[:, :own_rows]
    fill_kernel(rows, own_points.T, centre_ref, shift_ref, floor_ref, own_high, own_low)
    own_out_ref[...] = apply_kernel(own_high[rows], own_low[rows], parts_ref[...], outs)
    for copy in copies[2:]:
        copy.wait()

    def step(i, _):
        now = lax.rem(i, 2)
        before = 1 - now
        coefficients = parts_ref[...]
        total = back_products(made_high[before], made_low[before], coefficients, outs)
        if share:
            rows = pl.ds(pl.multiple_of(i * share, share), share)
            total = total + back_products(high_ref[rows], low_ref[rows], coefficients, outs)
        columns = pl.ds(pl.multiple_of(i * block_rows, block_rows), block_rows)
        points = (sample_ref[:, columns].astype(F32) * scale).T
        for first in range(0, block_rows, 128):
            rows = pl.ds(first, 128)
            fill_kernel(
                rows, points[first : first + 128], centre_ref, shift_ref, floor_ref,
                made_high.at[now], made_low.at[now],
            )
        sum_ref[...] += total

    lax.fori_loop(0, steps, step, None)
    now = (steps - 1) % 2
    last = sum_ref[...] + back_products(made_high[now], made_low[now], parts_ref[...], outs)
    last = add_parts(last, outs)
    width = last.shape[1] // len(backward_refs)
    for i, backward_ref in enumerate(backward_refs):
        backward_ref[...] = last[:, i * width : (i + 1) * width]


def apply_products(store, coefficients, own_rows, block_rows, order, lattice):
    outs, centres_all = coefficients.shape
    dims, samples_dev = lattice[2].shape
    stored = tuple(high.shape[0] for high, _ in store)
    made = pltpu.VMEM((2, block_rows, centres_all), BF16)
    kept = pltpu.VMEM((max(16, sum(stored)), centres_all), BF16)
    rows = samples_dev - sum(stored)
    return pl.pallas_call(
        functools.partial(products, outs, block_rows, stored, order),
        in_specs=[VMEM, HBM, HBM, HBM, *[FREE] * (2 * len(stored))],
        out_specs=[VMEM, VMEM, VMEM],
        out_shape=[
            jax.ShapeDtypeStruct((outs, centres_all // 2), F32),
            jax.ShapeDtypeStruct((outs, centres_all // 2), F32),
            jax.ShapeDtypeStruct((outs, own_rows), F32),
        ],
        scratch_shapes=[
            *set_up_scratch(dims, rows, centres_all),
            pltpu.VMEM((3 * outs, centres_all), BF16),
            pltpu.VMEM((3 * outs, centres_all), F32),
            made,
            made,
            kept,
            kept,
            pltpu.SemaphoreType.DMA((3 + 2 * len(stored),)),
        ],
        compiler_params=pltpu.CompilerParams(
            vmem_limit_bytes=(14 << 20) + (16 * block_rows + 4 * sum(stored)) * centres_all
        ),
        cost_estimate=pl.CostEstimate(
            flops=6 * dims * rows * centres_all,
            bytes_accessed=4 * sum(stored) * centres_all,
            transcendentals=0,
        ),
        name="products",
    )(coefficients, *lattice, *[part for pair in store for part in pair])


def row_products(outs, count, state_ref, *refs):
    coef_ref, parts_ref, fetched_ref, sems = refs[count:]
    copy = pltpu.make_async_copy(refs[0], fetched_ref, sems.at[0])
    copy.start()
    state = stack3(state_ref[:outs])
    cen_dev = refs[0].shape[0]
    piece_refs = [*enumerate(refs[1:count], 1), (0, fetched_ref)]
    for i, piece_ref in piece_refs:
        if i == 0:
            copy.wait()
        rows = slice(i * cen_dev, (i + 1) * cen_dev)
        for k, part in enumerate(split3(piece_ref[...])):
            parts_ref[k, rows] = part
    total = None
    for k in range(3):
        term = lax.dot_general(
            state, parts_ref[k], (((1,), (1,)), ((), ())), preferred_element_type=F32
        )
        total = term if total is None else total + term
    coef_ref[...] = add_parts(total, outs)


def image_rows(scale_total, ridge, kept_ref, came_ref, own_ref, *refs):
    *part_refs, image_ref = refs
    outs, cen_dev = own_ref.shape
    applied = (kept_ref[...] + came_ref[...]) * (1.0 / scale_total)
    own = ridge * own_ref[...]
    rest = applied.shape[1] - cen_dev
    if rest:
        own = jnp.concatenate([own, jnp.zeros((outs, rest), F32)], axis=1)
    rows = stack3(applied + own)
    total, first = None, 0
    for part_ref in part_refs:
        some = rows[:, first : first + part_ref.shape[1]]
        first += part_ref.shape[1]
        for k in range(3):
            term = jnp.dot(some, part_ref[k], preferred_element_type=F32)
            total = term if total is None else total + term
    image_ref[...] = add_parts(total, outs)


def finish(
    image_ref, more_ref, state_ref, solution_hbm, residual_hbm, direction_hbm,
    new_solution_ref, new_residual_ref, new_direction_ref,
    total_ref, solution_ref, residual_ref, direction_ref, sems,
):
    outs, cen_dev = solution_ref.shape
    copies = fetch(
        [
            (solution_hbm, solution_ref),
            (residual_hbm, residual_ref),
            (direction_hbm, direction_ref),
        ],
        sems,
    )
    image = image_ref[...] + more_ref[...]
    total_ref[...] = image
    residual_full = state_ref[outs:]
    norm_old = jnp.sum(residual_full * residual_full, axis=1, keepdims=True)
    curvature = jnp.sum(state_ref[:outs] * image, axis=1, keepdims=True)
    step_length = norm_old / curvature
    next_full = residual_full - step_length * image
    norm_new = jnp.sum(next_full * next_full, axis=1, keepdims=True)
    index = lax.axis_index("samp")
    share = 128 // cen_dev
    first = pl.multiple_of((index // share) * 128, 128)
    wide = total_ref[:, pl.ds(first, 128)]
    own_image = wide[:, :cen_dev]
    for k in range(1, share):
        here = lax.rem(index, share) == k
        own_image = jnp.where(here, wide[:, k * cen_dev : (k + 1) * cen_dev], own_image)
    for copy in copies:
        copy.wait()
    direction = direction_ref[...]
    new_solution_ref[...] = solution_ref[...] + step_length * direction
    new_residual = residual_ref[...] - step_length * own_image
    new_residual_ref[...] = new_residual
    new_direction_ref[...] = new_residual + (norm_new / norm_old) * direction


def body(samples, generator, weight_index, preconditioner, solution, residual, direction):
    devices = lax.axis_size("samp")
    index = lax.axis_index("samp")
    cen_dev, centres_all = preconditioner.shape
    samples_dev = samples.shape[1]
    outs = direction.shape[0]
    held, others = plan(devices, 4 * cen_dev * centres_all)

    order = ((*held, *others), cen_dev)
    lattice = (generator, weight_index, samples)

    half = samples_dev // 2
    use_store = 4 * half * centres_all <= STORE_BYTES
    store, filled = [], 0

    def fill(rows, passed):
        nonlocal filled
        rows = min(rows, half - filled) if use_store else 0
        if rows == 0:
            return passed
        made, handed = kernel_rows(passed, filled, rows, order, centres_all, lattice)
        store.append(made)
        filled += rows
        return handed

    pieces = [preconditioner]
    early = [swap(preconditioner, bit, devices) for bit in held[:2]]
    pieces += early[:1]
    if len(early) > 1:
        pieces += [early[1], swap(early[0], held[1], devices)]
    bit = 1
    state = None
    while bit < devices:
        upper = (index & bit) != 0
        if state is None:
            mine = [direction, residual]
            other = [swap(direction, bit, devices), swap(residual, bit, devices)]
            joined = [jnp.concatenate(pair, axis=1) for pair in zip(other, mine)]
            turned = [jnp.concatenate(pair, axis=1) for pair in zip(mine, other)]
            state = jnp.where(upper, jnp.concatenate(joined), jnp.concatenate(turned))
        else:
            other = swap(state, bit, devices)
            mine = fill(256 if 2 * bit == devices else 128, state)
            state = jnp.where(
                upper,
                jnp.concatenate([other, mine], axis=1),
                jnp.concatenate([mine, other], axis=1),
            )
        bit *= 2

    def coefficients_of(group):
        rows = len(group) * cen_dev
        return pl.pallas_call(
            functools.partial(row_products, outs, len(group)),
            out_shape=[
                jax.ShapeDtypeStruct((outs, rows), F32),
                jax.ShapeDtypeStruct((3, rows, centres_all), BF16),
            ],
            in_specs=[VMEM, HBM, *[VMEM] * (len(group) - 1)],
            scratch_shapes=[
                pltpu.VMEM((cen_dev, centres_all), F32),
                pltpu.SemaphoreType.DMA((1,)),
            ],
            compiler_params=pltpu.CompilerParams(
                vmem_limit_bytes=(4 << 20) + 24 * rows * centres_all
            ),
            name="row_products",
        )(state, *group)

    groups = [pieces]
    for bit in held[2:]:
        groups.append([swap(p, bit, devices) for p in sum(groups, [])])
    made = [coefficients_of(group) for group in groups]
    coefficients = jnp.concatenate([m[0] for m in made], axis=1)
    parts = [m[1] for m in made]
    for bit in others:
        other = swap(coefficients, bit, devices)
        mine = fill(512, coefficients)
        coefficients = jnp.concatenate([mine, other], axis=1)
    coefficients = fill(half, coefficients)

    kept, sent, kernel_products = apply_products(
        store, coefficients, cen_dev, 256, order, lattice
    )
    for bit in reversed(others):
        came = swap(sent, bit, devices)
        if bit != others[0]:
            summed = kept + came
            width = summed.shape[1] // 2
            kept, sent = summed[:, :width], summed[:, width:]
    scale_total = float(samples_dev * devices) * float(centres_all)
    image = pl.pallas_call(
        functools.partial(image_rows, scale_total, ridge_weight / centres_all),
        out_shape=jax.ShapeDtypeStruct((outs, centres_all), F32),
        compiler_params=pltpu.CompilerParams(
            vmem_limit_bytes=(4 << 20) + 8 * kept.shape[1] * centres_all
        ),
        name="image_rows",
    )(kept, came, kernel_products, *parts)
    bit = 1
    while 2 * bit < devices:
        image = image + swap(image, bit, devices)
        bit *= 2
    more = swap(image, bit, devices)
    own = jax.ShapeDtypeStruct(solution.shape, F32)
    return pl.pallas_call(
        finish,
        in_specs=[VMEM, VMEM, VMEM, HBM, HBM, HBM],
        out_shape=[own, own, own],
        scratch_shapes=[
            pltpu.VMEM((outs, centres_all), F32),
            *[pltpu.VMEM(solution.shape, F32)] * 3,
            pltpu.SemaphoreType.DMA((3,)),
        ],
        name="finish",
    )(image, more, state, solution, residual, direction)


def solution(mesh):
    placed = (
        P("groups", "samp"),
        P(),
        P(),
        P("samp", None),
        P("groups", "samp"),
        P("groups", "samp"),
        P("groups", "samp"),
    )
    return jax.shard_map(
        body,
        mesh=mesh,
        in_specs=placed,
        out_specs=(P("groups", "samp"), P("groups", "samp"), P("groups", "samp")),
        check_vma=False,
    )
```

```python
import functools
import math

import jax
import jax.numpy as jnp
from jax import lax
from jax.experimental import pallas as pl
from jax.experimental.pallas import tpu as pltpu
from jax.sharding import PartitionSpec as P

LATTICE = 65521

ridge_weight = 0.25
STORE_BYTES = 12 << 20
HELD_BYTES = 16 << 20
VMEM = pl.BlockSpec(memory_space=pltpu.VMEM)
FREE = pl.BlockSpec(memory_space=pl.ANY)
HBM = pl.BlockSpec(memory_space=pltpu.HBM)
SMEM = pl.BlockSpec(memory_space=pltpu.SMEM)
F32 = jnp.float32
BF16 = jnp.bfloat16


def swap(value, bit, devices):
    return lax.ppermute(value, "samp", [(i, i ^ bit) for i in range(devices)])


def plan(devices, piece_bytes):
    bits = [1 << k for k in range(devices.bit_length() - 1)]
    held = []
    for bit in [b for b in (devices // 4, *bits) if 0 < b < devices // 2]:
        if bit not in held and (2 << len(held)) * piece_bytes <= HELD_BYTES:
            held.append(bit)
    held = held[:1] + held[:0:-1] if len(held) > 1 else held
    return held, [b for b in bits if b not in held]


def split3(value):
    high = value.astype(BF16)
    rest = value - high.astype(F32)
    middle = rest.astype(BF16)
    low = (rest - middle.astype(F32)).astype(BF16)
    return high, middle, low


def stack3(value):
    return jnp.concatenate(split3(value), axis=0)


def add_parts(value, outs):
    return value[:outs] + (value[outs : 2 * outs] + value[2 * outs :])


def kernel_tile(points, centre_ref, shift_ref, floor_ref, first, width):
    rows, dims = points.shape
    product = None
    for axis_number in range(dims):
        centre = centre_ref[axis_number : axis_number + 1, pl.ds(first, width)]
        point = jnp.broadcast_to(points[:, axis_number : axis_number + 1], (rows, width))
        arm = jnp.abs(point - centre) - shift_ref[axis_number]
        factor = arm * arm + floor_ref[axis_number]
        product = factor if product is None else product * factor
    return product


def fill_kernel(rows, points, centre_ref, shift_ref, floor_ref, high_ref, low_ref):
    centres_all = centre_ref.shape[1]
    width = min(512, centres_all)
    span = min(1024, centres_all)

    def part(base):
        for piece in range(span // width):
            first = base + piece * width
            if not isinstance(first, int):
                first = pl.multiple_of(first, width)
            tile = kernel_tile(points, centre_ref, shift_ref, floor_ref, first, width)
            high = tile.astype(BF16)
            high_ref[rows, pl.ds(first, width)] = high
            low_ref[rows, pl.ds(first, width)] = (tile - high.astype(F32)).astype(BF16)

    if centres_all == span:
        part(0)
    else:
        lax.fori_loop(0, centres_all // span, lambda i, _: part(i * span), None)


def fetch(pairs, sems):
    copies = [pltpu.make_async_copy(src, dst, sems.at[i]) for i, (src, dst) in enumerate(pairs)]
    for copy in copies:
        copy.start()
    return copies


def modulo(value):
    turns = (value.astype(F32) * (1.0 / LATTICE)).astype(jnp.int32)
    rest = value - turns * LATTICE
    rest = jnp.where(rest < 0, rest + LATTICE, rest)
    return jnp.where(rest >= LATTICE, rest - LATTICE, rest)


def column_of(values_ref, dims, dtype):
    row = lax.broadcasted_iota(jnp.int32, (dims, 1), 0)
    column = jnp.zeros((dims, 1), dtype)
    for axis_number in range(dims):
        column = jnp.where(row == axis_number, values_ref[axis_number], column)
    return column


def set_up(order_bits, cen_dev, generator_ref, weight_ref, shift_ref, floor_ref, centre_ref):
    dims, centres_all = centre_ref.shape
    curves = [math.pi * math.pi * 0.75**weight for weight in range(8)]
    for axis_number in range(dims):
        weight = weight_ref[axis_number]
        shift, floor = 0.5 * math.sqrt(curves[7]), 1.0 - curves[7] / 12.0
        for k in range(7):
            shift = jnp.where(weight == k, F32(0.5 * math.sqrt(curves[k])), shift)
            floor = jnp.where(weight == k, F32(1.0 - curves[k] / 12.0), floor)
        shift_ref[axis_number] = shift
        floor_ref[axis_number] = floor
    scale = column_of(shift_ref, dims, F32) * (2.0 / LATTICE)
    generator = column_of(generator_ref, dims, jnp.int32)
    place = lax.broadcasted_iota(jnp.int32, (1, centres_all), 1)
    owner = jnp.zeros_like(place) + lax.axis_index("samp")
    for k, bit in enumerate(order_bits):
        owner = jnp.where((place & (cen_dev << k)) != 0, owner ^ bit, owner)
    column = owner * cen_dev + (place & (cen_dev - 1))
    upper = modulo(column * (generator >> 8))
    centre = modulo(upper * 256 + column * (generator & 255))
    centre_ref[...] = centre.astype(F32) * scale
    return scale


def store_rows(
    first_row, step_rows, order, generator_hbm, weight_hbm, samples_hbm, passed_ref,
    high_hbm, low_hbm, handed_ref, generator_ref, weight_ref, shift_ref, floor_ref, sample_ref,
    centre_ref, high_ref, low_ref, in_sems, out_sems,
):
    rows_all = high_hbm.shape[0]
    copies = fetch(
        [
            (generator_hbm, generator_ref),
            (weight_hbm, weight_ref),
            (samples_hbm.at[:, pl.ds(first_row, rows_all)], sample_ref),
        ],
        in_sems,
    )
    handed_ref[...] = passed_ref[...]
    copies[0].wait()
    copies[1].wait()
    scale = set_up(*order, generator_ref, weight_ref, shift_ref, floor_ref, centre_ref)
    copies[2].wait()

    def sends(step):
        slot = lax.rem(step, 2)
        rows = pl.ds(pl.multiple_of(step * step_rows, step_rows), step_rows)
        return [
            pltpu.make_async_copy(high_ref.at[slot], high_hbm.at[rows], out_sems.at[slot, 0]),
            pltpu.make_async_copy(low_ref.at[slot], low_hbm.at[rows], out_sems.at[slot, 1]),
        ]

    steps = rows_all // step_rows

    def step(i, _):
        slot = lax.rem(i, 2)

        @pl.when(i >= 2)
        def _():
            for copy in sends(i - 2):
                copy.wait()

        columns = pl.ds(pl.multiple_of(i * step_rows, step_rows), step_rows)
        points = (sample_ref[:, columns].astype(F32) * scale).T
        rows = pl.ds(0, step_rows)
        fill_kernel(
            rows, points, centre_ref, shift_ref, floor_ref, high_ref.at[slot], low_ref.at[slot]
        )
        for copy in sends(i):
            copy.start()

    lax.fori_loop(0, steps, step, None)
    for last in range(max(0, steps - 2), steps):
        for copy in sends(last):
            copy.wait()


def set_up_scratch(dims, rows, centres_all):
    return [
        pltpu.SMEM((dims,), jnp.int32),
        pltpu.SMEM((dims,), jnp.int32),
        pltpu.SMEM((dims,), F32),
        pltpu.SMEM((dims,), F32),
        pltpu.VMEM((dims, rows), jnp.int32),
        pltpu.VMEM((dims, centres_all), F32),
    ]


def in_hbm(*values):
    return [pltpu.with_memory_space_constraint(value, pltpu.HBM) for value in values]


def kernel_rows(passed, first_row, rows, order, centres_all, lattice):
    dims = lattice[2].shape[0]
    kept = jax.ShapeDtypeStruct((rows, centres_all), BF16)
    step_rows = min(128, rows)
    high, low, handed = pl.pallas_call(
        functools.partial(store_rows, first_row, step_rows, order),
        in_specs=[HBM, HBM, HBM, VMEM],
        out_specs=[FREE, FREE, VMEM],
        out_shape=[kept, kept, jax.ShapeDtypeStruct(passed.shape, passed.dtype)],
        scratch_shapes=[
            *set_up_scratch(dims, rows, centres_all),
            pltpu.VMEM((2, step_rows, centres_all), BF16),
            pltpu.VMEM((2, step_rows, centres_all), BF16),
            pltpu.SemaphoreType.DMA((3,)),
            pltpu.SemaphoreType.DMA((2, 2)),
        ],
        compiler_params=pltpu.CompilerParams(vmem_limit_bytes=12 << 20),
        cost_estimate=pl.CostEstimate(
            flops=6 * dims * rows * centres_all,
            bytes_accessed=4 * rows * centres_all,
            transcendentals=0,
        ),
        name="kernel_rows",
    )(*in_hbm(*lattice), passed)
    return (high, low), handed


def apply_kernel(high, low, coefficients, outs):
    contract = (((1,), (1,)), ((), ()))
    fitted = lax.dot_general(coefficients, high, contract, preferred_element_type=F32)
    fitted = fitted + lax.dot_general(coefficients, low, contract, preferred_element_type=F32)
    return add_parts(fitted, outs)


def back_products(high, low, coefficients, outs):
    parts = stack3(apply_kernel(high, low, coefficients, outs))
    return jnp.dot(parts, high, preferred_element_type=F32) + jnp.dot(
        parts, low, preferred_element_type=F32
    )


def products(
    outs, block_rows, stored, order, coef_ref, generator_hbm, weight_hbm, samples_hbm,
    solution_hbm, residual_hbm, direction_hbm, *refs,
):
    stored_hbm, refs = refs[: 2 * len(stored)], refs[2 * len(stored) :]
    *backward_refs, own_out_ref, own_state_ref = refs[:4]
    generator_ref, weight_ref, shift_ref, floor_ref, sample_ref, centre_ref = refs[4:10]
    parts_ref, sum_ref, made_high, made_low, high_ref, low_ref, sems = refs[10:]
    own_rows = own_out_ref.shape[1]
    steps = sample_ref.shape[1] // block_rows
    stored_rows = sum(stored)
    share = stored_rows // steps
    columns = pl.ds(stored_rows, sample_ref.shape[1])
    copies = fetch(
        [
            (generator_hbm, generator_ref),
            (weight_hbm, weight_ref),
            (samples_hbm.at[:, columns], sample_ref),
            (solution_hbm, own_state_ref.at[pl.ds(0, outs)]),
            (residual_hbm, own_state_ref.at[pl.ds(outs, outs)]),
            (direction_hbm, own_state_ref.at[pl.ds(2 * outs, outs)]),
        ],
        sems,
    )
    first = 0
    for i, rows in enumerate(stored):
        pairs = zip(stored_hbm[2 * i : 2 * i + 2], (high_ref, low_ref))
        place = pl.ds(first, rows)
        copies += fetch([(src, dst.at[place]) for src, dst in pairs], sems.at[pl.ds(6 + 2 * i, 2)])
        first += rows

    parts_ref[...] = stack3(coef_ref[...])
    sum_ref[...] = jnp.zeros_like(sum_ref)
    made_high[1] = jnp.zeros(made_high.shape[1:], BF16)
    made_low[1] = jnp.zeros(made_low.shape[1:], BF16)
    copies[0].wait()
    copies[1].wait()
    scale = set_up(*order, generator_ref, weight_ref, shift_ref, floor_ref, centre_ref)
    own_high, own_low = made_high.at[0], made_low.at[0]
    rows = pl.ds(0, own_rows)
    own_points = centre_ref[:, :own_rows]
    fill_kernel(rows, own_points.T, centre_ref, shift_ref, floor_ref, own_high, own_low)
    own_out_ref[...] = apply_kernel(own_high[rows], own_low[rows], parts_ref[...], outs)
    for copy in copies[2:]:
        copy.wait()

    def step(i, _):
        now = lax.rem(i, 2)
        before = 1 - now
        coefficients = parts_ref[...]
        total = back_products(made_high[before], made_low[before], coefficients, outs)
        if share:
            rows = pl.ds(pl.multiple_of(i * share, share), share)
            total = total + back_products(high_ref[rows], low_ref[rows], coefficients, outs)
        columns = pl.ds(pl.multiple_of(i * block_rows, block_rows), block_rows)
        points = (sample_ref[:, columns].astype(F32) * scale).T
        for first in range(0, block_rows, 128):
            rows = pl.ds(first, 128)
            fill_kernel(
                rows, points[first : first + 128], centre_ref, shift_ref, floor_ref,
                made_high.at[now], made_low.at[now],
            )
        sum_ref[...] += total

    lax.fori_loop(0, steps, step, None)
    now = (steps - 1) % 2
    last = sum_ref[...] + back_products(made_high[now], made_low[now], parts_ref[...], outs)
    last = add_parts(last, outs)
    width = last.shape[1] // len(backward_refs)
    for i, backward_ref in enumerate(backward_refs):
        backward_ref[...] = last[:, i * width : (i + 1) * width]


def apply_products(store, coefficients, own_state, block_rows, order, lattice):
    outs, centres_all = coefficients.shape
    own_rows = own_state[0].shape[1]
    dims, samples_dev = lattice[2].shape
    stored = tuple(high.shape[0] for high, _ in store)
    made = pltpu.VMEM((2, block_rows, centres_all), BF16)
    kept = pltpu.VMEM((max(16, sum(stored)), centres_all), BF16)
    rows = samples_dev - sum(stored)
    return pl.pallas_call(
        functools.partial(products, outs, block_rows, stored, order),
        in_specs=[VMEM, *[HBM] * 6, *[FREE] * (2 * len(stored))],
        out_specs=[VMEM, VMEM, VMEM, VMEM],
        out_shape=[
            jax.ShapeDtypeStruct((outs, centres_all // 2), F32),
            jax.ShapeDtypeStruct((outs, centres_all // 2), F32),
            jax.ShapeDtypeStruct((outs, own_rows), F32),
            jax.ShapeDtypeStruct((3 * outs, own_rows), F32),
        ],
        scratch_shapes=[
            *set_up_scratch(dims, rows, centres_all),
            pltpu.VMEM((3 * outs, centres_all), BF16),
            pltpu.VMEM((3 * outs, centres_all), F32),
            made,
            made,
            kept,
            kept,
            pltpu.SemaphoreType.DMA((6 + 2 * len(stored),)),
        ],
        compiler_params=pltpu.CompilerParams(
            vmem_limit_bytes=(14 << 20) + (16 * block_rows + 4 * sum(stored)) * centres_all
        ),
        cost_estimate=pl.CostEstimate(
            flops=6 * dims * rows * centres_all,
            bytes_accessed=4 * sum(stored) * centres_all,
            transcendentals=0,
        ),
        name="products",
    )(coefficients, *in_hbm(*lattice, *own_state), *[part for pair in store for part in pair])


def row_products(outs, count, state_ref, *refs):
    coef_ref, parts_ref, fetched_ref, sems = refs[count:]
    copy = pltpu.make_async_copy(refs[0], fetched_ref, sems.at[0])
    copy.start()
    state = stack3(state_ref[:outs])
    cen_dev = refs[0].shape[0]
    piece_refs = [*enumerate(refs[1:count], 1), (0, fetched_ref)]
    for i, piece_ref in piece_refs:
        if i == 0:
            copy.wait()
        rows = slice(i * cen_dev, (i + 1) * cen_dev)
        for k, part in enumerate(split3(piece_ref[...])):
            parts_ref[k, rows] = part
    total = None
    for k in range(3):
        term = lax.dot_general(
            state, parts_ref[k], (((1,), (1,)), ((), ())), preferred_element_type=F32
        )
        total = term if total is None else total + term
    coef_ref[...] = add_parts(total, outs)


def image_rows(scale_total, ridge, kept_ref, came_ref, own_ref, *refs):
    *part_refs, image_ref = refs
    outs, cen_dev = own_ref.shape
    applied = (kept_ref[...] + came_ref[...]) * (1.0 / scale_total)
    own = ridge * own_ref[...]
    rest = applied.shape[1] - cen_dev
    if rest:
        own = jnp.concatenate([own, jnp.zeros((outs, rest), F32)], axis=1)
    rows = stack3(applied + own)
    total, first = None, 0
    for part_ref in part_refs:
        some = rows[:, first : first + part_ref.shape[1]]
        first += part_ref.shape[1]
        for k in range(3):
            term = jnp.dot(some, part_ref[k], preferred_element_type=F32)
            total = term if total is None else total + term
    image_ref[...] = add_parts(total, outs)


def finish(
    image_ref, more_ref, state_ref, own_ref, new_solution_ref, new_residual_ref, new_direction_ref, total_ref
):
    outs, cen_dev = new_solution_ref.shape
    image = image_ref[...] + more_ref[...]
    total_ref[...] = image
    residual_full = state_ref[outs:]
    norm_old = jnp.sum(residual_full * residual_full, axis=1, keepdims=True)
    curvature = jnp.sum(state_ref[:outs] * image, axis=1, keepdims=True)
    step_length = norm_old / curvature
    next_full = residual_full - step_length * image
    norm_new = jnp.sum(next_full * next_full, axis=1, keepdims=True)
    index = lax.axis_index("samp")
    share = max(1, 128 // cen_dev)
    first = pl.multiple_of((index // share) * 128, 128)
    wide = total_ref[:, pl.ds(first, 128)]
    own_image = wide[:, :cen_dev]
    for k in range(1, share):
        here = lax.rem(index, share) == k
        own_image = jnp.where(here, wide[:, k * cen_dev : (k + 1) * cen_dev], own_image)
    direction = own_ref[2 * outs :]
    new_solution_ref[...] = own_ref[:outs] + step_length * direction
    new_residual = own_ref[outs : 2 * outs] - step_length * own_image
    new_residual_ref[...] = new_residual
    new_direction_ref[...] = new_residual + (norm_new / norm_old) * direction


def body(samples, generator, weight_index, preconditioner, solution, residual, direction):
    devices = lax.axis_size("samp")
    index = lax.axis_index("samp")
    cen_dev, centres_all = preconditioner.shape
    samples_dev = samples.shape[1]
    outs = direction.shape[0]
    held, others = plan(devices, 4 * cen_dev * centres_all)

    order = ((*held, *others), cen_dev)
    lattice = (generator, weight_index, samples)

    half = samples_dev // 2
    use_store = 4 * half * centres_all <= STORE_BYTES
    store, filled = [], 0

    def fill(rows, passed):
        nonlocal filled
        rows = min(rows, half - filled) if use_store else 0
        if rows == 0:
            return passed
        made, handed = kernel_rows(passed, filled, rows, order, centres_all, lattice)
        store.append(made)
        filled += rows
        return handed

    pieces = [preconditioner]
    early = [swap(preconditioner, bit, devices) for bit in held[:2]]
    pieces += early[:1]
    if len(early) > 1:
        pieces += [early[1], swap(early[0], held[1], devices)]
    bit = 1
    state = None
    while bit < devices:
        upper = (index & bit) != 0
        if state is None:
            mine = [direction, residual]
            other = [swap(direction, bit, devices), swap(residual, bit, devices)]
            joined = [jnp.concatenate(pair, axis=1) for pair in zip(other, mine)]
            turned = [jnp.concatenate(pair, axis=1) for pair in zip(mine, other)]
            state = jnp.where(upper, jnp.concatenate(joined), jnp.concatenate(turned))
        else:
            other = swap(state, bit, devices)
            mine = fill(256 if 2 * bit == devices else 128, state)
            state = jnp.where(
                upper,
                jnp.concatenate([other, mine], axis=1),
                jnp.concatenate([mine, other], axis=1),
            )
        bit *= 2

    def coefficients_of(group):
        rows = len(group) * cen_dev
        return pl.pallas_call(
            functools.partial(row_products, outs, len(group)),
            out_shape=[
                jax.ShapeDtypeStruct((outs, rows), F32),
                jax.ShapeDtypeStruct((3, rows, centres_all), BF16),
            ],
            in_specs=[VMEM, HBM, *[VMEM] * (len(group) - 1)],
            scratch_shapes=[
                pltpu.VMEM((cen_dev, centres_all), F32),
                pltpu.SemaphoreType.DMA((1,)),
            ],
            compiler_params=pltpu.CompilerParams(
                vmem_limit_bytes=(4 << 20) + 24 * rows * centres_all
            ),
            name="row_products",
        )(state, *in_hbm(group[0]), *group[1:])

    groups = [pieces]
    for bit in held[2:]:
        groups.append([swap(p, bit, devices) for p in sum(groups, [])])
    made = [coefficients_of(group) for group in groups]
    coefficients = jnp.concatenate([m[0] for m in made], axis=1)
    parts = [m[1] for m in made]
    for bit in others:
        other = swap(coefficients, bit, devices)
        mine = fill(512, coefficients)
        coefficients = jnp.concatenate([mine, other], axis=1)
    coefficients = fill(half, coefficients)

    kept, sent, kernel_products, own_state = apply_products(
        store, coefficients, (solution, residual, direction), 256, order, lattice
    )
    for bit in reversed(others):
        came = swap(sent, bit, devices)
        if bit != others[0]:
            summed = kept + came
            width = summed.shape[1] // 2
            kept, sent = summed[:, :width], summed[:, width:]
    scale_total = float(samples_dev * devices) * float(centres_all)
    image = pl.pallas_call(
        functools.partial(image_rows, scale_total, ridge_weight / centres_all),
        out_shape=jax.ShapeDtypeStruct((outs, centres_all), F32),
        compiler_params=pltpu.CompilerParams(
            vmem_limit_bytes=(4 << 20) + 8 * kept.shape[1] * centres_all
        ),
        name="image_rows",
    )(kept, came, kernel_products, *parts)
    bit = 1
    while 2 * bit < devices:
        image = image + swap(image, bit, devices)
        bit *= 2
    more = swap(image, bit, devices)
    own = jax.ShapeDtypeStruct(solution.shape, F32)
    return pl.pallas_call(
        finish,
        out_shape=[own, own, own],
        scratch_shapes=[pltpu.VMEM((outs, centres_all), F32)],
        name="finish",
    )(image, more, state, own_state)


def solution(mesh):
    placed = (
        P("groups", "samp"),
        P(),
        P(),
        P("samp", None),
        P("groups", "samp"),
        P("groups", "samp"),
        P("groups", "samp"),
    )
    return jax.shard_map(
        body,
        mesh=mesh,
        in_specs=placed,
        out_specs=(P("groups", "samp"), P("groups", "samp"), P("groups", "samp")),
        check_vma=False,
    )
```

```python
import functools
import math

import jax
import jax.numpy as jnp
from jax import lax
from jax.experimental import pallas as pl
from jax.experimental.pallas import tpu as pltpu
from jax.sharding import PartitionSpec as P

LATTICE = 65521
MIDDLE = LATTICE // 2

ridge_weight = 0.25
STORE_BYTES = 12 << 20
HELD_BYTES = 16 << 20
WIDTH = 256
STORED_MIXED = 16
PRODUCTS_MIXED = 4
VMEM = pl.BlockSpec(memory_space=pltpu.VMEM)
FREE = pl.BlockSpec(memory_space=pl.ANY)
HBM = pl.BlockSpec(memory_space=pltpu.HBM)
SMEM = pl.BlockSpec(memory_space=pltpu.SMEM)
F32 = jnp.float32
BF16 = jnp.bfloat16


def swap(value, bit, devices):
    return lax.ppermute(value, "samp", [(i, i ^ bit) for i in range(devices)])


def plan(devices, piece_bytes):
    bits = [1 << k for k in range(devices.bit_length() - 1)]
    held = []
    for bit in [b for b in (devices // 4, *bits) if 0 < b < devices // 2]:
        if bit not in held and (2 << len(held)) * piece_bytes <= HELD_BYTES:
            held.append(bit)
    held = held[:1] + held[:0:-1] if len(held) > 1 else held
    return held, [b for b in bits if b not in held]


def split3(value):
    high = value.astype(BF16)
    rest = value - high.astype(F32)
    middle = rest.astype(BF16)
    low = (rest - middle.astype(F32)).astype(BF16)
    return high, middle, low


def stack3(value):
    return jnp.concatenate(split3(value), axis=0)


def add_parts(value, outs):
    return value[:outs] + (value[outs : 2 * outs] + value[2 * outs :])


def bilinear_terms(sources, count, columns):
    place = lax.broadcasted_iota(jnp.int32, (count * 16, columns), 1)
    row = lax.broadcasted_iota(jnp.int32, (count * 16, columns), 0)
    term = place & 15
    source = jnp.full_like(place, -16)
    for k, which in enumerate(sources):
        source = jnp.where(term == k, which, source)
    return jnp.where(row == source * 16 + (place >> 4), 1.0, 0.0).astype(BF16)


def point_block(coordinates, constants, mixed, pick_ref, lhs_ref):
    scale, curve, base = constants
    centred = coordinates - MIDDLE
    if mixed:
        real = centred.astype(F32)
        unit = real * (1.0 / LATTICE)
        large = jnp.floor(real * (1.0 / 256.0) + 0.5) * 256.0
        alone = curve * (unit * unit + unit) + base
        ones = jnp.ones(real.shape, BF16)
        sources = [*split3(alone), large.astype(BF16), (real - large).astype(BF16), ones]
        terms = lax.dot_general(
            jnp.concatenate(sources, axis=0),
            pick_ref[...],
            (((0,), (0,)), ((), ())),
            preferred_element_type=F32,
        ).astype(BF16)
        rows = terms.shape[0]
        for axis_number in range(mixed):
            lhs_ref[axis_number, :rows] = terms[:, axis_number * 128 : axis_number * 128 + 16]
    return (centred.astype(F32) * scale).T


def kernel_tile(points, mixed, lhs_ref, rhs_ref, centre_ref, shift_ref, floor_ref, first, width):
    rows, dims = points.shape
    product = None
    columns = pl.ds(first, width)
    for axis_number in kernel_order(dims, mixed):
        centre = centre_ref[axis_number : axis_number + 1, columns]
        point = jnp.broadcast_to(points[:, axis_number : axis_number + 1], (rows, width))
        if axis_number < mixed:
            bilinear = jnp.dot(
                lhs_ref[axis_number, :rows],
                rhs_ref[pl.ds(axis_number * 16, 16), columns],
                preferred_element_type=F32,
            )
            factor = bilinear - jnp.maximum(point, centre)
        else:
            arm = jnp.abs(point - centre) - shift_ref[axis_number]
            factor = arm * arm + floor_ref[axis_number]
        product = factor if product is None else product * factor
    return product


def kernel_order(dims, mixed):
    kinds = [list(range(mixed)), list(range(mixed, dims))]
    order = []
    while kinds[0] or kinds[1]:
        first = len(kinds[0]) * (dims - mixed) >= len(kinds[1]) * mixed
        order.append(kinds[0 if kinds[0] and (first or not kinds[1]) else 1].pop(0))
    return order


def fill_kernel(rows, points, mixed, tables, high_ref, low_ref, between=()):
    lhs_ref, rhs_ref, centre_ref, shift_ref, floor_ref = tables
    centres_all = centre_ref.shape[1]
    width = min(WIDTH, centres_all)
    span = min(1024, centres_all)
    between = list(between)

    def part(base):
        for piece in range(span // width):
            if between:
                between.pop(0)()
            first = base + piece * width
            if not isinstance(first, int):
                first = pl.multiple_of(first, width)
            tile = kernel_tile(
                points, mixed, lhs_ref, rhs_ref, centre_ref, shift_ref, floor_ref, first, width
            )
            high = tile.astype(BF16)
            high_ref[rows, pl.ds(first, width)] = high
            low_ref[rows, pl.ds(first, width)] = (tile - high.astype(F32)).astype(BF16)

    if centres_all == span:
        part(0)
    else:
        while between:
            between.pop(0)()
        lax.fori_loop(0, centres_all // span, lambda i, _: part(i * span), None)
    while between:
        between.pop(0)()


def fetch(pairs, sems):
    copies = [pltpu.make_async_copy(src, dst, sems.at[i]) for i, (src, dst) in enumerate(pairs)]
    for copy in copies:
        copy.start()
    return copies


def modulo(value):
    turns = (value.astype(F32) * (1.0 / LATTICE)).astype(jnp.int32)
    rest = value - turns * LATTICE
    rest = jnp.where(rest < 0, rest + LATTICE, rest)
    return jnp.where(rest >= LATTICE, rest - LATTICE, rest)


def column_of(values_ref, dims, dtype):
    row = lax.broadcasted_iota(jnp.int32, (dims, 1), 0)
    column = jnp.zeros((dims, 1), dtype)
    for axis_number in range(dims):
        column = jnp.where(row == axis_number, values_ref[axis_number], column)
    return column


def centre_coordinates(order, generator_ref, dims, count):
    order_bits, cen_dev = order
    generator = column_of(generator_ref, dims, jnp.int32)
    place = lax.broadcasted_iota(jnp.int32, (1, count), 1)
    owner = jnp.zeros_like(place) + lax.axis_index("samp")
    for k, bit in enumerate(order_bits):
        owner = jnp.where((place & (cen_dev << k)) != 0, owner ^ bit, owner)
    column = owner * cen_dev + (place & (cen_dev - 1))
    upper = modulo(column * (generator >> 8))
    return modulo(upper * 256 + column * (generator & 255))


def set_up(order, mixed, generator_ref, weight_ref, tables, pick_ref):
    _, rhs_ref, centre_ref, shift_ref, floor_ref = tables
    dims, centres_all = centre_ref.shape
    curves = [math.pi * math.pi * 0.75**weight for weight in range(8)]
    for axis_number in range(dims):
        weight = weight_ref[axis_number]
        shift, floor = 0.5 * math.sqrt(curves[7]), 1.0 - curves[7] / 12.0
        for k in range(7):
            shift = jnp.where(weight == k, F32(0.5 * math.sqrt(curves[k])), shift)
            floor = jnp.where(weight == k, F32(1.0 - curves[k] / 12.0), floor)
        shift_ref[axis_number] = shift
        floor_ref[axis_number] = floor
    half_root = column_of(shift_ref, dims, F32)
    curve = 4.0 * half_root * half_root
    base = column_of(floor_ref, dims, F32) + 0.25 * curve
    row = lax.broadcasted_iota(jnp.int32, (dims, 1), 0)
    scale = jnp.where(row < mixed, 2.0 * curve, 2.0 * half_root) * (1.0 / LATTICE)
    centre = centre_coordinates(order, generator_ref, dims, centres_all)
    real = (centre - MIDDLE).astype(F32)
    centre_ref[...] = real * scale
    if mixed:
        unit = real * (1.0 / LATTICE)
        alone = curve * (unit * unit + unit)
        slope = (-2.0 / LATTICE) * curve * unit
        ones = jnp.ones(real.shape, BF16)
        sources = jnp.concatenate([ones, *split3(alone), *split3(slope)], axis=0)
        pick = bilinear_terms((0, 0, 0, 1, 2, 3, 4, 5, 6, 4, 5, 6), 7, 16 * dims)
        rhs_ref[...] = lax.dot_general(
            pick, sources, (((0,), (0,)), ((), ())), preferred_element_type=F32
        ).astype(BF16)
        place = lax.broadcasted_iota(jnp.int32, (6 * 16, 128), 1)
        row = lax.broadcasted_iota(jnp.int32, (6 * 16, 128), 0)
        source = jnp.full_like(place, -1000)
        for k, which in enumerate((0, 1, 2, 5, 5, 5, 3, 3, 3, 4, 4, 4)):
            source = jnp.where(place == k, which * 16, source)
        for axis_number in range(mixed):
            columns = slice(axis_number * 128, (axis_number + 1) * 128)
            pick_ref[:, columns] = jnp.where(row == source + axis_number, 1.0, 0.0).astype(BF16)
    return scale, curve, base


def store_rows(
    first_row, step_rows, order, mixed, generator_hbm, weight_hbm, samples_hbm, passed_ref,
    high_hbm, low_hbm, handed_ref, generator_ref, weight_ref, shift_ref, floor_ref, sample_ref,
    centre_ref, lhs_ref, rhs_ref, pick_ref, high_ref, low_ref, in_sems, out_sems,
):
    rows_all = high_hbm.shape[0]
    copies = fetch(
        [
            (generator_hbm, generator_ref),
            (weight_hbm, weight_ref),
            (samples_hbm.at[:, pl.ds(first_row, rows_all)], sample_ref),
        ],
        in_sems,
    )
    handed_ref[...] = passed_ref[...]
    copies[0].wait()
    copies[1].wait()
    tables = (lhs_ref, rhs_ref, centre_ref, shift_ref, floor_ref)
    constants = set_up(order, mixed, generator_ref, weight_ref, tables, pick_ref)
    copies[2].wait()

    def sends(step):
        slot = lax.rem(step, 2)
        rows = pl.ds(pl.multiple_of(step * step_rows, step_rows), step_rows)
        return [
            pltpu.make_async_copy(high_ref.at[slot], high_hbm.at[rows], out_sems.at[slot, 0]),
            pltpu.make_async_copy(low_ref.at[slot], low_hbm.at[rows], out_sems.at[slot, 1]),
        ]

    steps = rows_all // step_rows

    def step(i, _):
        slot = lax.rem(i, 2)

        @pl.when(i >= 2)
        def _():
            for copy in sends(i - 2):
                copy.wait()

        columns = pl.ds(pl.multiple_of(i * step_rows, step_rows), step_rows)
        points = point_block(sample_ref[:, columns], constants, mixed, pick_ref, lhs_ref)
        fill_kernel(
            pl.ds(0, step_rows), points, mixed, tables, high_ref.at[slot], low_ref.at[slot]
        )
        for copy in sends(i):
            copy.start()

    lax.fori_loop(0, steps, step, None)
    for last in range(max(0, steps - 2), steps):
        for copy in sends(last):
            copy.wait()


def set_up_scratch(dims, rows, centres_all, step_rows, mixed):
    return [
        pltpu.SMEM((dims,), jnp.int32),
        pltpu.SMEM((dims,), jnp.int32),
        pltpu.SMEM((dims,), F32),
        pltpu.SMEM((dims,), F32),
        pltpu.VMEM((dims, rows), jnp.int32),
        pltpu.VMEM((dims, centres_all), F32),
        pltpu.VMEM((max(1, mixed), step_rows, 16), BF16),
        pltpu.VMEM((16 * dims, centres_all if mixed else 128), BF16),
        pltpu.VMEM((6 * 16, 128 * max(1, mixed)), BF16),
    ]


def in_hbm(*values):
    return [pltpu.with_memory_space_constraint(value, pltpu.HBM) for value in values]


def kernel_rows(passed, first_row, rows, order, centres_all, lattice):
    dims = lattice[2].shape[0]
    kept = jax.ShapeDtypeStruct((rows, centres_all), BF16)
    step_rows = min(256, rows)
    high, low, handed = pl.pallas_call(
        functools.partial(store_rows, first_row, step_rows, order, STORED_MIXED),
        in_specs=[HBM, HBM, HBM, VMEM],
        out_specs=[FREE, FREE, VMEM],
        out_shape=[kept, kept, jax.ShapeDtypeStruct(passed.shape, passed.dtype)],
        scratch_shapes=[
            *set_up_scratch(dims, rows, centres_all, step_rows, STORED_MIXED),
            pltpu.VMEM((2, step_rows, centres_all), BF16),
            pltpu.VMEM((2, step_rows, centres_all), BF16),
            pltpu.SemaphoreType.DMA((3,)),
            pltpu.SemaphoreType.DMA((2, 2)),
        ],
        compiler_params=pltpu.CompilerParams(vmem_limit_bytes=16 << 20),
        cost_estimate=pl.CostEstimate(
            flops=6 * dims * rows * centres_all,
            bytes_accessed=4 * rows * centres_all,
            transcendentals=0,
        ),
        name="kernel_rows",
    )(*in_hbm(*lattice), passed)
    return (high, low), handed


def apply_kernel(high, low, coefficients, outs):
    contract = (((1,), (1,)), ((), ()))
    fitted = lax.dot_general(coefficients, high, contract, preferred_element_type=F32)
    fitted = fitted + lax.dot_general(coefficients, low, contract, preferred_element_type=F32)
    return add_parts(fitted, outs)


def back_products(high_ref, low_ref, coef_ref, outs):
    result = {}

    def there():
        result["parts"] = stack3(apply_kernel(high_ref[...], low_ref[...], coef_ref[...], outs))

    def back():
        parts = result["parts"]
        total = jnp.dot(parts, high_ref[...], preferred_element_type=F32)
        result["sum"] = total + jnp.dot(parts, low_ref[...], preferred_element_type=F32)

    return there, back, result


def products(
    outs, block_rows, stored, order, coef_ref, generator_hbm, weight_hbm, samples_hbm,
    solution_hbm, residual_hbm, direction_hbm, *refs,
):
    stored_hbm, refs = refs[: 2 * len(stored)], refs[2 * len(stored) :]
    *backward_refs, own_out_ref, own_state_ref = refs[:4]
    generator_ref, weight_ref, shift_ref, floor_ref, sample_ref = refs[4:9]
    centre_ref, lhs_ref, rhs_ref, pick_ref = refs[9:13]
    parts_ref, sum_ref, *made, high_ref, low_ref, sems = refs[13:]
    mixed = PRODUCTS_MIXED
    tables = (lhs_ref, rhs_ref, centre_ref, shift_ref, floor_ref)
    own_rows = own_out_ref.shape[1]
    steps = sample_ref.shape[1] // block_rows
    stored_rows = sum(stored)
    share = stored_rows // steps
    columns = pl.ds(stored_rows, sample_ref.shape[1])
    copies = fetch(
        [
            (generator_hbm, generator_ref),
            (weight_hbm, weight_ref),
            (samples_hbm.at[:, columns], sample_ref),
            (solution_hbm, own_state_ref.at[pl.ds(0, outs)]),
            (residual_hbm, own_state_ref.at[pl.ds(outs, outs)]),
            (direction_hbm, own_state_ref.at[pl.ds(2 * outs, outs)]),
        ],
        sems,
    )
    first = 0
    for i, rows in enumerate(stored):
        pairs = zip(stored_hbm[2 * i : 2 * i + 2], (high_ref, low_ref))
        place = pl.ds(first, rows)
        copies += fetch([(src, dst.at[place]) for src, dst in pairs], sems.at[pl.ds(6 + 2 * i, 2)])
        first += rows

    parts_ref[...] = stack3(coef_ref[...])
    sum_ref[...] = jnp.zeros_like(sum_ref)
    last_high, last_low = made[2:]
    last_high[...] = jnp.zeros_like(last_high)
    last_low[...] = jnp.zeros_like(last_low)
    copies[0].wait()
    copies[1].wait()
    constants = set_up(order, mixed, generator_ref, weight_ref, tables, pick_ref)
    own_high, own_low = made[:2]
    rows = pl.ds(0, own_rows)
    own_points = centre_coordinates(order, generator_ref, centre_ref.shape[0], own_rows)
    own_points = point_block(own_points, constants, mixed, pick_ref, lhs_ref)
    fill_kernel(rows, own_points, mixed, tables, own_high, own_low)
    own_out_ref[...] = apply_kernel(own_high[rows], own_low[rows], parts_ref[...], outs)
    for copy in copies[2:]:
        copy.wait()

    def half_step(i, now, before):
        work = [back_products(*before, parts_ref, outs)]
        if share:
            rows = pl.ds(pl.multiple_of(i * share, share), share)
            work.append(back_products(high_ref.at[rows], low_ref.at[rows], parts_ref, outs))
        between = [there for there, _, _ in work] + [back for _, back, _ in work]
        columns = pl.ds(pl.multiple_of(i * block_rows, block_rows), block_rows)
        points = point_block(sample_ref[:, columns], constants, mixed, pick_ref, lhs_ref)
        fill_kernel(pl.ds(0, block_rows), points, mixed, tables, *now, between)
        for _, _, result in work:
            sum_ref[...] += result["sum"]

    def step(i, _):
        half_step(2 * i, made[:2], made[2:])
        half_step(2 * i + 1, made[2:], made[:2])

    lax.fori_loop(0, steps // 2, step, None)
    there, back, result = back_products(*made[2:], parts_ref, outs)
    there()
    back()
    last = sum_ref[...] + result["sum"]
    last = add_parts(last, outs)
    width = last.shape[1] // len(backward_refs)
    for i, backward_ref in enumerate(backward_refs):
        backward_ref[...] = last[:, i * width : (i + 1) * width]


def apply_products(store, coefficients, own_state, block_rows, order, lattice):
    outs, centres_all = coefficients.shape
    own_rows = own_state[0].shape[1]
    dims, samples_dev = lattice[2].shape
    stored = tuple(high.shape[0] for high, _ in store)
    made = pltpu.VMEM((block_rows, centres_all), BF16)
    kept = pltpu.VMEM((max(16, sum(stored)), centres_all), BF16)
    rows = samples_dev - sum(stored)
    return pl.pallas_call(
        functools.partial(products, outs, block_rows, stored, order),
        in_specs=[VMEM, *[HBM] * 6, *[FREE] * (2 * len(stored))],
        out_specs=[VMEM, VMEM, VMEM, VMEM],
        out_shape=[
            jax.ShapeDtypeStruct((outs, centres_all // 2), F32),
            jax.ShapeDtypeStruct((outs, centres_all // 2), F32),
            jax.ShapeDtypeStruct((outs, own_rows), F32),
            jax.ShapeDtypeStruct((3 * outs, own_rows), F32),
        ],
        scratch_shapes=[
            *set_up_scratch(dims, rows, centres_all, block_rows, PRODUCTS_MIXED),
            pltpu.VMEM((3 * outs, centres_all), BF16),
            pltpu.VMEM((3 * outs, centres_all), F32),
            *[made] * 4,
            kept,
            kept,
            pltpu.SemaphoreType.DMA((6 + 2 * len(stored),)),
        ],
        compiler_params=pltpu.CompilerParams(
            vmem_limit_bytes=(16 << 20) + (16 * block_rows + 4 * sum(stored)) * centres_all
        ),
        cost_estimate=pl.CostEstimate(
            flops=6 * dims * rows * centres_all,
            bytes_accessed=4 * sum(stored) * centres_all,
            transcendentals=0,
        ),
        name="products",
    )(coefficients, *in_hbm(*lattice, *own_state), *[part for pair in store for part in pair])


def row_products(outs, count, state_ref, *refs):
    coef_ref, parts_ref, fetched_ref, sems = refs[count:]
    copy = pltpu.make_async_copy(refs[0], fetched_ref, sems.at[0])
    copy.start()
    state = stack3(state_ref[:outs])
    cen_dev = refs[0].shape[0]
    piece_refs = [*enumerate(refs[1:count], 1), (0, fetched_ref)]
    for i, piece_ref in piece_refs:
        if i == 0:
            copy.wait()
        rows = slice(i * cen_dev, (i + 1) * cen_dev)
        for k, part in enumerate(split3(piece_ref[...])):
            parts_ref[k, rows] = part
    total = None
    for k in range(3):
        term = lax.dot_general(
            state, parts_ref[k], (((1,), (1,)), ((), ())), preferred_element_type=F32
        )
        total = term if total is None else total + term
    coef_ref[...] = add_parts(total, outs)


def image_rows(scale_total, ridge, kept_ref, came_ref, own_ref, *refs):
    *part_refs, image_ref = refs
    outs, cen_dev = own_ref.shape
    applied = (kept_ref[...] + came_ref[...]) * (1.0 / scale_total)
    own = ridge * own_ref[...]
    rest = applied.shape[1] - cen_dev
    if rest:
        own = jnp.concatenate([own, jnp.zeros((outs, rest), F32)], axis=1)
    rows = stack3(applied + own)
    total, first = None, 0
    for part_ref in part_refs:
        some = rows[:, first : first + part_ref.shape[1]]
        first += part_ref.shape[1]
        for k in range(3):
            term = jnp.dot(some, part_ref[k], preferred_element_type=F32)
            total = term if total is None else total + term
    image_ref[...] = add_parts(total, outs)


def finish(
    image_ref, more_ref, state_ref, own_ref, new_solution_ref, new_residual_ref, new_direction_ref, total_ref
):
    outs, cen_dev = new_solution_ref.shape
    image = image_ref[...] + more_ref[...]
    total_ref[...] = image
    residual_full = state_ref[outs:]
    norm_old = jnp.sum(residual_full * residual_full, axis=1, keepdims=True)
    curvature = jnp.sum(state_ref[:outs] * image, axis=1, keepdims=True)
    step_length = norm_old / curvature
    next_full = residual_full - step_length * image
    norm_new = jnp.sum(next_full * next_full, axis=1, keepdims=True)
    index = lax.axis_index("samp")
    share = max(1, 128 // cen_dev)
    first = pl.multiple_of((index // share) * 128, 128)
    wide = total_ref[:, pl.ds(first, 128)]
    own_image = wide[:, :cen_dev]
    for k in range(1, share):
        here = lax.rem(index, share) == k
        own_image = jnp.where(here, wide[:, k * cen_dev : (k + 1) * cen_dev], own_image)
    direction = own_ref[2 * outs :]
    new_solution_ref[...] = own_ref[:outs] + step_length * direction
    new_residual = own_ref[outs : 2 * outs] - step_length * own_image
    new_residual_ref[...] = new_residual
    new_direction_ref[...] = new_residual + (norm_new / norm_old) * direction


def body(samples, generator, weight_index, preconditioner, solution, residual, direction):
    devices = lax.axis_size("samp")
    index = lax.axis_index("samp")
    cen_dev, centres_all = preconditioner.shape
    samples_dev = samples.shape[1]
    outs = direction.shape[0]
    held, others = plan(devices, 4 * cen_dev * centres_all)

    order = ((*held, *others), cen_dev)
    lattice = (generator, weight_index, samples)

    half = samples_dev // 2
    use_store = 4 * half * centres_all <= STORE_BYTES
    store, filled = [], 0

    def fill(rows, passed):
        nonlocal filled
        rows = min(rows, half - filled) if use_store else 0
        if rows == 0:
            return passed
        made, handed = kernel_rows(passed, filled, rows, order, centres_all, lattice)
        store.append(made)
        filled += rows
        return handed

    pieces = [preconditioner]
    early = [swap(preconditioner, bit, devices) for bit in held[:2]]
    pieces += early[:1]
    if len(early) > 1:
        pieces += [early[1], swap(early[0], held[1], devices)]
    bit = 1
    state = None
    while bit < devices:
        upper = (index & bit) != 0
        if state is None:
            mine = [direction, residual]
            other = [swap(direction, bit, devices), swap(residual, bit, devices)]
            joined = [jnp.concatenate(pair, axis=1) for pair in zip(other, mine)]
            turned = [jnp.concatenate(pair, axis=1) for pair in zip(mine, other)]
            state = jnp.where(upper, jnp.concatenate(joined), jnp.concatenate(turned))
        else:
            other = swap(state, bit, devices)
            mine = fill(256, state)
            state = jnp.where(
                upper,
                jnp.concatenate([other, mine], axis=1),
                jnp.concatenate([mine, other], axis=1),
            )
        bit *= 2

    def coefficients_of(group):
        rows = len(group) * cen_dev
        return pl.pallas_call(
            functools.partial(row_products, outs, len(group)),
            out_shape=[
                jax.ShapeDtypeStruct((outs, rows), F32),
                jax.ShapeDtypeStruct((3, rows, centres_all), BF16),
            ],
            in_specs=[VMEM, HBM, *[VMEM] * (len(group) - 1)],
            scratch_shapes=[
                pltpu.VMEM((cen_dev, centres_all), F32),
                pltpu.SemaphoreType.DMA((1,)),
            ],
            compiler_params=pltpu.CompilerParams(
                vmem_limit_bytes=(4 << 20) + 24 * rows * centres_all
            ),
            name="row_products",
        )(state, *in_hbm(group[0]), *group[1:])

    groups = [pieces]
    for bit in held[2:]:
        groups.append([swap(p, bit, devices) for p in sum(groups, [])])
    made = [coefficients_of(group) for group in groups]
    coefficients = jnp.concatenate([m[0] for m in made], axis=1)
    parts = [m[1] for m in made]
    for bit in others:
        other = swap(coefficients, bit, devices)
        mine = fill(256, coefficients)
        coefficients = jnp.concatenate([mine, other], axis=1)
    coefficients = fill(half, coefficients)

    kept, sent, kernel_products, own_state = apply_products(
        store, coefficients, (solution, residual, direction), 256, order, lattice
    )
    for bit in reversed(others):
        came = swap(sent, bit, devices)
        if bit != others[0]:
            summed = kept + came
            width = summed.shape[1] // 2
            kept, sent = summed[:, :width], summed[:, width:]
    scale_total = float(samples_dev * devices) * float(centres_all)
    image = pl.pallas_call(
        functools.partial(image_rows, scale_total, ridge_weight / centres_all),
        out_shape=jax.ShapeDtypeStruct((outs, centres_all), F32),
        compiler_params=pltpu.CompilerParams(
            vmem_limit_bytes=(4 << 20) + 8 * kept.shape[1] * centres_all
        ),
        name="image_rows",
    )(kept, came, kernel_products, *parts)
    bit = 1
    while 2 * bit < devices:
        image = image + swap(image, bit, devices)
        bit *= 2
    more = swap(image, bit, devices)
    own = jax.ShapeDtypeStruct(solution.shape, F32)
    return pl.pallas_call(
        finish,
        out_shape=[own, own, own],
        scratch_shapes=[pltpu.VMEM((outs, centres_all), F32)],
        name="finish",
    )(image, more, state, own_state)


def solution(mesh):
    placed = (
        P("groups", "samp"),
        P(),
        P(),
        P("samp", None),
        P("groups", "samp"),
        P("groups", "samp"),
        P("groups", "samp"),
    )
    return jax.shard_map(
        body,
        mesh=mesh,
        in_specs=placed,
        out_specs=(P("groups", "samp"), P("groups", "samp"), P("groups", "samp")),
        check_vma=False,
    )
```

```python
import functools
import math

import jax
import jax.numpy as jnp
from jax import lax
from jax.experimental import pallas as pl
from jax.experimental.pallas import tpu as pltpu
from jax.sharding import PartitionSpec as P

LATTICE = 65521
MIDDLE = LATTICE // 2

ridge_weight = 0.25
STORE_BYTES = 12 << 20
HELD_BYTES = 16 << 20
WIDTH = 256
STORED_MIXED = 16
PRODUCTS_MIXED = 4
VMEM = pl.BlockSpec(memory_space=pltpu.VMEM)
FREE = pl.BlockSpec(memory_space=pl.ANY)
HBM = pl.BlockSpec(memory_space=pltpu.HBM)
SMEM = pl.BlockSpec(memory_space=pltpu.SMEM)
F32 = jnp.float32
BF16 = jnp.bfloat16


def swap(value, bit, devices):
    return lax.ppermute(value, "samp", [(i, i ^ bit) for i in range(devices)])


def plan(devices, piece_bytes):
    bits = [1 << k for k in range(devices.bit_length() - 1)]
    held = []
    for bit in [b for b in (devices // 4, *bits) if 0 < b < devices // 2]:
        if bit not in held and (2 << len(held)) * piece_bytes <= HELD_BYTES:
            held.append(bit)
    held = held[:1] + held[:0:-1] if len(held) > 1 else held
    return held, [b for b in bits if b not in held]


def split3(value):
    high = value.astype(BF16)
    rest = value - high.astype(F32)
    middle = rest.astype(BF16)
    low = (rest - middle.astype(F32)).astype(BF16)
    return high, middle, low


def stack3(value):
    return jnp.concatenate(split3(value), axis=0)


def add_parts(value, outs):
    return value[:outs] + (value[outs : 2 * outs] + value[2 * outs :])


def bilinear_terms(sources, count, columns):
    place = lax.broadcasted_iota(jnp.int32, (count * 16, columns), 1)
    row = lax.broadcasted_iota(jnp.int32, (count * 16, columns), 0)
    term = place & 15
    source = jnp.full_like(place, -16)
    for k, which in enumerate(sources):
        source = jnp.where(term == k, which, source)
    return jnp.where(row == source * 16 + (place >> 4), 1.0, 0.0).astype(BF16)


def point_block(coordinates, tables, mixed, lhs_ref):
    _, _, constant_ref, pick_ref = tables
    curve, base = constant_ref[:, 0:1], constant_ref[:, 1:2]
    scale = scale_of(constant_ref[:, 2:3], curve, mixed)
    centred = coordinates - MIDDLE
    if mixed:
        real = centred.astype(F32)
        unit = real * (1.0 / LATTICE)
        large = jnp.floor(real * (1.0 / 256.0) + 0.5) * 256.0
        alone = curve * (unit * unit + unit) + base
        ones = jnp.ones(real.shape, BF16)
        sources = [*split3(alone), large.astype(BF16), (real - large).astype(BF16), ones]
        terms = lax.dot_general(
            jnp.concatenate(sources, axis=0),
            pick_ref[...],
            (((0,), (0,)), ((), ())),
            preferred_element_type=F32,
        ).astype(BF16)
        rows = terms.shape[0]
        for axis_number in range(mixed):
            lhs_ref[axis_number, :rows] = terms[:, axis_number * 128 : axis_number * 128 + 16]
    return (centred.astype(F32) * scale).T


def scale_of(shift, curve, mixed):
    row = lax.broadcasted_iota(jnp.int32, shift.shape, 0)
    return jnp.where(row < mixed, 2.0 * curve, 2.0 * shift) * (1.0 / LATTICE)


def kernel_tile(points, mixed, lhs_ref, tables, first, width):
    centre_ref, rhs_ref, constant_ref, _ = tables
    rows, dims = points.shape
    product = None
    columns = pl.ds(first, width)
    for axis_number in kernel_order(dims, mixed):
        own = slice(axis_number, axis_number + 1)
        kind = 0 if axis_number < mixed else 1
        centre = centre_ref[kind, own, columns]
        point = jnp.broadcast_to(points[:, axis_number : axis_number + 1], (rows, width))
        if axis_number < mixed:
            bilinear = jnp.dot(
                lhs_ref[axis_number, :rows],
                rhs_ref[pl.ds(axis_number * 16, 16), columns],
                preferred_element_type=F32,
            )
            factor = bilinear - jnp.maximum(point, centre)
        else:
            shift = jnp.broadcast_to(constant_ref[own, 2:3], (rows, width))
            floor = jnp.broadcast_to(constant_ref[own, 3:4], (rows, width))
            arm = jnp.abs(point - centre) - shift
            factor = arm * arm + floor
        product = factor if product is None else product * factor
    return product


def kernel_order(dims, mixed):
    kinds = [list(range(mixed)), list(range(mixed, dims))]
    order = []
    while kinds[0] or kinds[1]:
        first = len(kinds[0]) * (dims - mixed) >= len(kinds[1]) * mixed
        order.append(kinds[0 if kinds[0] and (first or not kinds[1]) else 1].pop(0))
    return order


def fill_kernel(rows, points, mixed, lhs_ref, tables, high_ref, low_ref, between=()):
    centres_all = tables[0].shape[2]
    width = min(WIDTH, centres_all)
    span = min(1024, centres_all)
    between = list(between)

    def part(base):
        for piece in range(span // width):
            if between:
                between.pop(0)()
            first = base + piece * width
            if not isinstance(first, int):
                first = pl.multiple_of(first, width)
            tile = kernel_tile(points, mixed, lhs_ref, tables, first, width)
            high = tile.astype(BF16)
            high_ref[rows, pl.ds(first, width)] = high
            low_ref[rows, pl.ds(first, width)] = (tile - high.astype(F32)).astype(BF16)

    if centres_all == span:
        part(0)
    else:
        while between:
            between.pop(0)()
        lax.fori_loop(0, centres_all // span, lambda i, _: part(i * span), None)
    while between:
        between.pop(0)()


def fetch(pairs, sems):
    copies = [pltpu.make_async_copy(src, dst, sems.at[i]) for i, (src, dst) in enumerate(pairs)]
    for copy in copies:
        copy.start()
    return copies


def modulo(value):
    turns = (value.astype(F32) * (1.0 / LATTICE)).astype(jnp.int32)
    rest = value - turns * LATTICE
    rest = jnp.where(rest < 0, rest + LATTICE, rest)
    return jnp.where(rest >= LATTICE, rest - LATTICE, rest)


def column_of(values_ref, dims, dtype):
    row = lax.broadcasted_iota(jnp.int32, (dims, 1), 0)
    column = jnp.zeros((dims, 1), dtype)
    for axis_number in range(dims):
        column = jnp.where(row == axis_number, values_ref[axis_number], column)
    return column


def centre_coordinates(order, generator_ref, dims, count):
    order_bits, cen_dev = order
    generator = column_of(generator_ref, dims, jnp.int32)
    place = lax.broadcasted_iota(jnp.int32, (1, count), 1)
    owner = jnp.zeros_like(place) + lax.axis_index("samp")
    for k, bit in enumerate(order_bits):
        owner = jnp.where((place & (cen_dev << k)) != 0, owner ^ bit, owner)
    column = owner * cen_dev + (place & (cen_dev - 1))
    upper = modulo(column * (generator >> 8))
    return modulo(upper * 256 + column * (generator & 255))


def begin(
    order, generator_hbm, weight_hbm, samples_hbm, piece_hbm, solution_hbm, residual_hbm, direction_hbm,
    sample_ref, piece_ref, own_state_ref, centre_ref, rhs_ref, constant_ref, pick_ref, own_points_ref,
    generator_ref, weight_ref, sems,
):
    outs = solution_hbm.shape[0]
    copies = fetch(
        [
            (generator_hbm, generator_ref),
            (weight_hbm, weight_ref),
            (samples_hbm, sample_ref),
            (piece_hbm, piece_ref),
            (solution_hbm, own_state_ref.at[pl.ds(0, outs)]),
            (residual_hbm, own_state_ref.at[pl.ds(outs, outs)]),
            (direction_hbm, own_state_ref.at[pl.ds(2 * outs, outs)]),
        ],
        sems,
    )
    _, dims, centres_all = centre_ref.shape
    place = lax.broadcasted_iota(jnp.int32, (6 * dims, 128), 1)
    row = lax.broadcasted_iota(jnp.int32, (6 * dims, 128), 0)
    source = jnp.full_like(place, -1000)
    for k, which in enumerate((0, 1, 2, 5, 5, 5, 3, 3, 3, 4, 4, 4)):
        source = jnp.where(place == k, which * dims, source)
    for axis_number in range(dims):
        columns = slice(axis_number * 128, (axis_number + 1) * 128)
        pick_ref[:, columns] = jnp.where(row == source + axis_number, 1.0, 0.0).astype(BF16)
    pick = bilinear_terms((0, 0, 0, 1, 2, 3, 4, 5, 6, 4, 5, 6), 7, 16 * dims)

    copies[0].wait()
    copies[1].wait()
    curves = [math.pi * math.pi * 0.75**weight for weight in range(8)]
    weight = column_of(weight_ref, dims, jnp.int32)
    shift = jnp.full((dims, 1), 0.5 * math.sqrt(curves[7]), F32)
    for k in range(7):
        shift = jnp.where(weight == k, 0.5 * math.sqrt(curves[k]), shift)
    curve = 4.0 * shift * shift
    floor = 1.0 - curve * (1.0 / 12.0)
    lane = lax.broadcasted_iota(jnp.int32, (dims, 128), 1)
    table = jnp.where(lane == 0, curve, jnp.where(lane == 1, floor + 0.25 * curve, 0.0))
    constant_ref[...] = jnp.where(lane == 2, shift, jnp.where(lane == 3, floor, table))

    centre = centre_coordinates(order, generator_ref, dims, centres_all)
    own_points_ref[...] = centre[:, :128]
    real = (centre - MIDDLE).astype(F32)
    for kind, mixed in ((0, dims), (1, 0)):
        centre_ref[kind] = real * scale_of(shift, curve, mixed)
    unit = real * (1.0 / LATTICE)
    alone = curve * (unit * unit + unit)
    slope = (-2.0 / LATTICE) * curve * unit
    ones = jnp.ones(real.shape, BF16)
    sources = jnp.concatenate([ones, *split3(alone), *split3(slope)], axis=0)
    rhs_ref[...] = lax.dot_general(
        pick, sources, (((0,), (0,)), ((), ())), preferred_element_type=F32
    ).astype(BF16)
    for copy in copies[2:]:
        copy.wait()


def store_rows(
    first_row, mixed, sample_ref, centre_ref, rhs_ref, constant_ref, pick_ref, passed_ref,
    high_ref, low_ref, handed_ref, lhs_ref,
):
    tables = (centre_ref, rhs_ref, constant_ref, pick_ref)
    handed_ref[...] = passed_ref[...]
    step_rows = lhs_ref.shape[1]

    def step(i, _):
        rows = pl.ds(pl.multiple_of(i * step_rows, step_rows), step_rows)
        columns = pl.ds(pl.multiple_of(first_row + i * step_rows, 128), step_rows)
        points = point_block(sample_ref[:, columns], tables, mixed, lhs_ref)
        fill_kernel(rows, points, mixed, lhs_ref, tables, high_ref, low_ref)

    lax.fori_loop(0, high_ref.shape[0] // step_rows, step, None)


def kernel_rows(passed, first_row, rows, tables):
    _, dims, centres_all = tables[1].shape
    kept = jax.ShapeDtypeStruct((rows, centres_all), BF16)
    high, low, handed = pl.pallas_call(
        functools.partial(store_rows, first_row, STORED_MIXED),
        out_shape=[kept, kept, jax.ShapeDtypeStruct(passed.shape, passed.dtype)],
        scratch_shapes=[pltpu.VMEM((max(1, STORED_MIXED), min(256, rows), 16), BF16)],
        compiler_params=pltpu.CompilerParams(vmem_limit_bytes=16 << 20),
        cost_estimate=pl.CostEstimate(
            flops=6 * dims * rows * centres_all,
            bytes_accessed=4 * rows * centres_all,
            transcendentals=0,
        ),
        name="kernel_rows",
    )(*tables, passed)
    return (high, low), handed


def in_hbm(*values):
    return [pltpu.with_memory_space_constraint(value, pltpu.HBM) for value in values]


def apply_kernel(high, low, coefficients, outs):
    contract = (((1,), (1,)), ((), ()))
    fitted = lax.dot_general(coefficients, high, contract, preferred_element_type=F32)
    fitted = fitted + lax.dot_general(coefficients, low, contract, preferred_element_type=F32)
    return add_parts(fitted, outs)


def back_products(high_ref, low_ref, coef_ref, outs):
    result = {}

    def there():
        result["parts"] = stack3(apply_kernel(high_ref[...], low_ref[...], coef_ref[...], outs))

    def back():
        parts = result["parts"]
        total = jnp.dot(parts, high_ref[...], preferred_element_type=F32)
        result["sum"] = total + jnp.dot(parts, low_ref[...], preferred_element_type=F32)

    return there, back, result


def products(
    outs, stored, coef_ref, sample_ref, centre_ref, rhs_ref, constant_ref, pick_ref, own_points_ref, *refs
):
    stored_refs, refs = refs[: 2 * len(stored)], refs[2 * len(stored) :]
    *backward_refs, own_out_ref = refs[:3]
    lhs_ref, parts_ref, sum_ref, *made = refs[3:]
    tables = (centre_ref, rhs_ref, constant_ref, pick_ref)
    mixed = PRODUCTS_MIXED
    own_rows = own_out_ref.shape[1]
    block_rows = made[0].shape[0]
    first_row = sum(stored)
    steps = (sample_ref.shape[1] - first_row) // block_rows

    parts_ref[...] = stack3(coef_ref[...])
    sum_ref[...] = jnp.zeros_like(sum_ref)
    last_high, last_low = made[2:]
    last_high[...] = jnp.zeros_like(last_high)
    last_low[...] = jnp.zeros_like(last_low)
    own_high, own_low = made[:2]
    rows = pl.ds(0, own_rows)
    own_points = point_block(own_points_ref[:, :own_rows], tables, mixed, lhs_ref)
    fill_kernel(rows, own_points, mixed, lhs_ref, tables, own_high, own_low)
    own_out_ref[...] = apply_kernel(own_high[rows], own_low[rows], parts_ref[...], outs)

    def half_step(i, now, before, given):
        work = [back_products(*before, parts_ref, outs)]
        if given:
            work.append(back_products(*given, parts_ref, outs))
        between = [there for there, _, _ in work] + [back for _, back, _ in work]
        columns = pl.ds(pl.multiple_of(first_row + i * block_rows, 128), block_rows)
        points = point_block(sample_ref[:, columns], tables, mixed, lhs_ref)
        fill_kernel(pl.ds(0, block_rows), points, mixed, lhs_ref, tables, *now, between)
        for _, _, result in work:
            sum_ref[...] += result["sum"]

    pairs = [stored_refs[2 * i : 2 * i + 2] for i in range(len(stored))]
    if pairs:
        for i in range(steps):
            now, before = (made[:2], made[2:]) if i % 2 == 0 else (made[2:], made[:2])
            half_step(i, now, before, pairs[i] if i < len(pairs) else None)
    else:

        def step(i, _):
            half_step(2 * i, made[:2], made[2:], None)
            half_step(2 * i + 1, made[2:], made[:2], None)

        lax.fori_loop(0, steps // 2, step, None)
    there, back, result = back_products(*made[2:], parts_ref, outs)
    there()
    back()
    last = sum_ref[...] + result["sum"]
    last = add_parts(last, outs)
    width = last.shape[1] // len(backward_refs)
    for i, backward_ref in enumerate(backward_refs):
        backward_ref[...] = last[:, i * width : (i + 1) * width]


def apply_products(store, coefficients, own_points, block_rows, tables):
    outs, centres_all = coefficients.shape
    dims, samples_dev = tables[0].shape
    own_rows = own_points.shape[1]
    stored = tuple(high.shape[0] for high, _ in store)
    made = pltpu.VMEM((block_rows, centres_all), BF16)
    rows = samples_dev - sum(stored)
    half = jax.ShapeDtypeStruct((outs, centres_all // 2), F32)
    return pl.pallas_call(
        functools.partial(products, outs, stored),
        out_shape=[half, half, jax.ShapeDtypeStruct((outs, own_rows), F32)],
        scratch_shapes=[
            pltpu.VMEM((max(1, PRODUCTS_MIXED), block_rows, 16), BF16),
            pltpu.VMEM((3 * outs, centres_all), BF16),
            pltpu.VMEM((3 * outs, centres_all), F32),
            *[made] * 4,
        ],
        compiler_params=pltpu.CompilerParams(
            vmem_limit_bytes=(16 << 20) + 16 * block_rows * centres_all
        ),
        cost_estimate=pl.CostEstimate(
            flops=6 * dims * rows * centres_all,
            bytes_accessed=4 * sum(stored) * centres_all,
            transcendentals=0,
        ),
        name="products",
    )(coefficients, *tables, own_points, *[part for pair in store for part in pair])


def row_products(outs, count, state_ref, *refs):
    coef_ref, parts_ref = refs[count:]
    state = stack3(state_ref[:outs])
    cen_dev = refs[0].shape[0]
    for i, piece_ref in enumerate(refs[:count]):
        rows = slice(i * cen_dev, (i + 1) * cen_dev)
        for k, part in enumerate(split3(piece_ref[...])):
            parts_ref[k, rows] = part
    total = None
    for k in range(3):
        term = lax.dot_general(
            state, parts_ref[k], (((1,), (1,)), ((), ())), preferred_element_type=F32
        )
        total = term if total is None else total + term
    coef_ref[...] = add_parts(total, outs)


def image_rows(scale_total, ridge, kept_ref, came_ref, own_ref, *refs):
    *part_refs, image_ref = refs
    outs, cen_dev = own_ref.shape
    applied = (kept_ref[...] + came_ref[...]) * (1.0 / scale_total)
    own = ridge * own_ref[...]
    rest = applied.shape[1] - cen_dev
    if rest:
        own = jnp.concatenate([own, jnp.zeros((outs, rest), F32)], axis=1)
    rows = stack3(applied + own)
    total, first = None, 0
    for part_ref in part_refs:
        some = rows[:, first : first + part_ref.shape[1]]
        first += part_ref.shape[1]
        for k in range(3):
            term = jnp.dot(some, part_ref[k], preferred_element_type=F32)
            total = term if total is None else total + term
    image_ref[...] = add_parts(total, outs)


def finish(
    image_ref, more_ref, state_ref, own_ref, new_solution_ref, new_residual_ref, new_direction_ref, total_ref
):
    outs, cen_dev = new_solution_ref.shape
    image = image_ref[...] + more_ref[...]
    total_ref[...] = image
    residual_full = state_ref[outs:]
    norm_old = jnp.sum(residual_full * residual_full, axis=1, keepdims=True)
    curvature = jnp.sum(state_ref[:outs] * image, axis=1, keepdims=True)
    step_length = norm_old / curvature
    next_full = residual_full - step_length * image
    norm_new = jnp.sum(next_full * next_full, axis=1, keepdims=True)
    index = lax.axis_index("samp")
    share = max(1, 128 // cen_dev)
    first = pl.multiple_of((index // share) * 128, 128)
    wide = total_ref[:, pl.ds(first, 128)]
    own_image = wide[:, :cen_dev]
    for k in range(1, share):
        here = lax.rem(index, share) == k
        own_image = jnp.where(here, wide[:, k * cen_dev : (k + 1) * cen_dev], own_image)
    direction = own_ref[2 * outs :]
    new_solution_ref[...] = own_ref[:outs] + step_length * direction
    new_residual = own_ref[outs : 2 * outs] - step_length * own_image
    new_residual_ref[...] = new_residual
    new_direction_ref[...] = new_residual + (norm_new / norm_old) * direction


def body(samples, generator, weight_index, preconditioner, solution, residual, direction):
    devices = lax.axis_size("samp")
    index = lax.axis_index("samp")
    cen_dev, centres_all = preconditioner.shape
    samples_dev = samples.shape[1]
    outs = direction.shape[0]
    held, others = plan(devices, 4 * cen_dev * centres_all)

    order = ((*held, *others), cen_dev)
    dims = samples.shape[0]
    sample_copy, piece_copy, own_state, *tables = pl.pallas_call(
        functools.partial(begin, order),
        in_specs=[HBM] * 7,
        out_shape=[
            jax.ShapeDtypeStruct(samples.shape, jnp.int32),
            jax.ShapeDtypeStruct(preconditioner.shape, F32),
            jax.ShapeDtypeStruct((3 * outs, cen_dev), F32),
            jax.ShapeDtypeStruct((2, dims, centres_all), F32),
            jax.ShapeDtypeStruct((16 * dims, centres_all), BF16),
            jax.ShapeDtypeStruct((dims, 128), F32),
            jax.ShapeDtypeStruct((6 * dims, 128 * dims), BF16),
            jax.ShapeDtypeStruct((dims, 128), jnp.int32),
        ],
        scratch_shapes=[
            pltpu.SMEM((dims,), jnp.int32),
            pltpu.SMEM((dims,), jnp.int32),
            pltpu.SemaphoreType.DMA((7,)),
        ],
        compiler_params=pltpu.CompilerParams(vmem_limit_bytes=32 << 20),
        name="begin",
    )(*in_hbm(generator, weight_index, samples, preconditioner, solution, residual, direction))
    own_points = tables.pop()[:, :cen_dev]
    tables = (sample_copy, *tables)

    half = samples_dev // 2
    use_store = 4 * half * centres_all <= STORE_BYTES
    store, filled = [], 0

    def fill(rows, passed):
        nonlocal filled
        rows = min(rows, half - filled) if use_store else 0
        if rows == 0:
            return passed
        made, handed = kernel_rows(passed, filled, rows, tables)
        store.append(made)
        filled += rows
        return handed

    pieces = [preconditioner]
    early = [swap(preconditioner, bit, devices) for bit in held[:2]]
    pieces += early[:1]
    if len(early) > 1:
        pieces += [early[1], swap(early[0], held[1], devices)]
    bit = 1
    state = None
    while bit < devices:
        upper = (index & bit) != 0
        if state is None:
            mine = [direction, residual]
            other = [swap(direction, bit, devices), swap(residual, bit, devices)]
            joined = [jnp.concatenate(pair, axis=1) for pair in zip(other, mine)]
            turned = [jnp.concatenate(pair, axis=1) for pair in zip(mine, other)]
            state = jnp.where(upper, jnp.concatenate(joined), jnp.concatenate(turned))
        else:
            other = swap(state, bit, devices)
            mine = fill(256, state)
            state = jnp.where(
                upper,
                jnp.concatenate([other, mine], axis=1),
                jnp.concatenate([mine, other], axis=1),
            )
        bit *= 2

    def coefficients_of(group):
        rows = len(group) * cen_dev
        return pl.pallas_call(
            functools.partial(row_products, outs, len(group)),
            out_shape=[
                jax.ShapeDtypeStruct((outs, rows), F32),
                jax.ShapeDtypeStruct((3, rows, centres_all), BF16),
            ],
            compiler_params=pltpu.CompilerParams(
                vmem_limit_bytes=(4 << 20) + 24 * rows * centres_all
            ),
            name="row_products",
        )(state, *group)

    groups = [[piece_copy, *pieces[1:]]]
    for bit in held[2:]:
        groups.append([swap(p, bit, devices) for p in [*pieces, *sum(groups[1:], [])]])
    made = [coefficients_of(group) for group in groups]
    coefficients = jnp.concatenate([m[0] for m in made], axis=1)
    parts = [m[1] for m in made]
    for bit in others:
        other = swap(coefficients, bit, devices)
        mine = fill(256, coefficients)
        coefficients = jnp.concatenate([mine, other], axis=1)
    coefficients = fill(half, coefficients)

    kept, sent, kernel_products = apply_products(store, coefficients, own_points, 256, tables)
    for bit in reversed(others):
        came = swap(sent, bit, devices)
        if bit != others[0]:
            summed = kept + came
            width = summed.shape[1] // 2
            kept, sent = summed[:, :width], summed[:, width:]
    scale_total = float(samples_dev * devices) * float(centres_all)
    image = pl.pallas_call(
        functools.partial(image_rows, scale_total, ridge_weight / centres_all),
        out_shape=jax.ShapeDtypeStruct((outs, centres_all), F32),
        compiler_params=pltpu.CompilerParams(
            vmem_limit_bytes=(4 << 20) + 8 * kept.shape[1] * centres_all
        ),
        name="image_rows",
    )(kept, came, kernel_products, *parts)
    bit = 1
    while 2 * bit < devices:
        image = image + swap(image, bit, devices)
        bit *= 2
    more = swap(image, bit, devices)
    own = jax.ShapeDtypeStruct(solution.shape, F32)
    return pl.pallas_call(
        finish,
        out_shape=[own, own, own],
        scratch_shapes=[pltpu.VMEM((outs, centres_all), F32)],
        name="finish",
    )(image, more, state, own_state)


def solution(mesh):
    placed = (
        P("groups", "samp"),
        P(),
        P(),
        P("samp", None),
        P("groups", "samp"),
        P("groups", "samp"),
        P("groups", "samp"),
    )
    return jax.shard_map(
        body,
        mesh=mesh,
        in_specs=placed,
        out_specs=(P("groups", "samp"), P("groups", "samp"), P("groups", "samp")),
        check_vma=False,
    )
```

```python
import functools
import math

import jax
import jax.numpy as jnp
from jax import lax
from jax.experimental import pallas as pl
from jax.experimental.pallas import tpu as pltpu
from jax.sharding import PartitionSpec as P

LATTICE = 65521
MIDDLE = LATTICE // 2

ridge_weight = 0.25
STORE_BYTES = 12 << 20
HELD_BYTES = 16 << 20
WIDTH = 256
STORED_MIXED = 16
PRODUCTS_MIXED = 10
VMEM = pl.BlockSpec(memory_space=pltpu.VMEM)
FREE = pl.BlockSpec(memory_space=pl.ANY)
HBM = pl.BlockSpec(memory_space=pltpu.HBM)
SMEM = pl.BlockSpec(memory_space=pltpu.SMEM)
F32 = jnp.float32
BF16 = jnp.bfloat16


def swap(value, bit, devices):
    return lax.ppermute(value, "samp", [(i, i ^ bit) for i in range(devices)])


def plan(devices, piece_bytes):
    bits = [1 << k for k in range(devices.bit_length() - 1)]
    held = []
    for bit in [b for b in (devices // 4, *bits) if 0 < b < devices // 2]:
        if bit not in held and (2 << len(held)) * piece_bytes <= HELD_BYTES:
            held.append(bit)
    held = held[:1] + held[:0:-1] if len(held) > 1 else held
    return held, [b for b in bits if b not in held]


def split3(value):
    high = value.astype(BF16)
    rest = value - high.astype(F32)
    middle = rest.astype(BF16)
    low = (rest - middle.astype(F32)).astype(BF16)
    return high, middle, low


def stack3(value):
    return jnp.concatenate(split3(value), axis=0)


def add_parts(value, outs):
    return value[:outs] + (value[outs : 2 * outs] + value[2 * outs :])


def bilinear_terms(sources, count, columns):
    place = lax.broadcasted_iota(jnp.int32, (count * 16, columns), 1)
    row = lax.broadcasted_iota(jnp.int32, (count * 16, columns), 0)
    term = place & 15
    source = jnp.full_like(place, -16)
    for k, which in enumerate(sources):
        source = jnp.where(term == k, which, source)
    return jnp.where(row == source * 16 + (place >> 4), 1.0, 0.0).astype(BF16)


def point_block(coordinates, tables, mixed, lhs_ref):
    _, _, constant_ref, pick_ref = tables
    curve, base = constant_ref[:, 0:1], constant_ref[:, 1:2]
    scale = scale_of(constant_ref[:, 2:3], curve, mixed)
    centred = coordinates - MIDDLE
    if mixed:
        real = centred.astype(F32)
        unit = real * (1.0 / LATTICE)
        large = jnp.floor(real * (1.0 / 256.0) + 0.5) * 256.0
        alone = curve * (unit * unit + unit) + base
        ones = jnp.ones(real.shape, BF16)
        sources = [*split3(alone), large.astype(BF16), (real - large).astype(BF16), ones]
        terms = lax.dot_general(
            jnp.concatenate(sources, axis=0),
            pick_ref[...],
            (((0,), (0,)), ((), ())),
            preferred_element_type=F32,
        ).astype(BF16)
        rows = terms.shape[0]
        for axis_number in range(mixed):
            lhs_ref[axis_number, :rows] = terms[:, axis_number * 128 : axis_number * 128 + 16]
    return (centred.astype(F32) * scale).T


def scale_of(shift, curve, mixed):
    row = lax.broadcasted_iota(jnp.int32, shift.shape, 0)
    return jnp.where(row < mixed, 2.0 * curve, 2.0 * shift) * (1.0 / LATTICE)


def kernel_tile(points, mixed, lhs_ref, tables, first, width):
    centre_ref, rhs_ref, constant_ref, _ = tables
    rows, dims = points.shape
    product = None
    columns = pl.ds(first, width)
    for axis_number in kernel_order(dims, mixed):
        own = slice(axis_number, axis_number + 1)
        kind = 0 if axis_number < mixed else 1
        centre = centre_ref[kind, own, columns]
        point = jnp.broadcast_to(points[:, axis_number : axis_number + 1], (rows, width))
        if axis_number < mixed:
            bilinear = jnp.dot(
                lhs_ref[axis_number, :rows],
                rhs_ref[pl.ds(axis_number * 16, 16), columns],
                preferred_element_type=F32,
            )
            factor = bilinear - jnp.maximum(point, centre)
        else:
            shift = jnp.broadcast_to(constant_ref[own, 2:3], (rows, width))
            floor = jnp.broadcast_to(constant_ref[own, 3:4], (rows, width))
            arm = jnp.abs(point - centre) - shift
            factor = arm * arm + floor
        product = factor if product is None else product * factor
    return product


def kernel_order(dims, mixed):
    kinds = [list(range(mixed)), list(range(mixed, dims))]
    order = []
    while kinds[0] or kinds[1]:
        first = len(kinds[0]) * (dims - mixed) >= len(kinds[1]) * mixed
        order.append(kinds[0 if kinds[0] and (first or not kinds[1]) else 1].pop(0))
    return order


def fill_kernel(rows, points, mixed, lhs_ref, tables, high_ref, low_ref, between=()):
    centres_all = tables[0].shape[2]
    width = min(WIDTH, centres_all)
    span = min(1024, centres_all)
    between = list(between)

    def part(base):
        for piece in range(span // width):
            if between:
                between.pop(0)()
            first = base + piece * width
            if not isinstance(first, int):
                first = pl.multiple_of(first, width)
            tile = kernel_tile(points, mixed, lhs_ref, tables, first, width)
            high = tile.astype(BF16)
            high_ref[rows, pl.ds(first, width)] = high
            low_ref[rows, pl.ds(first, width)] = (tile - high.astype(F32)).astype(BF16)

    if centres_all == span:
        part(0)
    else:
        while between:
            between.pop(0)()
        lax.fori_loop(0, centres_all // span, lambda i, _: part(i * span), None)
    while between:
        between.pop(0)()


def fetch(pairs, sems):
    copies = [pltpu.make_async_copy(src, dst, sems.at[i]) for i, (src, dst) in enumerate(pairs)]
    for copy in copies:
        copy.start()
    return copies


def modulo(value):
    turns = (value.astype(F32) * (1.0 / LATTICE)).astype(jnp.int32)
    rest = value - turns * LATTICE
    rest = jnp.where(rest < 0, rest + LATTICE, rest)
    return jnp.where(rest >= LATTICE, rest - LATTICE, rest)


def column_of(values_ref, dims, dtype):
    row = lax.broadcasted_iota(jnp.int32, (dims, 1), 0)
    column = jnp.zeros((dims, 1), dtype)
    for axis_number in range(dims):
        column = jnp.where(row == axis_number, values_ref[axis_number], column)
    return column


def centre_coordinates(order, generator_ref, dims, count):
    order_bits, cen_dev = order
    generator = column_of(generator_ref, dims, jnp.int32)
    place = lax.broadcasted_iota(jnp.int32, (1, count), 1)
    owner = jnp.zeros_like(place) + lax.axis_index("samp")
    for k, bit in enumerate(order_bits):
        owner = jnp.where((place & (cen_dev << k)) != 0, owner ^ bit, owner)
    column = owner * cen_dev + (place & (cen_dev - 1))
    upper = modulo(column * (generator >> 8))
    return modulo(upper * 256 + column * (generator & 255))


def begin(
    order, generator_hbm, weight_hbm, samples_hbm, piece_hbm, solution_hbm, residual_hbm, direction_hbm,
    sample_ref, piece_ref, own_state_ref, centre_ref, rhs_ref, constant_ref, pick_ref, own_points_ref,
    generator_ref, weight_ref, sems,
):
    outs = solution_hbm.shape[0]
    copies = fetch(
        [
            (generator_hbm, generator_ref),
            (weight_hbm, weight_ref),
            (samples_hbm, sample_ref),
            (piece_hbm, piece_ref),
            (solution_hbm, own_state_ref.at[pl.ds(0, outs)]),
            (residual_hbm, own_state_ref.at[pl.ds(outs, outs)]),
            (direction_hbm, own_state_ref.at[pl.ds(2 * outs, outs)]),
        ],
        sems,
    )
    _, dims, centres_all = centre_ref.shape
    place = lax.broadcasted_iota(jnp.int32, (6 * dims, 128), 1)
    row = lax.broadcasted_iota(jnp.int32, (6 * dims, 128), 0)
    source = jnp.full_like(place, -1000)
    for k, which in enumerate((0, 1, 2, 5, 5, 5, 3, 3, 3, 4, 4, 4)):
        source = jnp.where(place == k, which * dims, source)
    for axis_number in range(dims):
        columns = slice(axis_number * 128, (axis_number + 1) * 128)
        pick_ref[:, columns] = jnp.where(row == source + axis_number, 1.0, 0.0).astype(BF16)
    pick = bilinear_terms((0, 0, 0, 1, 2, 3, 4, 5, 6, 4, 5, 6), 7, 16 * dims)

    copies[0].wait()
    copies[1].wait()
    curves = [math.pi * math.pi * 0.75**weight for weight in range(8)]
    weight = column_of(weight_ref, dims, jnp.int32)
    shift = jnp.full((dims, 1), 0.5 * math.sqrt(curves[7]), F32)
    for k in range(7):
        shift = jnp.where(weight == k, 0.5 * math.sqrt(curves[k]), shift)
    curve = 4.0 * shift * shift
    floor = 1.0 - curve * (1.0 / 12.0)
    lane = lax.broadcasted_iota(jnp.int32, (dims, 128), 1)
    table = jnp.where(lane == 0, curve, jnp.where(lane == 1, floor + 0.25 * curve, 0.0))
    constant_ref[...] = jnp.where(lane == 2, shift, jnp.where(lane == 3, floor, table))

    centre = centre_coordinates(order, generator_ref, dims, centres_all)
    own_points_ref[...] = centre[:, :128]
    real = (centre - MIDDLE).astype(F32)
    for kind, mixed in ((0, dims), (1, 0)):
        centre_ref[kind] = real * scale_of(shift, curve, mixed)
    unit = real * (1.0 / LATTICE)
    alone = curve * (unit * unit + unit)
    slope = (-2.0 / LATTICE) * curve * unit
    ones = jnp.ones(real.shape, BF16)
    sources = jnp.concatenate([ones, *split3(alone), *split3(slope)], axis=0)
    rhs_ref[...] = lax.dot_general(
        pick, sources, (((0,), (0,)), ((), ())), preferred_element_type=F32
    ).astype(BF16)
    for copy in copies[2:]:
        copy.wait()


def store_rows(
    first_row, mixed, sample_ref, centre_ref, rhs_ref, constant_ref, pick_ref, passed_ref,
    high_ref, low_ref, handed_ref, lhs_ref,
):
    tables = (centre_ref, rhs_ref, constant_ref, pick_ref)
    handed_ref[...] = passed_ref[...]
    step_rows = lhs_ref.shape[1]

    def step(i, _):
        rows = pl.ds(pl.multiple_of(i * step_rows, step_rows), step_rows)
        columns = pl.ds(pl.multiple_of(first_row + i * step_rows, 128), step_rows)
        points = point_block(sample_ref[:, columns], tables, mixed, lhs_ref)
        fill_kernel(rows, points, mixed, lhs_ref, tables, high_ref, low_ref)

    lax.fori_loop(0, high_ref.shape[0] // step_rows, step, None)


def kernel_rows(passed, first_row, rows, tables):
    _, dims, centres_all = tables[1].shape
    kept = jax.ShapeDtypeStruct((rows, centres_all), BF16)
    high, low, handed = pl.pallas_call(
        functools.partial(store_rows, first_row, STORED_MIXED),
        out_shape=[kept, kept, jax.ShapeDtypeStruct(passed.shape, passed.dtype)],
        scratch_shapes=[pltpu.VMEM((max(1, STORED_MIXED), min(256, rows), 16), BF16)],
        compiler_params=pltpu.CompilerParams(vmem_limit_bytes=10 << 20),
        cost_estimate=pl.CostEstimate(
            flops=6 * dims * rows * centres_all,
            bytes_accessed=4 * rows * centres_all,
            transcendentals=0,
        ),
        name="kernel_rows",
    )(*tables, passed)
    return (high, low), handed


def in_hbm(*values):
    return [pltpu.with_memory_space_constraint(value, pltpu.HBM) for value in values]


def apply_kernel(high, low, coefficients, outs):
    contract = (((1,), (1,)), ((), ()))
    fitted = lax.dot_general(coefficients, high, contract, preferred_element_type=F32)
    fitted = fitted + lax.dot_general(coefficients, low, contract, preferred_element_type=F32)
    return add_parts(fitted, outs)


def back_products(high_ref, low_ref, coef_ref, outs):
    result = {}

    def there():
        result["parts"] = stack3(apply_kernel(high_ref[...], low_ref[...], coef_ref[...], outs))

    def back():
        parts = result["parts"]
        total = jnp.dot(parts, high_ref[...], preferred_element_type=F32)
        result["sum"] = total + jnp.dot(parts, low_ref[...], preferred_element_type=F32)

    return there, back, result


def products(
    outs, stored, coef_ref, sample_ref, centre_ref, rhs_ref, constant_ref, pick_ref, own_points_ref, *refs
):
    stored_refs, refs = refs[: 2 * len(stored)], refs[2 * len(stored) :]
    *backward_refs, own_out_ref = refs[:3]
    lhs_ref, parts_ref, sum_ref, *made = refs[3:]
    tables = (centre_ref, rhs_ref, constant_ref, pick_ref)
    mixed = PRODUCTS_MIXED
    own_rows = own_out_ref.shape[1]
    block_rows = made[0].shape[0]
    first_row = sum(stored)
    steps = (sample_ref.shape[1] - first_row) // block_rows

    parts_ref[...] = stack3(coef_ref[...])
    sum_ref[...] = jnp.zeros_like(sum_ref)
    last_high, last_low = made[2:]
    last_high[...] = jnp.zeros_like(last_high)
    last_low[...] = jnp.zeros_like(last_low)
    own_high, own_low = made[:2]
    rows = pl.ds(0, own_rows)
    own_points = point_block(own_points_ref[:, :own_rows], tables, mixed, lhs_ref)
    fill_kernel(rows, own_points, mixed, lhs_ref, tables, own_high, own_low)
    own_out_ref[...] = apply_kernel(own_high[rows], own_low[rows], parts_ref[...], outs)

    def half_step(i, now, before, given):
        work = [back_products(*before, parts_ref, outs)]
        if given:
            work.append(back_products(*given, parts_ref, outs))
        between = [there for there, _, _ in work] + [back for _, back, _ in work]
        columns = pl.ds(pl.multiple_of(first_row + i * block_rows, 128), block_rows)
        points = point_block(sample_ref[:, columns], tables, mixed, lhs_ref)
        fill_kernel(pl.ds(0, block_rows), points, mixed, lhs_ref, tables, *now, between)
        for _, _, result in work:
            sum_ref[...] += result["sum"]

    pairs = [stored_refs[2 * i : 2 * i + 2] for i in range(len(stored))]
    if pairs:
        for i in range(steps):
            now, before = (made[:2], made[2:]) if i % 2 == 0 else (made[2:], made[:2])
            half_step(i, now, before, pairs[i] if i < len(pairs) else None)
    else:

        def step(i, _):
            half_step(2 * i, made[:2], made[2:], None)
            half_step(2 * i + 1, made[2:], made[:2], None)

        lax.fori_loop(0, steps // 2, step, None)
    there, back, result = back_products(*made[2:], parts_ref, outs)
    there()
    back()
    last = sum_ref[...] + result["sum"]
    last = add_parts(last, outs)
    width = last.shape[1] // len(backward_refs)
    for i, backward_ref in enumerate(backward_refs):
        backward_ref[...] = last[:, i * width : (i + 1) * width]


def apply_products(store, coefficients, own_points, block_rows, tables):
    outs, centres_all = coefficients.shape
    dims, samples_dev = tables[0].shape
    own_rows = own_points.shape[1]
    stored = tuple(high.shape[0] for high, _ in store)
    made = pltpu.VMEM((block_rows, centres_all), BF16)
    rows = samples_dev - sum(stored)
    half = jax.ShapeDtypeStruct((outs, centres_all // 2), F32)
    return pl.pallas_call(
        functools.partial(products, outs, stored),
        out_shape=[half, half, jax.ShapeDtypeStruct((outs, own_rows), F32)],
        scratch_shapes=[
            pltpu.VMEM((max(1, PRODUCTS_MIXED), block_rows, 16), BF16),
            pltpu.VMEM((3 * outs, centres_all), BF16),
            pltpu.VMEM((3 * outs, centres_all), F32),
            *[made] * 4,
        ],
        compiler_params=pltpu.CompilerParams(
            vmem_limit_bytes=(14 << 20) + 16 * block_rows * centres_all
        ),
        cost_estimate=pl.CostEstimate(
            flops=6 * dims * rows * centres_all,
            bytes_accessed=4 * sum(stored) * centres_all,
            transcendentals=0,
        ),
        name="products",
    )(coefficients, *tables, own_points, *[part for pair in store for part in pair])


def row_products(outs, count, state_ref, *refs):
    coef_ref, parts_ref = refs[count:]
    state = stack3(state_ref[:outs])
    cen_dev = refs[0].shape[0]
    for i, piece_ref in enumerate(refs[:count]):
        rows = slice(i * cen_dev, (i + 1) * cen_dev)
        for k, part in enumerate(split3(piece_ref[...])):
            parts_ref[k, rows] = part
    total = None
    for k in range(3):
        term = lax.dot_general(
            state, parts_ref[k], (((1,), (1,)), ((), ())), preferred_element_type=F32
        )
        total = term if total is None else total + term
    coef_ref[...] = add_parts(total, outs)


def image_rows(scale_total, ridge, kept_ref, came_ref, own_ref, *refs):
    *part_refs, image_ref = refs
    outs, cen_dev = own_ref.shape
    applied = (kept_ref[...] + came_ref[...]) * (1.0 / scale_total)
    own = ridge * own_ref[...]
    rest = applied.shape[1] - cen_dev
    if rest:
        own = jnp.concatenate([own, jnp.zeros((outs, rest), F32)], axis=1)
    rows = stack3(applied + own)
    total, first = None, 0
    for part_ref in part_refs:
        some = rows[:, first : first + part_ref.shape[1]]
        first += part_ref.shape[1]
        for k in range(3):
            term = jnp.dot(some, part_ref[k], preferred_element_type=F32)
            total = term if total is None else total + term
    image_ref[...] = add_parts(total, outs)


def finish(
    image_ref, more_ref, state_ref, own_ref, new_solution_ref, new_residual_ref, new_direction_ref, total_ref
):
    outs, cen_dev = new_solution_ref.shape
    image = image_ref[...] + more_ref[...]
    total_ref[...] = image
    residual_full = state_ref[outs:]
    norm_old = jnp.sum(residual_full * residual_full, axis=1, keepdims=True)
    curvature = jnp.sum(state_ref[:outs] * image, axis=1, keepdims=True)
    step_length = norm_old / curvature
    next_full = residual_full - step_length * image
    norm_new = jnp.sum(next_full * next_full, axis=1, keepdims=True)
    index = lax.axis_index("samp")
    share = max(1, 128 // cen_dev)
    first = pl.multiple_of((index // share) * 128, 128)
    wide = total_ref[:, pl.ds(first, 128)]
    own_image = wide[:, :cen_dev]
    for k in range(1, share):
        here = lax.rem(index, share) == k
        own_image = jnp.where(here, wide[:, k * cen_dev : (k + 1) * cen_dev], own_image)
    direction = own_ref[2 * outs :]
    new_solution_ref[...] = own_ref[:outs] + step_length * direction
    new_residual = own_ref[outs : 2 * outs] - step_length * own_image
    new_residual_ref[...] = new_residual
    new_direction_ref[...] = new_residual + (norm_new / norm_old) * direction


def body(samples, generator, weight_index, preconditioner, solution, residual, direction):
    devices = lax.axis_size("samp")
    index = lax.axis_index("samp")
    cen_dev, centres_all = preconditioner.shape
    samples_dev = samples.shape[1]
    outs = direction.shape[0]
    held, others = plan(devices, 4 * cen_dev * centres_all)

    order = ((*held, *others), cen_dev)
    dims = samples.shape[0]
    sample_copy, piece_copy, own_state, *tables = pl.pallas_call(
        functools.partial(begin, order),
        in_specs=[HBM] * 7,
        out_shape=[
            jax.ShapeDtypeStruct(samples.shape, jnp.int32),
            jax.ShapeDtypeStruct(preconditioner.shape, F32),
            jax.ShapeDtypeStruct((3 * outs, cen_dev), F32),
            jax.ShapeDtypeStruct((2, dims, centres_all), F32),
            jax.ShapeDtypeStruct((16 * dims, centres_all), BF16),
            jax.ShapeDtypeStruct((dims, 128), F32),
            jax.ShapeDtypeStruct((6 * dims, 128 * dims), BF16),
            jax.ShapeDtypeStruct((dims, 128), jnp.int32),
        ],
        scratch_shapes=[
            pltpu.SMEM((dims,), jnp.int32),
            pltpu.SMEM((dims,), jnp.int32),
            pltpu.SemaphoreType.DMA((7,)),
        ],
        compiler_params=pltpu.CompilerParams(vmem_limit_bytes=(6 << 20) + 1200 * centres_all),
        name="begin",
    )(*in_hbm(generator, weight_index, samples, preconditioner, solution, residual, direction))
    own_points = tables.pop()[:, :cen_dev]
    tables = (sample_copy, *tables)

    half = samples_dev // 2
    use_store = 4 * half * centres_all <= STORE_BYTES
    store, filled = [], 0

    def fill(rows, passed):
        nonlocal filled
        rows = min(rows, half - filled) if use_store else 0
        if rows == 0:
            return passed
        made, handed = kernel_rows(passed, filled, rows, tables)
        store.append(made)
        filled += rows
        return handed

    pieces = [preconditioner]
    early = [swap(preconditioner, bit, devices) for bit in held[:2]]
    pieces += early[:1]
    if len(early) > 1:
        pieces += [early[1], swap(early[0], held[1], devices)]
    bit = 1
    state = None
    while bit < devices:
        upper = (index & bit) != 0
        if state is None:
            mine = [direction, residual]
            other = [swap(direction, bit, devices), swap(residual, bit, devices)]
            joined = [jnp.concatenate(pair, axis=1) for pair in zip(other, mine)]
            turned = [jnp.concatenate(pair, axis=1) for pair in zip(mine, other)]
            state = jnp.where(upper, jnp.concatenate(joined), jnp.concatenate(turned))
        else:
            other = swap(state, bit, devices)
            mine = fill(256, state)
            state = jnp.where(
                upper,
                jnp.concatenate([other, mine], axis=1),
                jnp.concatenate([mine, other], axis=1),
            )
        bit *= 2

    def coefficients_of(group):
        rows = len(group) * cen_dev
        return pl.pallas_call(
            functools.partial(row_products, outs, len(group)),
            out_shape=[
                jax.ShapeDtypeStruct((outs, rows), F32),
                jax.ShapeDtypeStruct((3, rows, centres_all), BF16),
            ],
            compiler_params=pltpu.CompilerParams(
                vmem_limit_bytes=(4 << 20) + 24 * rows * centres_all
            ),
            name="row_products",
        )(state, *group)

    groups = [[piece_copy, *pieces[1:]]]
    for bit in held[2:]:
        groups.append([swap(p, bit, devices) for p in [*pieces, *sum(groups[1:], [])]])
    made = [coefficients_of(group) for group in groups]
    coefficients = jnp.concatenate([m[0] for m in made], axis=1)
    parts = [m[1] for m in made]
    for bit in others:
        other = swap(coefficients, bit, devices)
        mine = fill(256, coefficients)
        coefficients = jnp.concatenate([mine, other], axis=1)
    coefficients = fill(half, coefficients)

    kept, sent, kernel_products = apply_products(store, coefficients, own_points, 256, tables)
    for bit in reversed(others):
        came = swap(sent, bit, devices)
        if bit != others[0]:
            summed = kept + came
            width = summed.shape[1] // 2
            kept, sent = summed[:, :width], summed[:, width:]
    scale_total = float(samples_dev * devices) * float(centres_all)
    image = pl.pallas_call(
        functools.partial(image_rows, scale_total, ridge_weight / centres_all),
        out_shape=jax.ShapeDtypeStruct((outs, centres_all), F32),
        compiler_params=pltpu.CompilerParams(
            vmem_limit_bytes=(4 << 20) + 8 * kept.shape[1] * centres_all
        ),
        name="image_rows",
    )(kept, came, kernel_products, *parts)
    bit = 1
    while 2 * bit < devices:
        image = image + swap(image, bit, devices)
        bit *= 2
    more = swap(image, bit, devices)
    own = jax.ShapeDtypeStruct(solution.shape, F32)
    return pl.pallas_call(
        finish,
        out_shape=[own, own, own],
        scratch_shapes=[pltpu.VMEM((outs, centres_all), F32)],
        compiler_params=pltpu.CompilerParams(vmem_limit_bytes=(2 << 20) + 512 * centres_all),
        name="finish",
    )(image, more, state, own_state)


def solution(mesh):
    placed = (
        P("groups", "samp"),
        P(),
        P(),
        P("samp", None),
        P("groups", "samp"),
        P("groups", "samp"),
        P("groups", "samp"),
    )
    return jax.shard_map(
        body,
        mesh=mesh,
        in_specs=placed,
        out_specs=(P("groups", "samp"), P("groups", "samp"), P("groups", "samp")),
        check_vma=False,
    )
```

```python
import functools
import math

import jax
import jax.numpy as jnp
from jax import lax
from jax.experimental import pallas as pl
from jax.experimental.pallas import tpu as pltpu
from jax.sharding import PartitionSpec as P

LATTICE = 65521
MIDDLE = LATTICE // 2

ridge_weight = 0.25
STORE_BYTES = 12 << 20
HELD_BYTES = 16 << 20
WIDTH = 256
STORED_MIXED = 16
PRODUCTS_MIXED = 10
VMEM = pl.BlockSpec(memory_space=pltpu.VMEM)
FREE = pl.BlockSpec(memory_space=pl.ANY)
HBM = pl.BlockSpec(memory_space=pltpu.HBM)
SMEM = pl.BlockSpec(memory_space=pltpu.SMEM)
F32 = jnp.float32
BF16 = jnp.bfloat16


def swap(value, bit, devices):
    return lax.ppermute(value, "samp", [(i, i ^ bit) for i in range(devices)])


def plan(devices, piece_bytes):
    bits = [1 << k for k in range(devices.bit_length() - 1)]
    held = []
    for bit in [b for b in (devices // 4, *bits) if 0 < b < devices // 2]:
        if bit not in held and (2 << len(held)) * piece_bytes <= HELD_BYTES:
            held.append(bit)
    held = held[:1] + held[:0:-1] if len(held) > 1 else held
    return held, [b for b in bits if b not in held]


def split3(value):
    high = value.astype(BF16)
    rest = value - high.astype(F32)
    middle = rest.astype(BF16)
    low = (rest - middle.astype(F32)).astype(BF16)
    return high, middle, low


def stack3(value):
    return jnp.concatenate(split3(value), axis=0)


def add_parts(value, outs):
    return value[:outs] + (value[outs : 2 * outs] + value[2 * outs :])


def bilinear_terms(sources, count, columns):
    place = lax.broadcasted_iota(jnp.int32, (count * 16, columns), 1)
    row = lax.broadcasted_iota(jnp.int32, (count * 16, columns), 0)
    term = place & 15
    source = jnp.full_like(place, -16)
    for k, which in enumerate(sources):
        source = jnp.where(term == k, which, source)
    return jnp.where(row == source * 16 + (place >> 4), 1.0, 0.0).astype(BF16)


def point_block(coordinates, tables, mixed, lhs_ref):
    _, _, constant_ref, pick_ref = tables
    curve, base = constant_ref[:, 0:1], constant_ref[:, 1:2]
    scale = scale_of(constant_ref[:, 2:3], curve, mixed)
    centred = coordinates - MIDDLE
    if mixed:
        real = centred.astype(F32)
        unit = real * (1.0 / LATTICE)
        large = jnp.floor(real * (1.0 / 256.0) + 0.5) * 256.0
        alone = curve * (unit * unit + unit) + base
        ones = jnp.ones(real.shape, BF16)
        sources = [*split3(alone), large.astype(BF16), (real - large).astype(BF16), ones]
        terms = lax.dot_general(
            jnp.concatenate(sources, axis=0),
            pick_ref[...],
            (((0,), (0,)), ((), ())),
            preferred_element_type=F32,
        ).astype(BF16)
        rows = terms.shape[0]
        for axis_number in range(mixed):
            lhs_ref[axis_number, :rows] = terms[:, axis_number * 128 : axis_number * 128 + 16]
    return (centred.astype(F32) * scale).T


def scale_of(shift, curve, mixed):
    row = lax.broadcasted_iota(jnp.int32, shift.shape, 0)
    return jnp.where(row < mixed, 2.0 * curve, 2.0 * shift) * (1.0 / LATTICE)


def kernel_tile(points, mixed, lhs_ref, tables, first, width):
    centre_ref, rhs_ref, constant_ref, _ = tables
    rows, dims = points.shape
    product = None
    columns = pl.ds(first, width)
    for axis_number in kernel_order(dims, mixed):
        own = slice(axis_number, axis_number + 1)
        kind = 0 if axis_number < mixed else 1
        centre = centre_ref[kind, own, columns]
        point = jnp.broadcast_to(points[:, axis_number : axis_number + 1], (rows, width))
        if axis_number < mixed:
            bilinear = jnp.dot(
                lhs_ref[axis_number, :rows],
                rhs_ref[pl.ds(axis_number * 16, 16), columns],
                preferred_element_type=F32,
            )
            factor = bilinear - jnp.maximum(point, centre)
        else:
            shift = jnp.broadcast_to(constant_ref[own, 2:3], (rows, width))
            floor = jnp.broadcast_to(constant_ref[own, 3:4], (rows, width))
            arm = jnp.abs(point - centre) - shift
            factor = arm * arm + floor
        product = factor if product is None else product * factor
    return product


def kernel_order(dims, mixed):
    kinds = [list(range(mixed)), list(range(mixed, dims))]
    order = []
    while kinds[0] or kinds[1]:
        first = len(kinds[0]) * (dims - mixed) >= len(kinds[1]) * mixed
        order.append(kinds[0 if kinds[0] and (first or not kinds[1]) else 1].pop(0))
    return order


def fill_kernel(rows, points, mixed, lhs_ref, tables, high_ref, low_ref, between=()):
    centres_all = tables[0].shape[2]
    width = min(WIDTH, centres_all)
    span = min(1024, centres_all)
    between = list(between)

    def part(base):
        for piece in range(span // width):
            if between:
                between.pop(0)()
            first = base + piece * width
            if not isinstance(first, int):
                first = pl.multiple_of(first, width)
            tile = kernel_tile(points, mixed, lhs_ref, tables, first, width)
            high = tile.astype(BF16)
            high_ref[rows, pl.ds(first, width)] = high
            low_ref[rows, pl.ds(first, width)] = (tile - high.astype(F32)).astype(BF16)

    if centres_all == span:
        part(0)
    else:
        while between:
            between.pop(0)()
        lax.fori_loop(0, centres_all // span, lambda i, _: part(i * span), None)
    while between:
        between.pop(0)()


def fetch(pairs, sems):
    copies = [pltpu.make_async_copy(src, dst, sems.at[i]) for i, (src, dst) in enumerate(pairs)]
    for copy in copies:
        copy.start()
    return copies


def modulo(value):
    turns = (value.astype(F32) * (1.0 / LATTICE)).astype(jnp.int32)
    rest = value - turns * LATTICE
    rest = jnp.where(rest < 0, rest + LATTICE, rest)
    return jnp.where(rest >= LATTICE, rest - LATTICE, rest)


def column_of(values_ref, dims, dtype):
    row = lax.broadcasted_iota(jnp.int32, (dims, 1), 0)
    column = jnp.zeros((dims, 1), dtype)
    for axis_number in range(dims):
        column = jnp.where(row == axis_number, values_ref[axis_number], column)
    return column


def centre_coordinates(order, generator_ref, dims, count):
    order_bits, cen_dev = order
    generator = column_of(generator_ref, dims, jnp.int32)
    place = lax.broadcasted_iota(jnp.int32, (1, count), 1)
    owner = jnp.zeros_like(place) + lax.axis_index("samp")
    for k, bit in enumerate(order_bits):
        owner = jnp.where((place & (cen_dev << k)) != 0, owner ^ bit, owner)
    column = owner * cen_dev + (place & (cen_dev - 1))
    upper = modulo(column * (generator >> 8))
    return modulo(upper * 256 + column * (generator & 255))


def begin(
    order, generator_hbm, weight_hbm, samples_hbm, solution_hbm, residual_hbm, direction_hbm,
    sample_ref, solution_ref, residual_ref, direction_ref, centre_ref, rhs_ref, constant_ref, pick_ref, own_points_ref,
    generator_ref, weight_ref, sems,
):
    copies = fetch(
        [
            (generator_hbm, generator_ref),
            (weight_hbm, weight_ref),
            (samples_hbm, sample_ref),
            (solution_hbm, solution_ref),
            (residual_hbm, residual_ref),
            (direction_hbm, direction_ref),
        ],
        sems,
    )
    _, dims, centres_all = centre_ref.shape
    place = lax.broadcasted_iota(jnp.int32, (6 * dims, 128), 1)
    row = lax.broadcasted_iota(jnp.int32, (6 * dims, 128), 0)
    source = jnp.full_like(place, -1000)
    for k, which in enumerate((0, 1, 2, 5, 5, 5, 3, 3, 3, 4, 4, 4)):
        source = jnp.where(place == k, which * dims, source)
    for axis_number in range(dims):
        columns = slice(axis_number * 128, (axis_number + 1) * 128)
        pick_ref[:, columns] = jnp.where(row == source + axis_number, 1.0, 0.0).astype(BF16)
    pick = bilinear_terms((0, 0, 0, 1, 2, 3, 4, 5, 6, 4, 5, 6), 7, 16 * dims)

    copies[0].wait()
    copies[1].wait()
    curves = [math.pi * math.pi * 0.75**weight for weight in range(8)]
    weight = column_of(weight_ref, dims, jnp.int32)
    shift = jnp.full((dims, 1), 0.5 * math.sqrt(curves[7]), F32)
    for k in range(7):
        shift = jnp.where(weight == k, 0.5 * math.sqrt(curves[k]), shift)
    curve = 4.0 * shift * shift
    floor = 1.0 - curve * (1.0 / 12.0)
    lane = lax.broadcasted_iota(jnp.int32, (dims, 128), 1)
    table = jnp.where(lane == 0, curve, jnp.where(lane == 1, floor + 0.25 * curve, 0.0))
    constant_ref[...] = jnp.where(lane == 2, shift, jnp.where(lane == 3, floor, table))

    centre = centre_coordinates(order, generator_ref, dims, centres_all)
    own_points_ref[...] = centre[:, :128]
    real = (centre - MIDDLE).astype(F32)
    for kind, mixed in ((0, dims), (1, 0)):
        centre_ref[kind] = real * scale_of(shift, curve, mixed)
    unit = real * (1.0 / LATTICE)
    alone = curve * (unit * unit + unit)
    slope = (-2.0 / LATTICE) * curve * unit
    ones = jnp.ones(real.shape, BF16)
    sources = jnp.concatenate([ones, *split3(alone), *split3(slope)], axis=0)
    rhs_ref[...] = lax.dot_general(
        pick, sources, (((0,), (0,)), ((), ())), preferred_element_type=F32
    ).astype(BF16)
    for copy in copies[2:]:
        copy.wait()


def store_rows(
    first_row, mixed, sample_ref, centre_ref, rhs_ref, constant_ref, pick_ref, passed_ref,
    high_ref, low_ref, handed_ref, lhs_ref,
):
    tables = (centre_ref, rhs_ref, constant_ref, pick_ref)
    handed_ref[...] = passed_ref[...]
    step_rows = lhs_ref.shape[1]

    def step(i, _):
        rows = pl.ds(pl.multiple_of(i * step_rows, step_rows), step_rows)
        columns = pl.ds(pl.multiple_of(first_row + i * step_rows, 128), step_rows)
        points = point_block(sample_ref[:, columns], tables, mixed, lhs_ref)
        fill_kernel(rows, points, mixed, lhs_ref, tables, high_ref, low_ref)

    lax.fori_loop(0, high_ref.shape[0] // step_rows, step, None)


def kernel_rows(passed, first_row, rows, tables):
    _, dims, centres_all = tables[1].shape
    kept = jax.ShapeDtypeStruct((rows, centres_all), BF16)
    high, low, handed = pl.pallas_call(
        functools.partial(store_rows, first_row, STORED_MIXED),
        out_shape=[kept, kept, jax.ShapeDtypeStruct(passed.shape, passed.dtype)],
        scratch_shapes=[pltpu.VMEM((max(1, STORED_MIXED), min(256, rows), 16), BF16)],
        compiler_params=pltpu.CompilerParams(vmem_limit_bytes=10 << 20),
        cost_estimate=pl.CostEstimate(
            flops=6 * dims * rows * centres_all,
            bytes_accessed=4 * rows * centres_all,
            transcendentals=0,
        ),
        name="kernel_rows",
    )(*tables, passed)
    return (high, low), handed


def in_hbm(*values):
    return [pltpu.with_memory_space_constraint(value, pltpu.HBM) for value in values]


def apply_kernel(high, low, coefficients, outs):
    contract = (((1,), (1,)), ((), ()))
    fitted = lax.dot_general(coefficients, high, contract, preferred_element_type=F32)
    fitted = fitted + lax.dot_general(coefficients, low, contract, preferred_element_type=F32)
    return add_parts(fitted, outs)


def back_products(high_ref, low_ref, coef_ref, outs):
    result = {}

    def there():
        result["parts"] = stack3(apply_kernel(high_ref[...], low_ref[...], coef_ref[...], outs))

    def back():
        parts = result["parts"]
        total = jnp.dot(parts, high_ref[...], preferred_element_type=F32)
        result["sum"] = total + jnp.dot(parts, low_ref[...], preferred_element_type=F32)

    return there, back, result


def products(
    outs, stored, coef_ref, sample_ref, centre_ref, rhs_ref, constant_ref, pick_ref, own_points_ref, *refs
):
    stored_refs, refs = refs[: 2 * len(stored)], refs[2 * len(stored) :]
    *backward_refs, own_out_ref = refs[:3]
    lhs_ref, parts_ref, sum_ref, *made = refs[3:]
    tables = (centre_ref, rhs_ref, constant_ref, pick_ref)
    mixed = PRODUCTS_MIXED
    own_rows = own_out_ref.shape[1]
    block_rows = made[0].shape[0]
    first_row = sum(stored)
    steps = (sample_ref.shape[1] - first_row) // block_rows

    parts_ref[...] = stack3(coef_ref[...])
    sum_ref[...] = jnp.zeros_like(sum_ref)
    last_high, last_low = made[2:]
    last_high[...] = jnp.zeros_like(last_high)
    last_low[...] = jnp.zeros_like(last_low)
    own_high, own_low = made[:2]
    rows = pl.ds(0, own_rows)
    own_points = point_block(own_points_ref[:, :own_rows], tables, mixed, lhs_ref)
    fill_kernel(rows, own_points, mixed, lhs_ref, tables, own_high, own_low)
    own_out_ref[...] = apply_kernel(own_high[rows], own_low[rows], parts_ref[...], outs)

    def half_step(i, now, before, given):
        work = [back_products(*before, parts_ref, outs)]
        if given:
            work.append(back_products(*given, parts_ref, outs))
        between = [there for there, _, _ in work] + [back for _, back, _ in work]
        columns = pl.ds(pl.multiple_of(first_row + i * block_rows, 128), block_rows)
        points = point_block(sample_ref[:, columns], tables, mixed, lhs_ref)
        fill_kernel(pl.ds(0, block_rows), points, mixed, lhs_ref, tables, *now, between)
        for _, _, result in work:
            sum_ref[...] += result["sum"]

    pairs = [stored_refs[2 * i : 2 * i + 2] for i in range(len(stored))]
    if pairs:
        for i in range(steps):
            now, before = (made[:2], made[2:]) if i % 2 == 0 else (made[2:], made[:2])
            half_step(i, now, before, pairs[i] if i < len(pairs) else None)
    else:

        def step(i, _):
            half_step(2 * i, made[:2], made[2:], None)
            half_step(2 * i + 1, made[2:], made[:2], None)

        lax.fori_loop(0, steps // 2, step, None)
    there, back, result = back_products(*made[2:], parts_ref, outs)
    there()
    back()
    last = sum_ref[...] + result["sum"]
    last = add_parts(last, outs)
    width = last.shape[1] // len(backward_refs)
    for i, backward_ref in enumerate(backward_refs):
        backward_ref[...] = last[:, i * width : (i + 1) * width]


def apply_products(store, coefficients, own_points, block_rows, tables):
    outs, centres_all = coefficients.shape
    dims, samples_dev = tables[0].shape
    own_rows = own_points.shape[1]
    stored = tuple(high.shape[0] for high, _ in store)
    made = pltpu.VMEM((block_rows, centres_all), BF16)
    rows = samples_dev - sum(stored)
    half = jax.ShapeDtypeStruct((outs, centres_all // 2), F32)
    return pl.pallas_call(
        functools.partial(products, outs, stored),
        out_shape=[half, half, jax.ShapeDtypeStruct((outs, own_rows), F32)],
        scratch_shapes=[
            pltpu.VMEM((max(1, PRODUCTS_MIXED), block_rows, 16), BF16),
            pltpu.VMEM((3 * outs, centres_all), BF16),
            pltpu.VMEM((3 * outs, centres_all), F32),
            *[made] * 4,
        ],
        compiler_params=pltpu.CompilerParams(
            vmem_limit_bytes=(14 << 20) + 16 * block_rows * centres_all
        ),
        cost_estimate=pl.CostEstimate(
            flops=6 * dims * rows * centres_all,
            bytes_accessed=4 * sum(stored) * centres_all,
            transcendentals=0,
        ),
        name="products",
    )(coefficients, *tables, own_points, *[part for pair in store for part in pair])


def join(bit, count, riders, *refs):
    mine_refs, other_refs, joined_ref = refs[:count], refs[count : 2 * count], refs[2 * count + riders]
    width = mine_refs[0].shape[1]
    upper = (lax.axis_index("samp") & bit) != 0
    first = 0
    for mine_ref, other_ref in zip(mine_refs, other_refs):
        rows = slice(first, first + mine_ref.shape[0])
        first += mine_ref.shape[0]
        mine, other = mine_ref[...], other_ref[...]
        joined_ref[rows, :width] = jnp.where(upper, other, mine)
        joined_ref[rows, width:] = jnp.where(upper, mine, other)


def joined(bit, mine, other, riders=()):
    rows = sum(value.shape[0] for value in mine)
    count = len(mine)
    like = [jax.ShapeDtypeStruct(value.shape, value.dtype) for value in riders]
    value, *riders = pl.pallas_call(
        functools.partial(join, bit, count, len(riders)),
        in_specs=[*[VMEM] * (2 * count), *[FREE] * len(riders)],
        out_specs=[VMEM, *[FREE] * len(riders)],
        out_shape=[jax.ShapeDtypeStruct((rows, 2 * mine[0].shape[1]), F32), *like],
        input_output_aliases={2 * count + i: 1 + i for i in range(len(riders))},
        compiler_params=pltpu.CompilerParams(vmem_limit_bytes=4 << 20),
        name="join",
    )(*mine, *other, *riders)
    return value, riders


def row_products(outs, count, state_ref, *refs):
    coef_ref, parts_ref = refs[count:]
    state = stack3(state_ref[:outs])
    cen_dev = refs[0].shape[0]
    for i, piece_ref in enumerate(refs[:count]):
        rows = slice(i * cen_dev, (i + 1) * cen_dev)
        for k, part in enumerate(split3(piece_ref[...])):
            parts_ref[k, rows] = part
    total = None
    for k in range(3):
        term = lax.dot_general(
            state, parts_ref[k], (((1,), (1,)), ((), ())), preferred_element_type=F32
        )
        total = term if total is None else total + term
    coef_ref[...] = add_parts(total, outs)


def image_rows(scale_total, ridge, kept_ref, came_ref, own_ref, *refs):
    *part_refs, image_ref = refs
    outs, cen_dev = own_ref.shape
    applied = (kept_ref[...] + came_ref[...]) * (1.0 / scale_total)
    own = ridge * own_ref[...]
    rest = applied.shape[1] - cen_dev
    if rest:
        own = jnp.concatenate([own, jnp.zeros((outs, rest), F32)], axis=1)
    rows = stack3(applied + own)
    total, first = None, 0
    for part_ref in part_refs:
        some = rows[:, first : first + part_ref.shape[1]]
        first += part_ref.shape[1]
        for k in range(3):
            term = jnp.dot(some, part_ref[k], preferred_element_type=F32)
            total = term if total is None else total + term
    image_ref[...] = add_parts(total, outs)


def finish(
    image_ref, more_ref, state_ref, solution_ref, residual_ref, direction_ref, new_solution_ref, new_residual_ref, new_direction_ref, total_ref
):
    outs, cen_dev = new_solution_ref.shape
    image = image_ref[...] + more_ref[...]
    total_ref[...] = image
    residual_full = state_ref[outs:]
    norm_old = jnp.sum(residual_full * residual_full, axis=1, keepdims=True)
    curvature = jnp.sum(state_ref[:outs] * image, axis=1, keepdims=True)
    step_length = norm_old / curvature
    next_full = residual_full - step_length * image
    norm_new = jnp.sum(next_full * next_full, axis=1, keepdims=True)
    index = lax.axis_index("samp")
    share = max(1, 128 // cen_dev)
    first = pl.multiple_of((index // share) * 128, 128)
    wide = total_ref[:, pl.ds(first, 128)]
    own_image = wide[:, :cen_dev]
    for k in range(1, share):
        here = lax.rem(index, share) == k
        own_image = jnp.where(here, wide[:, k * cen_dev : (k + 1) * cen_dev], own_image)
    direction = direction_ref[...]
    new_solution_ref[...] = solution_ref[...] + step_length * direction
    new_residual = residual_ref[...] - step_length * own_image
    new_residual_ref[...] = new_residual
    new_direction_ref[...] = new_residual + (norm_new / norm_old) * direction


def body(samples, generator, weight_index, preconditioner, solution, residual, direction):
    devices = lax.axis_size("samp")
    cen_dev, centres_all = preconditioner.shape
    samples_dev = samples.shape[1]
    outs = direction.shape[0]
    held, others = plan(devices, 4 * cen_dev * centres_all)

    order = ((*held, *others), cen_dev)
    dims = samples.shape[0]
    sample_copy, *own_state, centre_table, rhs, constant, pick, points = pl.pallas_call(
        functools.partial(begin, order),
        in_specs=[HBM] * 6,
        out_shape=[
            jax.ShapeDtypeStruct(samples.shape, jnp.int32),
            *[jax.ShapeDtypeStruct(direction.shape, F32)] * 3,
            jax.ShapeDtypeStruct((2, dims, centres_all), F32),
            jax.ShapeDtypeStruct((16 * dims, centres_all), BF16),
            jax.ShapeDtypeStruct((dims, 128), F32),
            jax.ShapeDtypeStruct((6 * dims, 128 * dims), BF16),
            jax.ShapeDtypeStruct((dims, 128), jnp.int32),
        ],
        scratch_shapes=[
            pltpu.SMEM((dims,), jnp.int32),
            pltpu.SMEM((dims,), jnp.int32),
            pltpu.SemaphoreType.DMA((6,)),
        ],
        compiler_params=pltpu.CompilerParams(vmem_limit_bytes=(6 << 20) + 1200 * centres_all),
        name="begin",
    )(*in_hbm(generator, weight_index, samples, solution, residual, direction))
    own_points = points[:, :cen_dev]
    tables = (sample_copy, centre_table, rhs, constant, pick)

    half = samples_dev // 2
    use_store = 4 * half * centres_all <= STORE_BYTES
    store, filled = [], 0

    def fill(rows, passed):
        nonlocal filled
        rows = min(rows, half - filled) if use_store else 0
        if rows == 0:
            return passed
        made, handed = kernel_rows(passed, filled, rows, tables)
        store.append(made)
        filled += rows
        return handed

    early = [swap(preconditioner, bit, devices) for bit in held[:2]]
    later = []
    bit = 1
    state = None
    while bit < devices:
        if state is None:
            other = [swap(value, bit, devices) for value in (direction, residual)]
            state, _ = joined(bit, [own_state[2], own_state[1]], other)
        else:
            other = swap(state, bit, devices)
            riders = early if bit == 2 else later if 2 * bit == devices else []
            state, riders = joined(bit, [fill(256, state)], [other], riders)
            if bit == 2 and len(early) > 1:
                early = riders
                later = [swap(early[0], held[1], devices)]
            elif riders:
                later = riders
        bit *= 2
    pieces = [preconditioner, *early, *later]

    def coefficients_of(group):
        rows = len(group) * cen_dev
        return pl.pallas_call(
            functools.partial(row_products, outs, len(group)),
            out_shape=[
                jax.ShapeDtypeStruct((outs, rows), F32),
                jax.ShapeDtypeStruct((3, rows, centres_all), BF16),
            ],
            compiler_params=pltpu.CompilerParams(
                vmem_limit_bytes=(4 << 20) + 24 * rows * centres_all
            ),
            name="row_products",
        )(state, *group)

    groups = [pieces]
    for bit in held[2:]:
        groups.append([swap(p, bit, devices) for p in sum(groups, [])])
    made = [coefficients_of(group) for group in groups]
    coefficients = jnp.concatenate([m[0] for m in made], axis=1)
    parts = [m[1] for m in made]
    for bit in others:
        other = swap(coefficients, bit, devices)
        mine = fill(256, coefficients)
        coefficients = jnp.concatenate([mine, other], axis=1)
    coefficients = fill(half, coefficients)

    kept, sent, kernel_products = apply_products(store, coefficients, own_points, 256, tables)
    for bit in reversed(others):
        came = swap(sent, bit, devices)
        if bit != others[0]:
            summed = kept + came
            width = summed.shape[1] // 2
            kept, sent = summed[:, :width], summed[:, width:]
    scale_total = float(samples_dev * devices) * float(centres_all)
    image = pl.pallas_call(
        functools.partial(image_rows, scale_total, ridge_weight / centres_all),
        out_shape=jax.ShapeDtypeStruct((outs, centres_all), F32),
        compiler_params=pltpu.CompilerParams(
            vmem_limit_bytes=(4 << 20) + 8 * kept.shape[1] * centres_all
        ),
        name="image_rows",
    )(kept, came, kernel_products, *parts)
    bit = 1
    while 2 * bit < devices:
        image = image + swap(image, bit, devices)
        bit *= 2
    more = swap(image, bit, devices)
    own = jax.ShapeDtypeStruct(solution.shape, F32)
    return pl.pallas_call(
        finish,
        out_shape=[own, own, own],
        scratch_shapes=[pltpu.VMEM((outs, centres_all), F32)],
        compiler_params=pltpu.CompilerParams(vmem_limit_bytes=(2 << 20) + 512 * centres_all),
        name="finish",
    )(image, more, state, *own_state)


def solution(mesh):
    placed = (
        P("groups", "samp"),
        P(),
        P(),
        P("samp", None),
        P("groups", "samp"),
        P("groups", "samp"),
        P("groups", "samp"),
    )
    return jax.shard_map(
        body,
        mesh=mesh,
        in_specs=placed,
        out_specs=(P("groups", "samp"), P("groups", "samp"), P("groups", "samp")),
        check_vma=False,
    )
```
